256 devices in a mesh: dp: 32 (over z, x), tensor: 8 (over y, core).
Axes of the slice: x: 4, y: 4, z: 8, core: 2. Of those that a mesh axis runs over, the one named last changes fastest.
Arguments:
- queries: bfloat16 [16384, 4096], P('dp', 'tensor'), may hold values from -5 to 5
- new_keys: bfloat16 [16384, 1024], P('dp', 'tensor'), may hold values from -5 to 5
- new_values: bfloat16 [16384, 1024], P('dp', 'tensor'), may hold values from -5 to 5
- hidden: bfloat16 [16384, 8192], P('dp', 'tensor'), may hold values from -6 to 6
- row_counts: int32 [32, 32], P('dp'), may hold values from 1 to 64, 512 in all within a row
- pack_of: int32 [32, 32], P('dp'), may hold values from 0 to 31, each once within a row
- cache_keys: bfloat16 [32, 32, 128, 1024], P('dp', None, None, 'tensor'), may hold values from -5 to 5
- cache_values: bfloat16 [32, 32, 128, 1024], P('dp', None, None, 'tensor'), may hold values from -5 to 5
- prefix_lengths: int32 [32, 32], P('dp'), may hold values from 32 to 128
- out_weight: bfloat16 [4096, 8192], P('tensor'), may hold values from -0.09375 to 0.09375
- norm_gain: float32 [8192], P('tensor'), may hold values from 0.1 to 1.9
Outputs:
- residual_out: bfloat16 [16384, 8192], P('dp', 'tensor')
- normed: bfloat16 [16384, 8192], P('dp', 'tensor')
The draws below stay inside these ranges and needn't reach their ends.
Inputs may be any that keep to these rules, and one draw needn't show every extreme that they name: Each row of row_counts sums to 512; its largest count is exactly 64. Each row of pack_of names every pack once.
All inputs are finite; a program needn't handle non-finite values.
Results may differ from the reference program's by a relative error of at most 0.011.
Values may be sent and summed in bfloat16 or wider, within the bound.
No kernel may reach another device: no remote copies, remote signals or barrier semaphores. Data moves between devices by JAX's collectives and lax.ppermute only.
A program may use at most 64 MiB of HBM per device.

```python
import math
import jax
import jax.numpy as jnp
import numpy as np
from jax import lax

D = 8192
HEADS = 32
KV_HEADS = 8
HD = 128
PREFIX = 128
MOST = 64
ROWS_DEV = 512
ROWS = 16384
N_DP = 32
N_TENSOR = 8


def draw_queries(key, part):
    key = jax.random.fold_in(key, 11)
    draw_shape = (ROWS, HEADS * HD)
    values = jax.random.truncated_normal(key, -4.0, 4.0, draw_shape, jnp.float32)
    return values.astype(jnp.bfloat16)


def draw_cache_keys(key, part):
    key = jax.random.fold_in(key, 23)
    draw_shape = (N_DP, N_DP, PREFIX, KV_HEADS * HD)
    values = jax.random.truncated_normal(key, -4.0, 4.0, draw_shape, jnp.float32)
    return values.astype(jnp.bfloat16)


def draw_hidden(key, part):
    key = jax.random.fold_in(key, 37)
    draw_shape = (ROWS, D)
    column = lax.broadcasted_iota(jnp.int32, draw_shape, 1).astype(jnp.float32) / D
    values = 0.8 * jax.random.truncated_normal(key, -4.0, 4.0, draw_shape, jnp.float32) * (0.5 + column)
    return values.astype(jnp.bfloat16)


def touch_ends(values, stream_key, smallest, high):
    longest = values.shape.index(max(values.shape))
    spots = []
    for shift in (0, 1):
        where = [jax.random.randint(jax.random.fold_in(stream_key, axis), (), 0, length) for axis, length in enumerate(values.shape)]
        where[longest] = (where[longest] + shift) % values.shape[longest]
        spots.append(tuple(where))
    return values.at[spots[0]].set(smallest).at[spots[1]].set(high)


def steps_of(rng, shape, split, smallest, top_value):
    factor_of = 1.0
    for dim, blocks in split:
        steps = jax.random.uniform(jax.random.fold_in(jax.random.fold_in(rng, 6), dim), (blocks,), jnp.float32, smallest / len(split), top_value / len(split))
        factor_of = factor_of * jnp.repeat(jnp.exp(steps), shape[dim] // blocks).reshape((-1,) + (1,) * (len(shape) - 1 - dim))
    return factor_of


def length_profile(amount, total, most, skew):
    portions = [(1 << 20) // math.isqrt(rank ** skew) + 1 for rank in range(2, amount + 1)]
    rest, given = total - most - (amount - 1), [1] * (amount - 1)
    while rest > 0:
        candidates = [i for i in range(amount - 1) if given[i] < most]
        pool, budget = sum([portions[i] for i in candidates]), rest
        for i in candidates:
            extra = min(most - given[i], max(1, budget * portions[i] // pool), rest)
            given[i] = given[i] + extra
            rest = rest - extra
    return np.array([most] + given)


def ragged(stream_key, amount, total, limit, skew):
    if amount == 2:
        one = jax.random.randint(stream_key, (), max(1, total - limit), min(limit, total - 1) + 1)
        return jnp.stack([one, total - one])
    tallies = jnp.asarray(length_profile(amount, total, limit, skew), jnp.int32)
    pairs = (amount - 1) // 2
    donor, sink = tallies[1:1 + 2 * pairs:2], tallies[2:2 + 2 * pairs:2]
    room = jnp.minimum(donor - 1, limit - sink)
    moved = jax.random.randint(jax.random.fold_in(stream_key, 1), (pairs,), 0, 1 << 20) % (room + 1)
    tallies = tallies.at[1:1 + 2 * pairs:2].set(donor - moved).at[2:2 + 2 * pairs:2].set(sink + moved)
    return tallies[jax.random.permutation(jax.random.fold_in(stream_key, 2), amount)]


def noise(rng, shape, scale, most, pieces=(), kind=jnp.bfloat16):
    drawn = jax.random.normal(rng, shape, jnp.float32) * scale
    if len(pieces) > 0:
        drawn = steps_of(rng, shape, pieces, -0.22, 0.18) * drawn
    return jnp.clip(drawn, min=-most, max=most).astype(kind)


def setup_inputs(seed: int = 0) -> dict:
    key_list = jax.random.split(jax.random.key(seed), 12)
    queries = draw_queries(jax.random.fold_in(key_list[11], 71), 0)
    new_keys = noise(key_list[1], (ROWS, KV_HEADS * HD), 1.0, 5.0, ((0, 32), (1, 8)))
    new_values = noise(key_list[2], (ROWS, KV_HEADS * HD), 1.0, 5.0, ((0, 32), (1, 8)))
    hidden = draw_hidden(jax.random.fold_in(key_list[11], 71), 0)
    row_counts = jax.vmap(lambda own: ragged(own, N_DP, ROWS_DEV, MOST, 2))(jax.random.split(key_list[4], N_DP)).reshape((N_DP, N_DP)).astype(jnp.int32)
    pack_of = jax.vmap(lambda own: jax.random.permutation(own, N_DP))(jax.random.split(key_list[5], N_DP)).reshape((N_DP, N_DP)).astype(jnp.int32)
    cache_keys = draw_cache_keys(jax.random.fold_in(key_list[11], 71), 0)
    cache_values = noise(key_list[7], (N_DP, N_DP, PREFIX, KV_HEADS * HD), 1.0, 5.0, ((0, 32), (3, 8)))
    prefix_lengths = touch_ends(jax.random.randint(key_list[8], (N_DP, N_DP), PREFIX // 4, PREFIX + 1), jax.random.fold_in(key_list[8], 1), PREFIX // 4, PREFIX).astype(jnp.int32)
    out_weight = noise(key_list[9], (HEADS * HD, D), (HEADS * HD) ** -0.5, 0.09375, ((0, 8),))
    norm_gain = jnp.clip(1.0 + 0.18 * jax.random.normal(key_list[10], (D,), jnp.float32), 0.1, 1.9)
    return dict(queries=queries, new_keys=new_keys, new_values=new_values, hidden=hidden, row_counts=row_counts, pack_of=pack_of, cache_keys=cache_keys, cache_values=cache_values, prefix_lengths=prefix_lengths, out_weight=out_weight, norm_gain=norm_gain)


def attend(query_slots, key_slots, value_slots, key_cache, value_cache, live_lengths):
    slot_most = query_slots.shape[1]
    head_size = query_slots.shape[4]
    prefix_len = key_cache.shape[1]
    score_scale = 1.0 / math.sqrt(head_size)
    query_wide = query_slots.astype(jnp.float32)
    cached = jnp.einsum('bmkgh,bpkh->bkgmp', query_wide, key_cache.astype(jnp.float32)) * score_scale
    fresh_scores = jnp.einsum('bmkgh,bnkh->bkgmn', query_wide, key_slots.astype(jnp.float32)) * score_scale
    positions = jnp.arange(prefix_len, dtype=jnp.int32)
    cached = jnp.where(positions[None, None, None, None, :] < live_lengths[:, None, None, None, None], cached, -1e+30)
    slot_order = jnp.arange(slot_most, dtype=jnp.int32)
    fresh_scores = jnp.where(slot_order[None, :] <= slot_order[:, None], fresh_scores, -1e+30)
    scores = jnp.concatenate([cached, fresh_scores], axis=-1)
    row_top = lax.optimization_barrier(jnp.max(scores, axis=-1, keepdims=True))
    lifted = jnp.exp(scores - row_top)
    weights = (lifted / lax.optimization_barrier(jnp.sum(lifted, axis=-1, keepdims=True))).astype(jnp.bfloat16)
    all_values = jnp.concatenate([value_cache, value_slots], axis=1)
    mixed = jnp.einsum('bkgmn,bnkh->bmkgh', weights.astype(jnp.float32), all_values.astype(jnp.float32))
    return mixed.astype(jnp.bfloat16).reshape(query_slots.shape[0], slot_most, -1)

def reference(queries, new_keys, new_values, hidden, row_counts, pack_of, cache_keys, cache_values, prefix_lengths, out_weight, norm_gain):
    group_size = HEADS // KV_HEADS

    def one_generator(generator):
        query_rows = lax.dynamic_slice_in_dim(queries, generator * ROWS_DEV, ROWS_DEV, 0)
        key_rows = lax.dynamic_slice_in_dim(new_keys, generator * ROWS_DEV, ROWS_DEV, 0)
        value_rows = lax.dynamic_slice_in_dim(new_values, generator * ROWS_DEV, ROWS_DEV, 0)
        counts = row_counts[generator]
        packs = pack_of[generator]
        starts = jnp.cumsum(counts) - counts
        offsets = jnp.arange(MOST, dtype=jnp.int32)
        index = jnp.minimum(starts[:, None] + offsets[None, :], ROWS_DEV - 1)
        valid = (offsets[None, :] < counts[:, None])[:, :, None]

        def take_rows(source):
            return jnp.where(valid, source[index], jnp.zeros((), source.dtype))
        query_slots = take_rows(query_rows).reshape(N_DP, MOST, KV_HEADS, group_size, HD)
        key_slots = take_rows(key_rows).reshape(N_DP, MOST, KV_HEADS, HD)
        value_slots = take_rows(value_rows).reshape(N_DP, MOST, KV_HEADS, HD)
        key_cache = cache_keys[packs, generator].reshape(N_DP, PREFIX, KV_HEADS, HD)
        value_cache = cache_values[packs, generator].reshape(N_DP, PREFIX, KV_HEADS, HD)
        live_lengths = prefix_lengths[packs, generator]
        result = attend(query_slots, key_slots, value_slots, key_cache, value_cache, live_lengths)
        row_ids = jnp.arange(ROWS_DEV, dtype=jnp.int32)
        ends = starts + counts
        rollout = lax.optimization_barrier(jnp.sum((ends[None, :] <= row_ids[:, None]).astype(jnp.int32), axis=1))
        return result[rollout, row_ids - starts[rollout]]
    attended = lax.map(one_generator, jnp.arange(N_DP, dtype=jnp.int32)).reshape(ROWS, HEADS * HD)
    width = HEADS * HD // N_TENSOR
    delta = jnp.zeros((ROWS, D), jnp.float32)
    for group_index in range(N_TENSOR):
        partial_value = jnp.dot(attended[:, group_index * width:(group_index + 1) * width], out_weight[group_index * width:(group_index + 1) * width], preferred_element_type=jnp.float32)
        partial_value = lax.optimization_barrier(partial_value.astype(jnp.bfloat16))
        delta = delta + partial_value.astype(jnp.float32)
    summed = hidden.astype(jnp.float32) + delta
    residual_out = summed.astype(jnp.bfloat16)
    mean_square = lax.optimization_barrier(jnp.mean(summed * summed, axis=1, keepdims=True))
    normed = (summed * lax.rsqrt(mean_square + 1e-06) * norm_gain[None, :]).astype(jnp.bfloat16)
    return (residual_out, normed)
```

```python
import math

import jax
import jax.numpy as jnp
from jax import lax
from jax.experimental import pallas as pl
from jax.experimental.pallas import tpu as pltpu
from jax.sharding import PartitionSpec as P

D = 8192
HEADS = 32
KV_HEADS = 8
HD = 128
MOST = 64
GROUP = HEADS // KV_HEADS
BLOCK = 32
FRESH = 128
PAIRS = 48
UNROLL = 8
LOW = -1e30
DEAD = 8192.0
SCALE = 1.0 / math.sqrt(HD)


def pair_plan(counts, packs):
    roll = counts.shape[0]
    ids = jnp.arange(roll, dtype=jnp.int32)
    before = ids[None, :] < ids[:, None]
    starts = jnp.sum(jnp.where(before, counts[None, :], 0), axis=1)
    ends = starts + counts
    first = starts // BLOCK
    spans = (ends - 1) // BLOCK - first + 1
    offsets = jnp.sum(jnp.where(before, spans[None, :], 0), axis=1)
    slot = jnp.arange(PAIRS, dtype=jnp.int32)[:, None]
    hit = (slot >= offsets[None, :]) & (slot < (offsets + spans)[None, :])

    def pick(values):
        return jnp.sum(jnp.where(hit, values, 0), axis=1)

    block = pick(first[None, :] + slot - offsets[None, :])
    plan = jnp.stack(
        [block, pick(packs[None, :]), pick(starts[None, :]), pick(ends[None, :])]
    ).astype(jnp.int32)
    rows = jnp.arange(512, dtype=jnp.int32)[:, None]
    row_start = jnp.max(jnp.where(starts[None, :] <= rows, starts[None, :], 0), axis=1)
    return plan, jnp.broadcast_to(row_start[:, None], (512, HD))


def stack_heads(ref, base):
    return [ref[pl.ds(base, BLOCK), h * HD : (h + 1) * HD] for h in range(GROUP)]


def block_rows(base):
    sub = lax.broadcasted_iota(jnp.int32, (GROUP * BLOCK, HD), 0)
    return base + jnp.bitwise_and(sub, BLOCK - 1)


def score_kernel(plan, q, k, fresh_k, fresh_v, row_start, weights, fresh_out, scores):
    ones = jnp.ones((16, HD), jnp.bfloat16)
    nt = (((1,), (1,)), ((), ()))

    def group(step, carry):
        for u in range(UNROLL):
            i = step * UNROLL + u
            block = plan[0, i]
            base = pl.multiple_of(block * BLOCK, BLOCK)
            left = jnp.concatenate(stack_heads(q, base) + [ones], axis=0)
            both = lax.dot_general(left, k[plan[1, i]], nt, preferred_element_type=jnp.float32)
            live = both[GROUP * BLOCK : GROUP * BLOCK + 1] < 32.0 * DEAD
            found = jnp.where(live, both[: GROUP * BLOCK] * SCALE, LOW)
            rows = block_rows(base)
            mine = (rows >= plan[2, i]) & (rows < plan[3, i])
            scores[block] = jnp.where(mine, found, scores[block])
        return carry

    lax.fori_loop(0, PAIRS // UNROLL, group, 0)

    def finish(block, carry):
        base = pl.multiple_of(block * BLOCK, BLOCK)
        left = jnp.concatenate(stack_heads(q, base), axis=0)
        window = pl.ds(base, FRESH)
        fresh = lax.dot_general(left, fresh_k[window, :], nt, preferred_element_type=jnp.float32)
        key = base - (FRESH - BLOCK) + lax.broadcasted_iota(jnp.int32, fresh.shape, 1)
        start = jnp.concatenate([row_start[pl.ds(base, BLOCK), :]] * GROUP, axis=0)
        fresh = jnp.where((key <= block_rows(base)) & (key >= start), fresh * SCALE, LOW)
        cached = scores[block]
        top = jnp.max(jnp.maximum(cached, fresh), axis=1, keepdims=True)
        lift_c = jnp.exp(cached - top)
        lift_f = jnp.exp(fresh - top)
        total = jnp.sum(lift_c + lift_f, axis=1, keepdims=True)
        share = 1.0 / total
        weights[block] = (lift_c * share).astype(jnp.bfloat16)
        fresh_out[block] = jnp.dot(
            (lift_f * share).astype(jnp.bfloat16),
            fresh_v[window, :],
            preferred_element_type=jnp.float32,
        )
        return carry

    lax.fori_loop(0, 512 // BLOCK, finish, 0, unroll=4)


def mix_kernel(plan, weights, v, fresh_out, out, mixed):
    def group(step, carry):
        for u in range(UNROLL):
            i = step * UNROLL + u
            block = plan[0, i]
            rows = block_rows(block * BLOCK)
            mine = (rows >= plan[2, i]) & (rows < plan[3, i])
            found = jnp.dot(weights[block], v[plan[1, i]], preferred_element_type=jnp.float32)
            mixed[block] = jnp.where(mine, found, mixed[block])
        return carry

    lax.fori_loop(0, PAIRS // UNROLL, group, 0)
    for block in range(512 // BLOCK):
        total = (mixed[block] + fresh_out[block]).astype(jnp.bfloat16)
        for h in range(GROUP):
            out[block * BLOCK : (block + 1) * BLOCK, h * HD : (h + 1) * HD] = total[
                h * BLOCK : (h + 1) * BLOCK
            ]


def call(kernel, inputs, out_shape, scratch, flops):
    return pl.pallas_call(
        kernel,
        out_shape=out_shape,
        grid_spec=pltpu.PrefetchScalarGridSpec(
            num_scalar_prefetch=1,
            grid=(),
            in_specs=[pl.BlockSpec(memory_space=pltpu.VMEM)] * inputs,
            out_specs=jax.tree.map(lambda _: pl.BlockSpec(memory_space=pltpu.VMEM), out_shape),
            scratch_shapes=[scratch],
        ),
        compiler_params=pltpu.CompilerParams(vmem_limit_bytes=24 * 1024 * 1024),
        cost_estimate=pl.CostEstimate(flops=flops, bytes_accessed=4 << 20, transcendentals=0),
    )


def on_device(
    queries,
    new_keys,
    new_values,
    hidden,
    row_counts,
    pack_of,
    cache_keys,
    cache_values,
    prefix_lengths,
    out_weight,
    norm_gain,
):
    count = lax.axis_size("tensor")
    me = lax.axis_index("tensor")
    core = jnp.bitwise_and(me, 1)
    place = lax.shift_right_logical(me, 1)
    f32 = jnp.float32
    bf16 = jnp.bfloat16

    def send(value, step):
        return lax.ppermute(value, "tensor", [(t, (t + 2 * step) % count) for t in range(count)])

    def swap(value):
        return lax.ppermute(value, "tensor", [(t, t ^ 1) for t in range(count)])

    position = lax.broadcasted_iota(jnp.int32, cache_keys.shape[1:], 1)
    marked = jnp.where(
        position < prefix_lengths[0][:, None, None], cache_keys[0], jnp.asarray(DEAD, bf16)
    )
    got_keys = lax.all_to_all(marked, "dp", split_axis=0, concat_axis=0, tiled=True)
    got_values = lax.all_to_all(cache_values[0], "dp", split_axis=0, concat_axis=0, tiled=True)

    order = [jnp.bitwise_and(place + ahead, 3) for ahead in (2, 1, 3, 0)]

    def columns(parity):
        return [
            lax.dynamic_slice_in_dim(out_weight, (2 * spot + parity) * 1024, 1024, 1)
            for spot in order
        ]

    theirs = swap(jnp.concatenate(columns(1 - core), axis=1))
    mats = [
        jnp.concatenate([mine, theirs[:, i * 1024 : (i + 1) * 1024]], axis=0)
        for i, mine in enumerate(columns(core))
    ]

    plan, row_start = pair_plan(row_counts[0], pack_of[0])
    front = ((FRESH - BLOCK, 0), (0, 0))
    blocks = 512 // BLOCK
    area = (blocks, GROUP * BLOCK, HD)
    weights, fresh_out = call(
        score_kernel,
        5,
        (jax.ShapeDtypeStruct(area, bf16), jax.ShapeDtypeStruct(area, f32)),
        pltpu.VMEM(area, f32),
        1 << 30,
    )(plan, queries, got_keys, jnp.pad(new_keys, front), jnp.pad(new_values, front), row_start)
    attended = call(
        mix_kernel,
        3,
        jax.ShapeDtypeStruct(queries.shape, bf16),
        pltpu.VMEM(area, f32),
        1 << 29,
    )(plan, weights, got_values, fresh_out)

    both = jnp.concatenate([attended, swap(attended)], axis=1)
    half_a, half_b = both[:256], both[256:]

    def part(rows, i):
        return jnp.dot(rows, mats[i], preferred_element_type=f32)

    far_a = send(part(half_a, 0).astype(bf16), -1)
    far_b = send(part(half_b, 0).astype(bf16), 1)
    near_up_a = send(part(half_a, 1).astype(bf16), 1)
    near_down_b = send(part(half_b, 2).astype(bf16), -1)
    near_down_a = send((part(half_a, 2) + far_a.astype(f32)).astype(bf16), -1)
    near_up_b = send((part(half_b, 1) + far_b.astype(f32)).astype(bf16), 1)
    delta = jnp.concatenate(
        [
            part(half_a, 3) + near_up_a.astype(f32) + near_down_a.astype(f32),
            part(half_b, 3) + near_up_b.astype(f32) + near_down_b.astype(f32),
        ],
        axis=0,
    )
    summed = hidden.astype(f32) + delta
    residual_out = summed.astype(bf16)
    squares = jnp.sum(summed * summed, axis=1)
    squares = squares + swap(squares)
    squares = squares + send(squares, 1) + send(squares, 2) + send(squares, 3)
    mean_square = squares / D
    normed = (summed * lax.rsqrt(mean_square + 1e-06)[:, None] * norm_gain[None, :]).astype(bf16)
    return (residual_out, normed)


def solution(mesh):
    return jax.shard_map(
        on_device,
        mesh=mesh,
        in_specs=(
            P("dp", "tensor"),
            P("dp", "tensor"),
            P("dp", "tensor"),
            P("dp", "tensor"),
            P("dp", None),
            P("dp", None),
            P("dp", None, None, "tensor"),
            P("dp", None, None, "tensor"),
            P("dp", None),
            P("tensor", None),
            P("tensor"),
        ),
        out_specs=(P("dp", "tensor"), P("dp", "tensor")),
        check_vma=False,
    )
```

```python
import math

import jax
import jax.numpy as jnp
from jax import lax
from jax.experimental import pallas as pl
from jax.experimental.pallas import tpu as pltpu
from jax.sharding import PartitionSpec as P

D = 8192
HEADS = 32
KV_HEADS = 8
HD = 128
MOST = 64
GROUP = HEADS // KV_HEADS
BLOCK = 32
FRESH = 128
PAIRS = 48
CHUNKS = 4
UNROLL = 8
LOW = -1e30
DEAD = 8192.0
SCALE = 1.0 / math.sqrt(HD)
NT = (((1,), (1,)), ((), ()))


def pair_plan(counts, packs):
    roll = counts.shape[0]
    ids = jnp.arange(roll, dtype=jnp.int32)
    before = ids[None, :] < ids[:, None]
    starts = jnp.sum(jnp.where(before, counts[None, :], 0), axis=1)
    ends = starts + counts
    first = starts // BLOCK
    spans = (ends - 1) // BLOCK - first + 1
    offsets = jnp.sum(jnp.where(before, spans[None, :], 0), axis=1)
    slot = jnp.arange(PAIRS, dtype=jnp.int32)[:, None]
    hit = (slot >= offsets[None, :]) & (slot < (offsets + spans)[None, :])

    def pick(values):
        return jnp.sum(jnp.where(hit, values, 0), axis=1)

    block = pick(first[None, :] + slot - offsets[None, :])
    plan = jnp.stack(
        [block, pick(packs[None, :]), pick(starts[None, :]), pick(ends[None, :])]
    ).astype(jnp.int32)
    rows = jnp.arange(512, dtype=jnp.int32)[:, None]
    row_start = jnp.max(jnp.where(starts[None, :] <= rows, starts[None, :], 0), axis=1)
    return plan, jnp.broadcast_to(row_start[:, None], (512, HD))


def stack_heads(ref, base):
    return [ref[pl.ds(base, BLOCK), h * HD : (h + 1) * HD] for h in range(GROUP)]


def payload_kernel(lengths, keys, values, out, held, sems):
    packs, prefix, _ = keys.shape
    tile = packs // CHUNKS

    def copies(c):
        part = pl.ds(c * tile, tile)
        front, back = held.at[part, pl.ds(0, prefix)], held.at[part, pl.ds(prefix, prefix)]
        return (
            pltpu.make_async_copy(keys.at[part], front, sems.at[0, c]),
            pltpu.make_async_copy(values.at[part], back, sems.at[1, c]),
            pltpu.make_async_copy(held.at[part], out.at[part], sems.at[2, c]),
        )

    steps = [copies(c) for c in range(CHUNKS)]
    for step in steps:
        step[0].start()
        step[1].start()
    position = lax.broadcasted_iota(jnp.int32, keys.shape[1:], 0)
    for c, step in enumerate(steps):
        step[0].wait()
        for u in range(tile):
            pack = c * tile + u
            found = held[pack, :prefix].astype(jnp.float32)
            marked = jnp.where(position < lengths[pack], found, DEAD)
            held[pack, :prefix] = marked.astype(jnp.bfloat16)
        step[1].wait()
        step[2].start()
    for step in steps:
        step[2].wait()


def fresh_kernel(q, fresh_k, fresh_v, row_start, mean_out, level_out):
    def body(block, carry):
        base = pl.multiple_of(block * BLOCK, BLOCK)
        left = jnp.concatenate(stack_heads(q, base), axis=0)
        window = pl.ds(base, FRESH)
        found = lax.dot_general(left, fresh_k[window, :], NT, preferred_element_type=jnp.float32)
        key = base - (FRESH - BLOCK) + lax.broadcasted_iota(jnp.int32, found.shape, 1)
        sub = lax.broadcasted_iota(jnp.int32, found.shape, 0)
        row = base + jnp.bitwise_and(sub, BLOCK - 1)
        start = jnp.concatenate([row_start[pl.ds(base, BLOCK), :]] * GROUP, axis=0)
        found = jnp.where((key <= row) & (key >= start), found * SCALE, LOW)
        top = jnp.max(found, axis=1, keepdims=True)
        lifted = jnp.exp(found - top)
        total = jnp.sum(lifted, axis=1, keepdims=True)
        mean_out[block] = jnp.dot(
            (lifted / total).astype(jnp.bfloat16),
            fresh_v[window, :],
            preferred_element_type=jnp.float32,
        )
        level_out[block] = jnp.broadcast_to(top + jnp.log(total), found.shape)
        return carry

    lax.fori_loop(0, 512 // BLOCK, body, 0, unroll=2)


def main_kernel(
    plan, q, cache_hbm, mean_hbm, level_hbm, out_a, out_b, cache, means, levels, scores, weights, mixed, sems
):
    half = cache.shape[1] // 2
    fetch = [
        pltpu.make_async_copy(
            cache_hbm.at[:, pl.ds(i * half, half)], cache.at[:, pl.ds(i * half, half)], sems.at[i]
        )
        for i in range(2)
    ]
    fetch.append(pltpu.make_async_copy(level_hbm, levels, sems.at[2]))
    fetch.append(pltpu.make_async_copy(mean_hbm, means, sems.at[3]))
    for i in (0, 2, 3, 1):
        fetch[i].start()
    ones = jnp.ones((16, HD), jnp.bfloat16)
    prefix = cache.shape[1] // 2

    def own_rows(base, i):
        row = base + lax.broadcasted_iota(jnp.int32, (BLOCK, HD), 0)
        return (row >= plan[2, i]) & (row < plan[3, i])

    def score(step, carry):
        for u in range(UNROLL):
            i = step * UNROLL + u
            block = plan[0, i]
            base = pl.multiple_of(block * BLOCK, BLOCK)
            left = jnp.concatenate(stack_heads(q, base) + [ones], axis=0)
            both = lax.dot_general(
                left, cache[plan[1, i], :prefix], NT, preferred_element_type=jnp.float32
            )
            live = both[GROUP * BLOCK : GROUP * BLOCK + 1] < 32.0 * DEAD
            found = jnp.where(live, both[: GROUP * BLOCK] * SCALE, LOW)
            mine = own_rows(base, i)
            for h in range(GROUP):
                part = pl.ds(h * BLOCK, BLOCK)
                scores[block, part] = jnp.where(
                    mine, found[h * BLOCK : (h + 1) * BLOCK], scores[block, part]
                )
        return carry

    def soften(block, carry):
        cached = scores[block]
        level = levels[block]
        top = jnp.maximum(jnp.max(cached, axis=1, keepdims=True), level)
        lifted = jnp.exp(cached - top)
        fresh = jnp.exp(level - top)
        share = 1.0 / (jnp.sum(lifted, axis=1, keepdims=True) + fresh)
        weights[block] = (lifted * share).astype(jnp.bfloat16)
        mixed[block] = means[block] * (fresh * share)
        return carry

    def mix(step, carry):
        for u in range(UNROLL):
            i = step * UNROLL + u
            block = plan[0, i]
            found = jnp.dot(
                weights[block], cache[plan[1, i], prefix:], preferred_element_type=jnp.float32
            )
            mine = own_rows(block * BLOCK, i)
            for h in range(GROUP):
                part = pl.ds(h * BLOCK, BLOCK)
                mixed[block, part] += jnp.where(mine, found[h * BLOCK : (h + 1) * BLOCK], 0.0)
        return carry

    fetch[0].wait()
    lax.fori_loop(0, PAIRS // UNROLL, score, 0)
    fetch[2].wait()
    fetch[3].wait()
    lax.fori_loop(0, 512 // BLOCK, soften, 0, unroll=8)
    fetch[1].wait()
    lax.fori_loop(0, PAIRS // UNROLL, mix, 0)
    for block in range(512 // BLOCK):
        total = mixed[block].astype(jnp.bfloat16)
        out = out_a if block < 8 else out_b
        base = (block % 8) * BLOCK
        for h in range(GROUP):
            out[base : base + BLOCK, h * HD : (h + 1) * HD] = total[h * BLOCK : (h + 1) * BLOCK]


def whole(count):
    return [pl.BlockSpec(memory_space=pltpu.VMEM)] * count


def in_hbm(*values):
    return [pltpu.with_memory_space_constraint(value, pltpu.HBM) for value in values]


def far(count):
    return [pl.BlockSpec(memory_space=pltpu.HBM)] * count


def anywhere(count):
    return [pl.BlockSpec(memory_space=pl.ANY)] * count


def make_payload(lengths, keys, values):
    packs, prefix, width = keys.shape
    return pl.pallas_call(
        payload_kernel,
        out_shape=jax.ShapeDtypeStruct((packs, 2 * prefix, width), keys.dtype),
        grid_spec=pltpu.PrefetchScalarGridSpec(
            num_scalar_prefetch=1,
            grid=(),
            in_specs=far(2),
            out_specs=far(1)[0],
            scratch_shapes=[
                pltpu.VMEM((packs, 2 * prefix, width), keys.dtype),
                pltpu.SemaphoreType.DMA((3, CHUNKS)),
            ],
        ),
        compiler_params=pltpu.CompilerParams(vmem_limit_bytes=4 << 20),
        cost_estimate=pl.CostEstimate(flops=1 << 20, bytes_accessed=4 << 20, transcendentals=0),
    )(lengths, *in_hbm(keys, values))


def cut_kernel(starts, weight, after, *refs):
    outs, held, sems = refs[:-2], refs[-2], refs[-1]
    fetch, store = [], []
    for out in outs:
        for i in range(out.shape[1] // 512):
            slot = len(fetch)
            start = pl.multiple_of(starts[slot], 512)
            source = weight.at[:, pl.ds(start, 512)]
            target = out.at[:, pl.ds(i * 512, 512)]
            fetch.append(pltpu.make_async_copy(source, held.at[slot], sems.at[0, slot]))
            store.append(pltpu.make_async_copy(held.at[slot], target, sems.at[1, slot]))
    for copy in fetch:
        copy.start()
    for first, second in zip(fetch, store):
        first.wait()
        second.start()
    for copy in store:
        copy.wait()


def cut(starts, weight, widths, after):
    rows = weight.shape[0]
    count = sum(widths) // 512
    return pl.pallas_call(
        cut_kernel,
        out_shape=tuple(jax.ShapeDtypeStruct((rows, width), weight.dtype) for width in widths),
        grid_spec=pltpu.PrefetchScalarGridSpec(
            num_scalar_prefetch=1,
            grid=(),
            in_specs=far(1) + anywhere(1),
            out_specs=tuple(far(len(widths))),
            scratch_shapes=[
                pltpu.VMEM((count, rows, 512), weight.dtype),
                pltpu.SemaphoreType.DMA((2, count)),
            ],
        ),
        compiler_params=pltpu.CompilerParams(vmem_limit_bytes=8 << 20),
        cost_estimate=pl.CostEstimate(flops=0, bytes_accessed=12 << 20, transcendentals=0),
    )(starts, *in_hbm(weight), after)


def attend_fresh(queries, new_keys, new_values, row_start):
    front = ((FRESH - BLOCK, 0), (0, 0))
    area = jax.ShapeDtypeStruct((512 // BLOCK, GROUP * BLOCK, HD), jnp.float32)
    return pl.pallas_call(
        fresh_kernel,
        out_shape=(area, area),
        in_specs=whole(4),
        out_specs=tuple(whole(2)),
        compiler_params=pltpu.CompilerParams(vmem_limit_bytes=5 << 20),
        cost_estimate=pl.CostEstimate(
            flops=1 << 31, bytes_accessed=4 << 20, transcendentals=1 << 18
        ),
    )(queries, jnp.pad(new_keys, front), jnp.pad(new_values, front), row_start)


def attend(plan, queries, cache, fresh_mean, fresh_level):
    area = fresh_mean.shape
    half = jax.ShapeDtypeStruct((256, queries.shape[1]), queries.dtype)
    return pl.pallas_call(
        main_kernel,
        out_shape=(half, half),
        grid_spec=pltpu.PrefetchScalarGridSpec(
            num_scalar_prefetch=1,
            grid=(),
            in_specs=whole(1) + anywhere(3),
            out_specs=tuple(whole(2)),
            scratch_shapes=[
                pltpu.VMEM(cache.shape, cache.dtype),
                pltpu.VMEM(area, jnp.float32),
                pltpu.VMEM(area, jnp.float32),
                pltpu.VMEM(area, jnp.float32),
                pltpu.VMEM(area, jnp.bfloat16),
                pltpu.VMEM(area, jnp.float32),
                pltpu.SemaphoreType.DMA((4,)),
            ],
        ),
        compiler_params=pltpu.CompilerParams(vmem_limit_bytes=10 << 20),
        cost_estimate=pl.CostEstimate(
            flops=1 << 31, bytes_accessed=4 << 20, transcendentals=1 << 18
        ),
    )(plan, queries, cache, fresh_mean, fresh_level)


def attention(counts, packs, queries, marked, values, new_keys, new_values):
    plan, row_start = pair_plan(counts, packs)
    fresh = attend_fresh(queries, new_keys, new_values, row_start)
    cache = jnp.concatenate([marked, values], axis=1)
    return jnp.concatenate(attend(plan, queries, cache, *fresh), axis=0)


def on_device(
    queries,
    new_keys,
    new_values,
    hidden,
    row_counts,
    pack_of,
    cache_keys,
    cache_values,
    prefix_lengths,
    out_weight,
    norm_gain,
):
    count = lax.axis_size("tensor")
    me = lax.axis_index("tensor")
    f32 = jnp.float32
    bf16 = jnp.bfloat16

    def swap(value, mask):
        return lax.ppermute(value, "tensor", [(t, t ^ mask) for t in range(count)])

    def shared(mask):
        to = jnp.bitwise_xor(me, mask)
        first = [to * 1024, jnp.bitwise_xor(to, 6) * 1024]
        second = [to * 1024 + 512, jnp.bitwise_xor(to, 2) * 1024 + 512]
        return first, second

    payload = make_payload(prefix_lengths[0], cache_keys[0], cache_values[0])
    cache = lax.all_to_all(payload, "dp", split_axis=0, concat_axis=0, tiled=True)

    starts = sum([shared(mask)[half] for mask, half in ((2, 0), (6, 1), (3, 0), (7, 1))], [])
    starts = jnp.stack(starts + sum(shared(1), []))
    pieces = cut(starts, out_weight, (1024, 1024, 1024, 1024, 2048), payload)
    starts, pieces = lax.optimization_barrier((jnp.stack(sum(shared(0), [])), pieces))
    arrived = [swap(piece, mask) for piece, mask in zip(pieces, (2, 6, 3, 7, 1))]
    sibling = arrived[4]
    mine = cut(starts, out_weight, (1024, 1024), payload)
    mats = [
        [mine[0], sibling[:, :1024], arrived[0], arrived[2]],
        [mine[1], sibling[:, 1024:], arrived[1], arrived[3]],
    ]

    plan, row_start = pair_plan(row_counts[0], pack_of[0])
    fresh = attend_fresh(queries, new_keys, new_values, row_start)
    plan, mats = lax.optimization_barrier((plan, mats))
    attended = attend(plan, queries, cache, *fresh)

    near = [[swap(rows, mask) for mask in (2, 6)] for rows in attended]
    others = [swap(rows, 1) for rows in attended]
    own = []
    got = []
    sent = []
    for rows, other, close in zip(attended, others, near):
        close, sent = lax.optimization_barrier((close, sent))
        totals = [
            sum(
                jnp.dot(part, mat, preferred_element_type=f32)
                for part, mat in zip((rows, other, arrival, swap(arrival, 1)), mats[half])
            )
            for half, arrival in enumerate(close)
        ]
        own.append([total[:, :512] for total in totals])
        sent = [total[:, 512:].astype(bf16) for total in totals]
        got.append([swap(part, mask) for part, mask in zip(sent, (6, 2))])

    delta = jnp.concatenate(
        [
            jnp.concatenate([a + b.astype(f32) for a, b in zip(*pair)], axis=1)
            for pair in zip(own, got)
        ],
        axis=0,
    )
    summed = hidden.astype(f32) + delta
    residual_out = summed.astype(bf16)
    squares = jnp.sum(summed * summed, axis=1)
    squares = squares + swap(squares, 1)
    squares = squares + swap(squares, 4) + swap(squares, 2) + swap(squares, 6)
    mean_square = squares / D
    normed = (summed * lax.rsqrt(mean_square + 1e-06)[:, None] * norm_gain[None, :]).astype(bf16)
    return (residual_out, normed)


def solution(mesh):
    return jax.shard_map(
        on_device,
        mesh=mesh,
        in_specs=(
            P("dp", "tensor"),
            P("dp", "tensor"),
            P("dp", "tensor"),
            P("dp", "tensor"),
            P("dp", None),
            P("dp", None),
            P("dp", None, None, "tensor"),
            P("dp", None, None, "tensor"),
            P("dp", None),
            P("tensor", None),
            P("tensor"),
        ),
        out_specs=(P("dp", "tensor"), P("dp", "tensor")),
        check_vma=False,
    )
```

```python
import functools
import math

import jax
import jax.numpy as jnp
from jax import lax
from jax.experimental import pallas as pl
from jax.experimental.pallas import tpu as pltpu
from jax.sharding import PartitionSpec as P

D = 8192
HEADS = 32
KV_HEADS = 8
HD = 128
MOST = 64
GROUP = HEADS // KV_HEADS
BLOCK = 32
FRESH = 128
PAIRS = 48
CHUNKS = 4
PIECE = 8
UNROLL = 8
LOW = -1e30
DEAD = 8192.0
SCALE = 1.0 / math.sqrt(HD)
NT = (((1,), (1,)), ((), ()))


def pair_plan(counts, packs):
    roll = counts.shape[0]
    ids = jnp.arange(roll, dtype=jnp.int32)
    before = ids[None, :] < ids[:, None]
    starts = jnp.sum(jnp.where(before, counts[None, :], 0), axis=1)
    ends = starts + counts
    first = starts // BLOCK
    spans = (ends - 1) // BLOCK - first + 1
    offsets = jnp.sum(jnp.where(before, spans[None, :], 0), axis=1)
    slot = jnp.arange(PAIRS, dtype=jnp.int32)[:, None]
    hit = (slot >= offsets[None, :]) & (slot < (offsets + spans)[None, :])

    def pick(values):
        return jnp.sum(jnp.where(hit, values, 0), axis=1)

    block = pick(first[None, :] + slot - offsets[None, :])
    ahead = jnp.sum(jnp.where((block < PIECE) & jnp.any(hit, axis=1), 1, 0))
    plan = jnp.stack(
        [
            block,
            pick(packs[None, :]),
            pick(starts[None, :]),
            pick(ends[None, :]),
            jnp.full((PAIRS,), ahead),
        ]
    ).astype(jnp.int32)
    rows = jnp.arange(512, dtype=jnp.int32)[:, None]
    row_start = jnp.max(jnp.where(starts[None, :] <= rows, starts[None, :], 0), axis=1)
    return plan, jnp.broadcast_to(row_start[:, None], (512, HD))


def stack_heads(ref, base):
    return [ref[pl.ds(base, BLOCK), h * HD : (h + 1) * HD] for h in range(GROUP)]


def payload_kernel(lengths, keys, values, out, held, sems):
    packs, prefix, _ = keys.shape
    tile = packs // CHUNKS

    def copies(c):
        part = pl.ds(c * tile, tile)
        front, back = held.at[part, pl.ds(0, prefix)], held.at[part, pl.ds(prefix, prefix)]
        return (
            pltpu.make_async_copy(keys.at[part], front, sems.at[0, c]),
            pltpu.make_async_copy(values.at[part], back, sems.at[1, c]),
            pltpu.make_async_copy(held.at[part], out.at[part], sems.at[2, c]),
        )

    steps = [copies(c) for c in range(CHUNKS)]
    for step in steps:
        step[0].start()
        step[1].start()
    position = lax.broadcasted_iota(jnp.int32, keys.shape[1:], 0)
    for c, step in enumerate(steps):
        step[0].wait()
        for u in range(tile):
            pack = c * tile + u
            found = held[pack, :prefix].astype(jnp.float32)
            marked = jnp.where(position < lengths[0, pack], found, DEAD)
            held[pack, :prefix] = marked.astype(jnp.bfloat16)
        step[1].wait()
        step[2].start()
    for step in steps:
        step[2].wait()


def fresh_kernel(q, fresh_k, fresh_v, row_start, mean_out, level_out):
    def body(block, carry):
        base = pl.multiple_of(block * BLOCK, BLOCK)
        left = jnp.concatenate(stack_heads(q, base), axis=0)
        window = pl.ds(base, FRESH)
        found = lax.dot_general(left, fresh_k[window, :], NT, preferred_element_type=jnp.float32)
        key = base - (FRESH - BLOCK) + lax.broadcasted_iota(jnp.int32, found.shape, 1)
        sub = lax.broadcasted_iota(jnp.int32, found.shape, 0)
        row = base + jnp.bitwise_and(sub, BLOCK - 1)
        start = jnp.concatenate([row_start[pl.ds(base, BLOCK), :]] * GROUP, axis=0)
        found = jnp.where((key <= row) & (key >= start), found * SCALE, LOW)
        top = jnp.max(found, axis=1, keepdims=True)
        lifted = jnp.exp(found - top)
        total = jnp.sum(lifted, axis=1, keepdims=True)
        mean_out[block] = jnp.dot(
            (lifted / total).astype(jnp.bfloat16),
            fresh_v[window, :],
            preferred_element_type=jnp.float32,
        )
        level_out[block] = jnp.broadcast_to(top + jnp.log(total), found.shape)
        return carry

    lax.fori_loop(0, 512 // BLOCK, body, 0, unroll=2)


def main_kernel(
    first, plan, q, cache_hbm, mean_hbm, level_hbm, out, cache, means, levels, scores, weights, mixed, sems
):
    half = cache.shape[1] // 2
    fetch = [
        pltpu.make_async_copy(
            cache_hbm.at[:, pl.ds(i * half, half)], cache.at[:, pl.ds(i * half, half)], sems.at[i]
        )
        for i in range(2)
    ]
    blocks = pl.ds(first, PIECE)
    fetch.append(pltpu.make_async_copy(level_hbm.at[blocks], levels, sems.at[2]))
    fetch.append(pltpu.make_async_copy(mean_hbm.at[blocks], means, sems.at[3]))
    for i in (0, 2, 3, 1):
        fetch[i].start()
    ones = jnp.ones((16, HD), jnp.bfloat16)
    ahead = plan[4, 0]
    if first == 0:
        lower, upper = 0, lax.div(ahead + UNROLL - 1, UNROLL)
    else:
        lower, upper = lax.div(ahead, UNROLL), PAIRS // UNROLL

    def place(i):
        block = plan[0, i] - first
        return jnp.where((block >= 0) & (block < PIECE), block, PIECE)

    def own_rows(base, i):
        row = base + lax.broadcasted_iota(jnp.int32, (BLOCK, HD), 0)
        return (row >= plan[2, i]) & (row < plan[3, i])

    def score(step, carry):
        for u in range(UNROLL):
            i = step * UNROLL + u
            block = place(i)
            base = pl.multiple_of(plan[0, i] * BLOCK, BLOCK)
            left = jnp.concatenate(stack_heads(q, base) + [ones], axis=0)
            both = lax.dot_general(
                left, cache[plan[1, i], :half], NT, preferred_element_type=jnp.float32
            )
            live = both[GROUP * BLOCK : GROUP * BLOCK + 1] < 32.0 * DEAD
            found = jnp.where(live, both[: GROUP * BLOCK] * SCALE, LOW)
            mine = own_rows(base, i)
            for h in range(GROUP):
                part = pl.ds(h * BLOCK, BLOCK)
                scores[block, part] = jnp.where(
                    mine, found[h * BLOCK : (h + 1) * BLOCK], scores[block, part]
                )
        return carry

    def soften(block, carry):
        cached = scores[block]
        level = levels[block]
        top = jnp.maximum(jnp.max(cached, axis=1, keepdims=True), level)
        lifted = jnp.exp(cached - top)
        fresh = jnp.exp(level - top)
        share = 1.0 / (jnp.sum(lifted, axis=1, keepdims=True) + fresh)
        weights[block] = (lifted * share).astype(jnp.bfloat16)
        mixed[block] = means[block] * (fresh * share)
        return carry

    def mix(step, carry):
        for u in range(UNROLL):
            i = step * UNROLL + u
            block = place(i)
            found = jnp.dot(
                weights[block], cache[plan[1, i], half:], preferred_element_type=jnp.float32
            )
            mine = own_rows(plan[0, i] * BLOCK, i)
            for h in range(GROUP):
                part = pl.ds(h * BLOCK, BLOCK)
                mixed[block, part] += jnp.where(mine, found[h * BLOCK : (h + 1) * BLOCK], 0.0)
        return carry

    fetch[0].wait()
    lax.fori_loop(lower, upper, score, 0)
    fetch[2].wait()
    fetch[3].wait()
    lax.fori_loop(0, PIECE, soften, 0, unroll=PIECE)
    fetch[1].wait()
    lax.fori_loop(lower, upper, mix, 0)
    for block in range(PIECE):
        total = mixed[block].astype(jnp.bfloat16)
        base = block * BLOCK
        for h in range(GROUP):
            out[base : base + BLOCK, h * HD : (h + 1) * HD] = total[h * BLOCK : (h + 1) * BLOCK]


def whole(count):
    return [pl.BlockSpec(memory_space=pltpu.VMEM)] * count


def in_hbm(*values):
    return [pltpu.with_memory_space_constraint(value, pltpu.HBM) for value in values]


def far(count):
    return [pl.BlockSpec(memory_space=pltpu.HBM)] * count


def anywhere(count):
    return [pl.BlockSpec(memory_space=pl.ANY)] * count


def make_payload(lengths, keys, values):
    packs, prefix, width = keys.shape
    return pl.pallas_call(
        payload_kernel,
        out_shape=jax.ShapeDtypeStruct((packs, 2 * prefix, width), keys.dtype),
        grid_spec=pltpu.PrefetchScalarGridSpec(
            num_scalar_prefetch=1,
            grid=(),
            in_specs=far(2),
            out_specs=far(1)[0],
            scratch_shapes=[
                pltpu.VMEM((packs, 2 * prefix, width), keys.dtype),
                pltpu.SemaphoreType.DMA((3, CHUNKS)),
            ],
        ),
        compiler_params=pltpu.CompilerParams(vmem_limit_bytes=4 << 20),
        cost_estimate=pl.CostEstimate(flops=1 << 20, bytes_accessed=4 << 20, transcendentals=0),
    )(lengths, *in_hbm(keys, values))


def cut_kernel(starts, weight, after, *refs):
    outs, held, sems = refs[:-2], refs[-2], refs[-1]
    fetch, store = [], []
    for out in outs:
        for i in range(out.shape[1] // 512):
            slot = len(fetch)
            start = pl.multiple_of(starts[slot], 512)
            source = weight.at[:, pl.ds(start, 512)]
            target = out.at[:, pl.ds(i * 512, 512)]
            fetch.append(pltpu.make_async_copy(source, held.at[slot], sems.at[0, slot]))
            store.append(pltpu.make_async_copy(held.at[slot], target, sems.at[1, slot]))
    for copy in fetch:
        copy.start()
    for first, second in zip(fetch, store):
        first.wait()
        second.start()
    for copy in store:
        copy.wait()


def cut(starts, weight, widths, after):
    rows = weight.shape[0]
    count = sum(widths) // 512
    return pl.pallas_call(
        cut_kernel,
        out_shape=tuple(jax.ShapeDtypeStruct((rows, width), weight.dtype) for width in widths),
        grid_spec=pltpu.PrefetchScalarGridSpec(
            num_scalar_prefetch=1,
            grid=(),
            in_specs=far(1) + anywhere(1),
            out_specs=tuple(far(len(widths))),
            scratch_shapes=[
                pltpu.VMEM((count, rows, 512), weight.dtype),
                pltpu.SemaphoreType.DMA((2, count)),
            ],
        ),
        compiler_params=pltpu.CompilerParams(vmem_limit_bytes=8 << 20),
        cost_estimate=pl.CostEstimate(flops=0, bytes_accessed=12 << 20, transcendentals=0),
    )(starts, *in_hbm(weight), after)


def attend_fresh(queries, new_keys, new_values, row_start):
    front = ((FRESH - BLOCK, 0), (0, 0))
    area = jax.ShapeDtypeStruct((512 // BLOCK, GROUP * BLOCK, HD), jnp.float32)
    return pl.pallas_call(
        fresh_kernel,
        out_shape=(area, area),
        in_specs=whole(4),
        out_specs=tuple(whole(2)),
        compiler_params=pltpu.CompilerParams(vmem_limit_bytes=5 << 20),
        cost_estimate=pl.CostEstimate(
            flops=1 << 31, bytes_accessed=4 << 20, transcendentals=1 << 18
        ),
    )(queries, jnp.pad(new_keys, front), jnp.pad(new_values, front), row_start)


def attend(first, plan, queries, cache, fresh_mean, fresh_level):
    area = fresh_mean.shape[1:]
    return pl.pallas_call(
        functools.partial(main_kernel, first),
        out_shape=jax.ShapeDtypeStruct((PIECE * BLOCK, queries.shape[1]), queries.dtype),
        grid_spec=pltpu.PrefetchScalarGridSpec(
            num_scalar_prefetch=1,
            grid=(),
            in_specs=whole(1) + anywhere(3),
            out_specs=whole(1)[0],
            scratch_shapes=[
                pltpu.VMEM(cache.shape, cache.dtype),
                pltpu.VMEM((PIECE, *area), jnp.float32),
                pltpu.VMEM((PIECE, *area), jnp.float32),
                pltpu.VMEM((PIECE + 1, *area), jnp.float32),
                pltpu.VMEM((PIECE + 1, *area), jnp.bfloat16),
                pltpu.VMEM((PIECE + 1, *area), jnp.float32),
                pltpu.SemaphoreType.DMA((4,)),
            ],
        ),
        compiler_params=pltpu.CompilerParams(vmem_limit_bytes=7 << 20),
        cost_estimate=pl.CostEstimate(
            flops=1 << 31, bytes_accessed=4 << 20, transcendentals=1 << 18
        ),
    )(plan, queries, cache, *in_hbm(fresh_mean, fresh_level))


def attention(counts, packs, queries, marked, values, new_keys, new_values):
    plan, row_start = pair_plan(counts, packs)
    fresh = attend_fresh(queries, new_keys, new_values, row_start)
    cache = jnp.concatenate([marked, values], axis=1)
    return jnp.concatenate([attend(i, plan, queries, cache, *fresh) for i in (0, PIECE)], axis=0)


def on_device(
    queries,
    new_keys,
    new_values,
    hidden,
    row_counts,
    pack_of,
    cache_keys,
    cache_values,
    prefix_lengths,
    out_weight,
    norm_gain,
):
    count = lax.axis_size("tensor")
    me = lax.axis_index("tensor")
    f32 = jnp.float32
    bf16 = jnp.bfloat16

    def swap(value, mask):
        return lax.ppermute(value, "tensor", [(t, t ^ mask) for t in range(count)])

    def shared(mask):
        to = jnp.bitwise_xor(me, mask)
        first = [to * 1024, jnp.bitwise_xor(to, 6) * 1024]
        second = [to * 1024 + 512, jnp.bitwise_xor(to, 2) * 1024 + 512]
        return first, second

    payload = make_payload(prefix_lengths, cache_keys[0], cache_values[0])
    cache = lax.all_to_all(payload, "dp", split_axis=0, concat_axis=0, tiled=True)

    starts = sum([shared(mask)[half] for mask, half in ((2, 0), (6, 1), (3, 0), (7, 1))], [])
    pieces = cut(jnp.stack(starts), out_weight, (1024,) * 4, payload)
    starts, pieces = lax.optimization_barrier(
        (jnp.stack(sum(shared(1), []) + sum(shared(0), [])), pieces)
    )
    same = [swap(piece, mask) for piece, mask in zip(pieces[:2], (2, 6))]
    cross = [swap(piece, mask) for piece, mask in zip(pieces[2:], (3, 7))]
    pieces = cut(starts, out_weight, (1024,) * 4, payload)
    sibling = [swap(piece, 1) for piece in pieces[:2]]
    here = pieces[2:]

    plan, row_start = pair_plan(row_counts[0], pack_of[0])
    fresh = attend_fresh(queries, new_keys, new_values, row_start)
    plan, same, sibling, here = lax.optimization_barrier((plan, same, sibling, here))
    attended = [attend(first, plan, queries, cache, *fresh) for first in (0, PIECE)]
    attended[0], cross = lax.optimization_barrier((attended[0], cross))

    def times(rows, mat):
        return jnp.dot(rows, mat, preferred_element_type=f32)

    others = [swap(rows, 1) for rows in attended]
    near = [[swap(rows, mask) for mask in (2, 6)] for rows in attended]
    own = []
    got = []
    sent = []
    for rows, other, close in zip(attended, others, near):
        local = [times(rows, here[half]) + times(other, sibling[half]) for half in range(2)]
        close, local, sent = lax.optimization_barrier((close, local, sent))
        totals = [
            local[half] + times(close[half], same[half]) + times(swap(close[half], 1), cross[half])
            for half in range(2)
        ]
        own.append([total[:, :512] for total in totals])
        sent = [total[:, 512:].astype(bf16) for total in totals]
        got.append([swap(part, mask) for part, mask in zip(sent, (6, 2))])

    delta = jnp.concatenate(
        [
            jnp.concatenate([a + b.astype(f32) for a, b in zip(*pair)], axis=1)
            for pair in zip(own, got)
        ],
        axis=0,
    )
    summed = hidden.astype(f32) + delta
    residual_out = summed.astype(bf16)
    squares = jnp.sum(summed * summed, axis=1)
    squares = squares + swap(squares, 1)
    squares = squares + swap(squares, 4) + swap(squares, 2) + swap(squares, 6)
    mean_square = squares / D
    normed = (summed * lax.rsqrt(mean_square + 1e-06)[:, None] * norm_gain[None, :]).astype(bf16)
    return (residual_out, normed)


def solution(mesh):
    return jax.shard_map(
        on_device,
        mesh=mesh,
        in_specs=(
            P("dp", "tensor"),
            P("dp", "tensor"),
            P("dp", "tensor"),
            P("dp", "tensor"),
            P("dp", None),
            P("dp", None),
            P("dp", None, None, "tensor"),
            P("dp", None, None, "tensor"),
            P("dp", None),
            P("tensor", None),
            P("tensor"),
        ),
        out_specs=(P("dp", "tensor"), P("dp", "tensor")),
        check_vma=False,
    )
```

```python
import functools
import math

import jax
import jax.numpy as jnp
from jax import lax
from jax.experimental import pallas as pl
from jax.experimental.pallas import tpu as pltpu
from jax.sharding import PartitionSpec as P

D = 8192
HEADS = 32
KV_HEADS = 8
HD = 128
MOST = 64
GROUP = HEADS // KV_HEADS
BLOCK = 32
FRESH = 128
PAIRS = 48
CHUNKS = 4
PIECE = 8
UNROLL = 8
LOW = -1e30
DEAD = 8192.0
SCALE = 1.0 / math.sqrt(HD)
NT = (((1,), (1,)), ((), ()))


def pair_plan(counts, packs):
    roll = counts.shape[0]
    ids = jnp.arange(roll, dtype=jnp.int32)
    before = ids[None, :] < ids[:, None]
    starts = jnp.sum(jnp.where(before, counts[None, :], 0), axis=1)
    ends = starts + counts
    first = starts // BLOCK
    spans = (ends - 1) // BLOCK - first + 1
    offsets = jnp.sum(jnp.where(before, spans[None, :], 0), axis=1)
    slot = jnp.arange(PAIRS, dtype=jnp.int32)[:, None]
    hit = (slot >= offsets[None, :]) & (slot < (offsets + spans)[None, :])

    def pick(values):
        return jnp.sum(jnp.where(hit, values, 0), axis=1)

    block = pick(first[None, :] + slot - offsets[None, :])
    ahead = jnp.sum(jnp.where((block < PIECE) & jnp.any(hit, axis=1), 1, 0))
    plan = jnp.stack(
        [
            block,
            pick(packs[None, :]),
            pick(starts[None, :]),
            pick(ends[None, :]),
            jnp.full((PAIRS,), ahead),
        ]
    ).astype(jnp.int32)
    rows = jnp.arange(512, dtype=jnp.int32)[:, None]
    row_start = jnp.max(jnp.where(starts[None, :] <= rows, starts[None, :], 0), axis=1)
    return plan, jnp.broadcast_to(row_start[:, None], (512, HD))


def stack_heads(ref, base):
    return [ref[pl.ds(base, BLOCK), h * HD : (h + 1) * HD] for h in range(GROUP)]


def payload_kernel(lengths, keys, values, out, held, sems):
    packs, prefix, _ = keys.shape
    tile = packs // CHUNKS

    def copies(c):
        part = pl.ds(c * tile, tile)
        front, back = held.at[part, pl.ds(0, prefix)], held.at[part, pl.ds(prefix, prefix)]
        return (
            pltpu.make_async_copy(keys.at[part], front, sems.at[0, c]),
            pltpu.make_async_copy(values.at[part], back, sems.at[1, c]),
            pltpu.make_async_copy(held.at[part], out.at[part], sems.at[2, c]),
        )

    steps = [copies(c) for c in range(CHUNKS)]
    for step in steps:
        step[0].start()
        step[1].start()
    position = lax.broadcasted_iota(jnp.int32, keys.shape[1:], 0)
    for c, step in enumerate(steps):
        step[0].wait()
        for u in range(tile):
            pack = c * tile + u
            found = held[pack, :prefix].astype(jnp.float32)
            marked = jnp.where(position < lengths[0, pack], found, DEAD)
            held[pack, :prefix] = marked.astype(jnp.bfloat16)
        step[1].wait()
        step[2].start()
    for step in steps:
        step[2].wait()


def fresh_kernel(q, fresh_k, fresh_v, row_start, mean_out, level_out):
    def body(block, carry):
        base = pl.multiple_of(block * BLOCK, BLOCK)
        left = jnp.concatenate(stack_heads(q, base), axis=0)
        window = pl.ds(base, FRESH)
        found = lax.dot_general(left, fresh_k[window, :], NT, preferred_element_type=jnp.float32)
        key = base - (FRESH - BLOCK) + lax.broadcasted_iota(jnp.int32, found.shape, 1)
        sub = lax.broadcasted_iota(jnp.int32, found.shape, 0)
        row = base + jnp.bitwise_and(sub, BLOCK - 1)
        start = jnp.concatenate([row_start[pl.ds(base, BLOCK), :]] * GROUP, axis=0)
        found = jnp.where((key <= row) & (key >= start), found * SCALE, LOW)
        top = jnp.max(found, axis=1, keepdims=True)
        lifted = jnp.exp(found - top)
        total = jnp.sum(lifted, axis=1, keepdims=True)
        mean_out[block] = jnp.dot(
            (lifted / total).astype(jnp.bfloat16),
            fresh_v[window, :],
            preferred_element_type=jnp.float32,
        )
        level_out[block] = jnp.broadcast_to(top + jnp.log(total), found.shape)
        return carry

    lax.fori_loop(0, 512 // BLOCK, body, 0, unroll=2)


def main_kernel(first, plan, starts, q, cache_hbm, mean_hbm, level_hbm, *refs):
    cache, means, levels, scores, weights, mixed, sems, stage_sems = refs[-8:]
    count = (len(refs) - 9) // 2
    sources, out, staged = refs[:count], refs[count], refs[count + 1 : -8]
    stage = []
    for place_of, (source, target) in enumerate(zip(sources, staged)):
        if source.shape == target.shape:
            parts = [(source, target)]
        elif source.shape[1] == 2 * target.shape[1]:
            parts = [(source.at[:, pl.ds(1024 * (place_of % 2), 1024)], target)]
        else:
            parts = [
                (source.at[:, pl.ds(pl.multiple_of(starts[i], 512), 512)], target.at[:, pl.ds(512 * (i % 2), 512)])
                for i in range(len(stage), len(stage) + 2)
            ]
        for origin, goal in parts:
            stage.append(pltpu.make_async_copy(origin, goal, stage_sems.at[len(stage)]))
    half = cache.shape[1] // 2
    fetch = [
        pltpu.make_async_copy(
            cache_hbm.at[:, pl.ds(i * half, half)], cache.at[:, pl.ds(i * half, half)], sems.at[i]
        )
        for i in range(2)
    ]
    blocks = pl.ds(first, PIECE)
    fetch.append(pltpu.make_async_copy(level_hbm.at[blocks], levels, sems.at[2]))
    fetch.append(pltpu.make_async_copy(mean_hbm.at[blocks], means, sems.at[3]))
    for i in (0, 2, 3, 1):
        fetch[i].start()
    for copy in stage:
        copy.start()
    ones = jnp.ones((16, HD), jnp.bfloat16)
    ahead = plan[4, 0]
    if first == 0:
        lower, upper = 0, lax.div(ahead + UNROLL - 1, UNROLL)
    else:
        lower, upper = lax.div(ahead, UNROLL), PAIRS // UNROLL

    def place(i):
        block = plan[0, i] - first
        return jnp.where((block >= 0) & (block < PIECE), block, PIECE)

    def own_rows(base, i):
        row = base + lax.broadcasted_iota(jnp.int32, (BLOCK, HD), 0)
        return (row >= plan[2, i]) & (row < plan[3, i])

    def score(step, carry):
        for u in range(UNROLL):
            i = step * UNROLL + u
            block = place(i)
            base = pl.multiple_of(plan[0, i] * BLOCK, BLOCK)
            left = jnp.concatenate(stack_heads(q, base) + [ones], axis=0)
            both = lax.dot_general(
                left, cache[plan[1, i], :half], NT, preferred_element_type=jnp.float32
            )
            live = both[GROUP * BLOCK : GROUP * BLOCK + 1] < 32.0 * DEAD
            found = jnp.where(live, both[: GROUP * BLOCK] * SCALE, LOW)
            mine = own_rows(base, i)
            for h in range(GROUP):
                part = pl.ds(h * BLOCK, BLOCK)
                scores[block, part] = jnp.where(
                    mine, found[h * BLOCK : (h + 1) * BLOCK], scores[block, part]
                )
        return carry

    def soften(block, carry):
        cached = scores[block]
        level = levels[block]
        top = jnp.maximum(jnp.max(cached, axis=1, keepdims=True), level)
        lifted = jnp.exp(cached - top)
        fresh = jnp.exp(level - top)
        share = 1.0 / (jnp.sum(lifted, axis=1, keepdims=True) + fresh)
        weights[block] = (lifted * share).astype(jnp.bfloat16)
        mixed[block] = means[block] * (fresh * share)
        return carry

    def mix(step, carry):
        for u in range(UNROLL):
            i = step * UNROLL + u
            block = place(i)
            found = jnp.dot(
                weights[block], cache[plan[1, i], half:], preferred_element_type=jnp.float32
            )
            mine = own_rows(plan[0, i] * BLOCK, i)
            for h in range(GROUP):
                part = pl.ds(h * BLOCK, BLOCK)
                mixed[block, part] += jnp.where(mine, found[h * BLOCK : (h + 1) * BLOCK], 0.0)
        return carry

    fetch[0].wait()
    lax.fori_loop(lower, upper, score, 0)
    fetch[2].wait()
    fetch[3].wait()
    lax.fori_loop(0, PIECE, soften, 0, unroll=PIECE)
    fetch[1].wait()
    lax.fori_loop(lower, upper, mix, 0)
    for block in range(PIECE):
        total = mixed[block].astype(jnp.bfloat16)
        base = block * BLOCK
        for h in range(GROUP):
            out[base : base + BLOCK, h * HD : (h + 1) * HD] = total[h * BLOCK : (h + 1) * BLOCK]
    for copy in stage:
        copy.wait()


def whole(count):
    return [pl.BlockSpec(memory_space=pltpu.VMEM)] * count


def in_hbm(*values):
    return [pltpu.with_memory_space_constraint(value, pltpu.HBM) for value in values]


def far(count):
    return [pl.BlockSpec(memory_space=pltpu.HBM)] * count


def anywhere(count):
    return [pl.BlockSpec(memory_space=pl.ANY)] * count


def make_payload(lengths, keys, values):
    packs, prefix, width = keys.shape
    return pl.pallas_call(
        payload_kernel,
        out_shape=jax.ShapeDtypeStruct((packs, 2 * prefix, width), keys.dtype),
        grid_spec=pltpu.PrefetchScalarGridSpec(
            num_scalar_prefetch=1,
            grid=(),
            in_specs=far(2),
            out_specs=far(1)[0],
            scratch_shapes=[
                pltpu.VMEM((packs, 2 * prefix, width), keys.dtype),
                pltpu.SemaphoreType.DMA((3, CHUNKS)),
            ],
        ),
        compiler_params=pltpu.CompilerParams(vmem_limit_bytes=4 << 20),
        cost_estimate=pl.CostEstimate(flops=1 << 20, bytes_accessed=4 << 20, transcendentals=0),
    )(lengths, *in_hbm(keys, values))


def cut_kernel(starts, weight, after, *refs):
    outs, held, sems = refs[:-2], refs[-2], refs[-1]
    fetch, store = [], []
    for out in outs:
        for i in range(out.shape[1] // 512):
            slot = len(fetch)
            start = pl.multiple_of(starts[slot], 512)
            source = weight.at[:, pl.ds(start, 512)]
            target = out.at[:, pl.ds(i * 512, 512)]
            fetch.append(pltpu.make_async_copy(source, held.at[slot], sems.at[0, slot]))
            store.append(pltpu.make_async_copy(held.at[slot], target, sems.at[1, slot]))
    for copy in fetch:
        copy.start()
    for first, second in zip(fetch, store):
        first.wait()
        second.start()
    for copy in store:
        copy.wait()


def cut(starts, weight, widths, after):
    rows = weight.shape[0]
    count = sum(widths) // 512
    return pl.pallas_call(
        cut_kernel,
        out_shape=tuple(jax.ShapeDtypeStruct((rows, width), weight.dtype) for width in widths),
        grid_spec=pltpu.PrefetchScalarGridSpec(
            num_scalar_prefetch=1,
            grid=(),
            in_specs=far(1) + anywhere(1),
            out_specs=tuple(far(len(widths))),
            scratch_shapes=[
                pltpu.VMEM((count, rows, 512), weight.dtype),
                pltpu.SemaphoreType.DMA((2, count)),
            ],
        ),
        compiler_params=pltpu.CompilerParams(vmem_limit_bytes=8 << 20),
        cost_estimate=pl.CostEstimate(flops=0, bytes_accessed=12 << 20, transcendentals=0),
    )(starts, *in_hbm(weight), after)


def attend_fresh(queries, new_keys, new_values, row_start):
    front = ((FRESH - BLOCK, 0), (0, 0))
    area = jax.ShapeDtypeStruct((512 // BLOCK, GROUP * BLOCK, HD), jnp.float32)
    return pl.pallas_call(
        fresh_kernel,
        out_shape=(area, area),
        in_specs=whole(4),
        out_specs=tuple(whole(2)),
        compiler_params=pltpu.CompilerParams(vmem_limit_bytes=5 << 20),
        cost_estimate=pl.CostEstimate(
            flops=1 << 31, bytes_accessed=4 << 20, transcendentals=1 << 18
        ),
    )(queries, jnp.pad(new_keys, front), jnp.pad(new_values, front), row_start)


def attend(first, plan, starts, queries, cache, fresh, sources=()):
    area = fresh[0].shape[1:]
    rows = jax.ShapeDtypeStruct((PIECE * BLOCK, queries.shape[1]), queries.dtype)
    staged = [pltpu.VMEM((source.shape[0], 1024), source.dtype) for source in sources]
    return pl.pallas_call(
        functools.partial(main_kernel, first),
        out_shape=(rows, *staged),
        grid_spec=pltpu.PrefetchScalarGridSpec(
            num_scalar_prefetch=2,
            grid=(),
            in_specs=whole(1) + anywhere(3 + len(sources)),
            out_specs=tuple(whole(1 + len(staged))),
            scratch_shapes=[
                pltpu.VMEM(cache.shape, cache.dtype),
                pltpu.VMEM((PIECE, *area), jnp.float32),
                pltpu.VMEM((PIECE, *area), jnp.float32),
                pltpu.VMEM((PIECE + 1, *area), jnp.float32),
                pltpu.VMEM((PIECE + 1, *area), jnp.bfloat16),
                pltpu.VMEM((PIECE + 1, *area), jnp.float32),
                pltpu.SemaphoreType.DMA((4,)),
                pltpu.SemaphoreType.DMA((len(sources) + 2,)),
            ],
        ),
        compiler_params=pltpu.CompilerParams(vmem_limit_bytes=(7 + len(sources)) << 20),
        cost_estimate=pl.CostEstimate(
            flops=1 << 31, bytes_accessed=4 << 20, transcendentals=1 << 18
        ),
    )(plan, starts, queries, cache, *in_hbm(*fresh), *in_hbm(*sources))


def attention(counts, packs, queries, marked, values, new_keys, new_values):
    plan, row_start = pair_plan(counts, packs)
    fresh = attend_fresh(queries, new_keys, new_values, row_start)
    cache = jnp.concatenate([marked, values], axis=1)
    return jnp.concatenate([attend(i, plan, plan[0], queries, cache, fresh)[0] for i in (0, PIECE)], axis=0)


def on_device(
    queries,
    new_keys,
    new_values,
    hidden,
    row_counts,
    pack_of,
    cache_keys,
    cache_values,
    prefix_lengths,
    out_weight,
    norm_gain,
):
    count = lax.axis_size("tensor")
    me = lax.axis_index("tensor")
    f32 = jnp.float32
    bf16 = jnp.bfloat16

    def swap(value, mask):
        return lax.ppermute(value, "tensor", [(t, t ^ mask) for t in range(count)])

    def shared(mask):
        to = jnp.bitwise_xor(me, mask)
        first = [to * 1024, jnp.bitwise_xor(to, 6) * 1024]
        second = [to * 1024 + 512, jnp.bitwise_xor(to, 2) * 1024 + 512]
        return first, second

    payload = make_payload(prefix_lengths, cache_keys[0], cache_values[0])
    cache = lax.all_to_all(payload, "dp", split_axis=0, concat_axis=0, tiled=True)

    starts = sum([shared(mask)[half] for mask, half in ((2, 0), (6, 1), (3, 0), (7, 1))], [])
    pieces = cut(jnp.stack(starts), out_weight, (1024,) * 4, payload)
    starts, pieces = lax.optimization_barrier((jnp.stack(sum(shared(1), [])), pieces))
    near_mats = [swap(piece, mask) for piece, mask in zip(pieces, (2, 6, 3, 7))]
    sibling = swap(cut(starts, out_weight, (2048,), payload)[0], 1)

    plan, row_start = pair_plan(row_counts[0], pack_of[0])
    fresh = attend_fresh(queries, new_keys, new_values, row_start)
    plan, sibling, near_mats[:2] = lax.optimization_barrier((plan, sibling, near_mats[:2]))
    starts = jnp.stack(sum(shared(0), []))
    attended = attend(0, plan, starts, queries, cache, fresh)
    sources = (out_weight, out_weight, sibling, sibling, *near_mats)
    rest, *mats = attend(PIECE, plan, starts, queries, cache, fresh, sources)
    attended = [attended[0], rest]
    here, sibling, same, cross = (mats[i : i + 2] for i in (0, 2, 4, 6))

    def times(rows, mat):
        return jnp.dot(rows, mat, preferred_element_type=f32)

    others = [swap(rows, 1) for rows in attended]
    near = [[swap(rows, mask) for mask in (2, 6)] for rows in attended]
    own = []
    got = []
    sent = []
    for rows, other, close in zip(attended, others, near):
        local = [times(rows, here[half]) + times(other, sibling[half]) for half in range(2)]
        close, local, sent = lax.optimization_barrier((close, local, sent))
        totals = [
            local[half] + times(close[half], same[half]) + times(swap(close[half], 1), cross[half])
            for half in range(2)
        ]
        own.append([total[:, :512] for total in totals])
        sent = [total[:, 512:].astype(bf16) for total in totals]
        got.append([swap(part, mask) for part, mask in zip(sent, (6, 2))])

    delta = jnp.concatenate(
        [
            jnp.concatenate([a + b.astype(f32) for a, b in zip(*pair)], axis=1)
            for pair in zip(own, got)
        ],
        axis=0,
    )
    summed = hidden.astype(f32) + delta
    residual_out = summed.astype(bf16)
    squares = jnp.sum(summed * summed, axis=1)
    squares = squares + swap(squares, 1)
    squares = squares + swap(squares, 4) + swap(squares, 2) + swap(squares, 6)
    mean_square = squares / D
    normed = (summed * lax.rsqrt(mean_square + 1e-06)[:, None] * norm_gain[None, :]).astype(bf16)
    return (residual_out, normed)


def solution(mesh):
    return jax.shard_map(
        on_device,
        mesh=mesh,
        in_specs=(
            P("dp", "tensor"),
            P("dp", "tensor"),
            P("dp", "tensor"),
            P("dp", "tensor"),
            P("dp", None),
            P("dp", None),
            P("dp", None, None, "tensor"),
            P("dp", None, None, "tensor"),
            P("dp", None),
            P("tensor", None),
            P("tensor"),
        ),
        out_specs=(P("dp", "tensor"), P("dp", "tensor")),
        check_vma=False,
    )
```

```python
import functools
import math

import jax
import jax.numpy as jnp
from jax import lax
from jax.experimental import pallas as pl
from jax.experimental.pallas import tpu as pltpu
from jax.sharding import PartitionSpec as P

D = 8192
HEADS = 32
KV_HEADS = 8
HD = 128
MOST = 64
GROUP = HEADS // KV_HEADS
BLOCK = 32
FRESH = 128
PAIRS = 48
CHUNKS = 8
PIECE = 8
UNROLL = 8
LOW = -1e30
DEAD = 8192.0
SCALE = 1.0 / math.sqrt(HD)
NT = (((1,), (1,)), ((), ()))


def pair_plan(counts, packs):
    roll = counts.shape[0]
    ids = jnp.arange(roll, dtype=jnp.int32)
    before = ids[None, :] < ids[:, None]
    starts = jnp.sum(jnp.where(before, counts[None, :], 0), axis=1)
    ends = starts + counts
    first = starts // BLOCK
    spans = (ends - 1) // BLOCK - first + 1
    offsets = jnp.sum(jnp.where(before, spans[None, :], 0), axis=1)
    slot = jnp.arange(PAIRS, dtype=jnp.int32)[:, None]
    hit = (slot >= offsets[None, :]) & (slot < (offsets + spans)[None, :])

    def pick(values):
        return jnp.sum(jnp.where(hit, values, 0), axis=1)

    block = pick(first[None, :] + slot - offsets[None, :])
    ahead = jnp.sum(jnp.where((block < PIECE) & jnp.any(hit, axis=1), 1, 0))
    plan = jnp.stack(
        [
            block,
            pick(packs[None, :]),
            pick(starts[None, :]),
            pick(ends[None, :]),
            jnp.full((PAIRS,), ahead),
        ]
    ).astype(jnp.int32)
    rows = jnp.arange(512, dtype=jnp.int32)[:, None]
    row_start = jnp.max(jnp.where(starts[None, :] <= rows, starts[None, :], 0), axis=1)
    return plan, jnp.broadcast_to(row_start[:, None], (512, HD))


def stack_heads(ref, base):
    return [ref[pl.ds(base, BLOCK), h * HD : (h + 1) * HD] for h in range(GROUP)]


def payload_kernel(lengths_hbm, keys, values, out, lengths, held, sems, lengths_sem):
    packs, prefix, _ = keys.shape
    tile = packs // CHUNKS

    def copies(c):
        part = pl.ds(c * tile, tile)
        front, back = held.at[part, pl.ds(0, prefix)], held.at[part, pl.ds(prefix, prefix)]
        return (
            pltpu.make_async_copy(keys.at[part], front, sems.at[0, c]),
            pltpu.make_async_copy(values.at[part], back, sems.at[1, c]),
            pltpu.make_async_copy(held.at[part], out.at[part], sems.at[2, c]),
        )

    steps = [copies(c) for c in range(CHUNKS)]
    fetch = pltpu.make_async_copy(lengths_hbm, lengths, lengths_sem)
    fetch.start()
    for step in steps:
        step[0].start()
        step[1].start()
    fetch.wait()
    position = lax.broadcasted_iota(jnp.int32, keys.shape[1:], 0)
    for c, step in enumerate(steps):
        step[0].wait()
        for u in range(tile):
            pack = c * tile + u
            found = held[pack, :prefix].astype(jnp.float32)
            marked = jnp.where(position < lengths[0, pack], found, DEAD)
            held[pack, :prefix] = marked.astype(jnp.bfloat16)
        step[1].wait()
        step[2].start()
    for step in steps:
        step[2].wait()


def fresh_kernel(q, fresh_k, fresh_v, row_start, mean_out, level_out):
    def body(block, carry):
        base = pl.multiple_of(block * BLOCK, BLOCK)
        left = jnp.concatenate(stack_heads(q, base), axis=0)
        window = pl.ds(base, FRESH)
        found = lax.dot_general(left, fresh_k[window, :], NT, preferred_element_type=jnp.float32)
        key = base - (FRESH - BLOCK) + lax.broadcasted_iota(jnp.int32, found.shape, 1)
        sub = lax.broadcasted_iota(jnp.int32, found.shape, 0)
        row = base + jnp.bitwise_and(sub, BLOCK - 1)
        start = jnp.concatenate([row_start[pl.ds(base, BLOCK), :]] * GROUP, axis=0)
        found = jnp.where((key <= row) & (key >= start), found * SCALE, LOW)
        top = jnp.max(found, axis=1, keepdims=True)
        lifted = jnp.exp(found - top)
        total = jnp.sum(lifted, axis=1, keepdims=True)
        mean_out[block] = jnp.dot(
            (lifted / total).astype(jnp.bfloat16),
            fresh_v[window, :],
            preferred_element_type=jnp.float32,
        )
        level_out[block] = jnp.broadcast_to(top + jnp.log(total), found.shape)
        return carry

    lax.fori_loop(0, 512 // BLOCK, body, 0, unroll=2)


def main_kernel(first, plan, starts, q, cache_in, mean_hbm, level_hbm, *refs):
    means, levels, scores, weights, mixed, sems, stage_sems = refs[-7:]
    refs = refs[:-7]
    if first == 0:
        cache, refs = refs[-1], refs[:-1]
    else:
        cache = cache_in
    count = (len(refs) - 1) // 2
    sources, out, staged = refs[:count], refs[count], refs[count + 1 :]
    stage = []
    for spot, (source, target) in enumerate(zip(sources, staged)):
        if source.shape == target.shape:
            parts = [(source, target)]
        elif source.shape[1] == 2 * target.shape[1]:
            parts = [(source.at[:, pl.ds(1024 * (spot % 2), 1024)], target)]
        else:
            parts = []
            for i in range(2):
                start = pl.multiple_of(starts[2 * spot + i], 512)
                parts.append((source.at[:, pl.ds(start, 512)], target.at[:, pl.ds(512 * i, 512)]))
        for origin, goal in parts:
            stage.append(pltpu.make_async_copy(origin, goal, stage_sems.at[len(stage)]))
    half = cache.shape[1] // 2
    blocks = pl.ds(first, PIECE)
    fetch = [
        pltpu.make_async_copy(level_hbm.at[blocks], levels, sems.at[0]),
        pltpu.make_async_copy(mean_hbm.at[blocks], means, sems.at[1]),
    ]
    halves = []
    if first == 0:
        for i in range(2):
            part = pl.ds(i * half, half)
            halves.append(
                pltpu.make_async_copy(cache_in.at[:, part], cache.at[:, part], sems.at[2 + i])
            )
    for copy in halves[:1] + fetch + halves[1:] + stage:
        copy.start()
    ones = jnp.ones((16, HD), jnp.bfloat16)
    ahead = plan[4, 0]
    if first == 0:
        lower, upper = 0, lax.div(ahead + UNROLL - 1, UNROLL)
    else:
        lower, upper = lax.div(ahead, UNROLL), PAIRS // UNROLL

    def place(i):
        block = plan[0, i] - first
        return jnp.where((block >= 0) & (block < PIECE), block, PIECE)

    def own_rows(base, i):
        row = base + lax.broadcasted_iota(jnp.int32, (BLOCK, HD), 0)
        return (row >= plan[2, i]) & (row < plan[3, i])

    def score(step, carry):
        for u in range(UNROLL):
            i = step * UNROLL + u
            block = place(i)
            base = pl.multiple_of(plan[0, i] * BLOCK, BLOCK)
            left = jnp.concatenate(stack_heads(q, base) + [ones], axis=0)
            both = lax.dot_general(
                left, cache[plan[1, i], :half], NT, preferred_element_type=jnp.float32
            )
            live = both[GROUP * BLOCK : GROUP * BLOCK + 1] < 32.0 * DEAD
            found = jnp.where(live, both[: GROUP * BLOCK] * SCALE, LOW)
            mine = own_rows(base, i)
            for h in range(GROUP):
                part = pl.ds(h * BLOCK, BLOCK)
                scores[block, part] = jnp.where(
                    mine, found[h * BLOCK : (h + 1) * BLOCK], scores[block, part]
                )
        return carry

    def soften(block, carry):
        cached = scores[block]
        level = levels[block]
        top = jnp.maximum(jnp.max(cached, axis=1, keepdims=True), level)
        lifted = jnp.exp(cached - top)
        fresh = jnp.exp(level - top)
        share = 1.0 / (jnp.sum(lifted, axis=1, keepdims=True) + fresh)
        weights[block] = (lifted * share).astype(jnp.bfloat16)
        mixed[block] = means[block] * (fresh * share)
        return carry

    def mix(step, carry):
        for u in range(UNROLL):
            i = step * UNROLL + u
            block = place(i)
            found = jnp.dot(
                weights[block], cache[plan[1, i], half:], preferred_element_type=jnp.float32
            )
            mine = own_rows(plan[0, i] * BLOCK, i)
            for h in range(GROUP):
                part = pl.ds(h * BLOCK, BLOCK)
                mixed[block, part] += jnp.where(mine, found[h * BLOCK : (h + 1) * BLOCK], 0.0)
        return carry

    for copy in halves[:1]:
        copy.wait()
    lax.fori_loop(lower, upper, score, 0)
    for copy in fetch:
        copy.wait()
    lax.fori_loop(0, PIECE, soften, 0, unroll=PIECE)
    for copy in halves[1:]:
        copy.wait()
    lax.fori_loop(lower, upper, mix, 0)
    for block in range(PIECE):
        total = mixed[block].astype(jnp.bfloat16)
        base = block * BLOCK
        for h in range(GROUP):
            out[base : base + BLOCK, h * HD : (h + 1) * HD] = total[h * BLOCK : (h + 1) * BLOCK]
    for copy in stage:
        copy.wait()


def whole(count):
    return [pl.BlockSpec(memory_space=pltpu.VMEM)] * count


def in_hbm(*values):
    return [pltpu.with_memory_space_constraint(value, pltpu.HBM) for value in values]


def far(count):
    return [pl.BlockSpec(memory_space=pltpu.HBM)] * count


def anywhere(count):
    return [pl.BlockSpec(memory_space=pl.ANY)] * count


def make_payload(lengths, keys, values):
    packs, prefix, width = keys.shape
    return pl.pallas_call(
        payload_kernel,
        out_shape=jax.ShapeDtypeStruct((packs, 2 * prefix, width), keys.dtype),
        in_specs=far(3),
        out_specs=far(1)[0],
        scratch_shapes=[
            pltpu.SMEM(lengths.shape, lengths.dtype),
            pltpu.VMEM((packs, 2 * prefix, width), keys.dtype),
            pltpu.SemaphoreType.DMA((3, CHUNKS)),
            pltpu.SemaphoreType.DMA,
        ],
        compiler_params=pltpu.CompilerParams(vmem_limit_bytes=4 << 20),
        cost_estimate=pl.CostEstimate(flops=1 << 20, bytes_accessed=4 << 20, transcendentals=0),
    )(*in_hbm(lengths, keys, values))


def cut_kernel(starts, weight, after, *refs):
    outs, held, sems = refs[:-2], refs[-2], refs[-1]
    fetch, store = [], []
    for out in outs:
        for i in range(out.shape[1] // 512):
            slot = len(fetch)
            start = pl.multiple_of(starts[slot], 512)
            source = weight.at[:, pl.ds(start, 512)]
            target = out.at[:, pl.ds(i * 512, 512)]
            fetch.append(pltpu.make_async_copy(source, held.at[slot], sems.at[0, slot]))
            store.append(pltpu.make_async_copy(held.at[slot], target, sems.at[1, slot]))
    for copy in fetch:
        copy.start()
    for first, second in zip(fetch, store):
        first.wait()
        second.start()
    for copy in store:
        copy.wait()


def cut(starts, weight, widths, after):
    rows = weight.shape[0]
    count = sum(widths) // 512
    return pl.pallas_call(
        cut_kernel,
        out_shape=tuple(jax.ShapeDtypeStruct((rows, width), weight.dtype) for width in widths),
        grid_spec=pltpu.PrefetchScalarGridSpec(
            num_scalar_prefetch=1,
            grid=(),
            in_specs=far(1) + anywhere(1),
            out_specs=tuple(far(len(widths))),
            scratch_shapes=[
                pltpu.VMEM((count, rows, 512), weight.dtype),
                pltpu.SemaphoreType.DMA((2, count)),
            ],
        ),
        compiler_params=pltpu.CompilerParams(vmem_limit_bytes=8 << 20),
        cost_estimate=pl.CostEstimate(flops=0, bytes_accessed=12 << 20, transcendentals=0),
    )(starts, *in_hbm(weight), after)


def attend_fresh(queries, new_keys, new_values, row_start):
    front = ((FRESH - BLOCK, 0), (0, 0))
    area = jax.ShapeDtypeStruct((512 // BLOCK, GROUP * BLOCK, HD), jnp.float32)
    return pl.pallas_call(
        fresh_kernel,
        out_shape=(area, area),
        in_specs=whole(4),
        out_specs=tuple(whole(2)),
        compiler_params=pltpu.CompilerParams(vmem_limit_bytes=5 << 20),
        cost_estimate=pl.CostEstimate(
            flops=1 << 31, bytes_accessed=4 << 20, transcendentals=1 << 18
        ),
    )(queries, jnp.pad(new_keys, front), jnp.pad(new_values, front), row_start)


def attend(first, plan, starts, queries, cache, fresh, sources):
    area = fresh[0].shape[1:]
    outs = [jax.ShapeDtypeStruct((PIECE * BLOCK, queries.shape[1]), queries.dtype)]
    outs += [pltpu.VMEM((source.shape[0], 1024), source.dtype) for source in sources]
    if first == 0:
        outs.append(pltpu.VMEM(cache.shape, cache.dtype))
    return pl.pallas_call(
        functools.partial(main_kernel, first),
        out_shape=tuple(outs),
        grid_spec=pltpu.PrefetchScalarGridSpec(
            num_scalar_prefetch=2,
            grid=(),
            in_specs=whole(1)
            + (anywhere(1) if first == 0 else whole(1))
            + anywhere(2 + len(sources)),
            out_specs=tuple(whole(len(outs))),
            scratch_shapes=[
                pltpu.VMEM((PIECE, *area), jnp.float32),
                pltpu.VMEM((PIECE, *area), jnp.float32),
                pltpu.VMEM((PIECE + 1, *area), jnp.float32),
                pltpu.VMEM((PIECE + 1, *area), jnp.bfloat16),
                pltpu.VMEM((PIECE + 1, *area), jnp.float32),
                pltpu.SemaphoreType.DMA((4,)),
                pltpu.SemaphoreType.DMA((len(sources) + 2,)),
            ],
        ),
        compiler_params=pltpu.CompilerParams(vmem_limit_bytes=12 << 20),
        cost_estimate=pl.CostEstimate(
            flops=1 << 31, bytes_accessed=4 << 20, transcendentals=1 << 18
        ),
    )(plan, starts, queries, cache, *in_hbm(*fresh, *sources))


def attend_all(plan, starts, queries, cache, fresh, sources):
    middle = len(sources) // 2
    rows_a, *mats_a, cache = attend(0, plan, starts, queries, cache, fresh, sources[:middle])
    rows_b, *mats_b = attend(PIECE, plan, starts, queries, cache, fresh, sources[middle:])
    return [rows_a, rows_b], mats_a + mats_b


def on_device(
    queries,
    new_keys,
    new_values,
    hidden,
    row_counts,
    pack_of,
    cache_keys,
    cache_values,
    prefix_lengths,
    out_weight,
    norm_gain,
):
    count = lax.axis_size("tensor")
    me = lax.axis_index("tensor")
    f32 = jnp.float32
    bf16 = jnp.bfloat16

    def swap(value, mask):
        return lax.ppermute(value, "tensor", [(t, t ^ mask) for t in range(count)])

    def shared(mask):
        to = jnp.bitwise_xor(me, mask)
        first = [to * 1024, jnp.bitwise_xor(to, 6) * 1024]
        second = [to * 1024 + 512, jnp.bitwise_xor(to, 2) * 1024 + 512]
        return first, second

    payload = make_payload(prefix_lengths, cache_keys[0], cache_values[0])
    cache = lax.all_to_all(payload, "dp", split_axis=0, concat_axis=0, tiled=True)

    starts = sum([shared(mask)[half] for mask, half in ((2, 0), (6, 1), (3, 0), (7, 1))], [])
    starts = jnp.stack(starts + sum(shared(1), []))
    pieces = cut(starts, out_weight, (1024, 1024, 1024, 1024, 2048), payload)
    *near_mats, sibling = [swap(piece, mask) for piece, mask in zip(pieces, (2, 6, 3, 7, 1))]

    plan, row_start = pair_plan(row_counts[0], pack_of[0])
    fresh = attend_fresh(queries, new_keys, new_values, row_start)
    plan, sibling, near_mats[:2] = lax.optimization_barrier((plan, sibling, near_mats[:2]))
    sources = (out_weight, out_weight, sibling, sibling, *near_mats)
    starts = jnp.stack(sum(shared(0), []))
    attended, mats = attend_all(plan, starts, queries, cache, fresh, sources)
    here, sibling, same, cross = (mats[i : i + 2] for i in (0, 2, 4, 6))

    def times(rows, mat):
        return jnp.dot(rows, mat, preferred_element_type=f32)

    others = [swap(rows, 1) for rows in attended]
    near = [[swap(rows, mask) for mask in (2, 6)] for rows in attended]
    own = []
    got = []
    sent = []
    for rows, other, close in zip(attended, others, near):
        rows, other, sent = lax.optimization_barrier((rows, other, sent))
        close, sent = lax.optimization_barrier((close, sent))
        side = [swap(part, 1) for part in close]
        local = [times(rows, here[half]) + times(other, sibling[half]) for half in range(2)]
        close, local = lax.optimization_barrier((close, local))
        totals = [
            local[half] + times(close[half], same[half]) + times(side[half], cross[half])
            for half in range(2)
        ]
        own.append([total[:, :512] for total in totals])
        sent = [total[:, 512:].astype(bf16) for total in totals]
        got.append([swap(part, mask) for part, mask in zip(sent, (6, 2))])

    delta = jnp.concatenate(
        [
            jnp.concatenate([a + b.astype(f32) for a, b in zip(*pair)], axis=1)
            for pair in zip(own, got)
        ],
        axis=0,
    )
    summed = hidden.astype(f32) + delta
    residual_out = summed.astype(bf16)
    squares = jnp.sum(summed * summed, axis=1)
    squares = squares + swap(squares, 1)
    squares = squares + swap(squares, 4) + swap(squares, 2) + swap(squares, 6)
    mean_square = squares / D
    normed = (summed * lax.rsqrt(mean_square + 1e-06)[:, None] * norm_gain[None, :]).astype(bf16)
    return (residual_out, normed)


def solution(mesh):
    return jax.shard_map(
        on_device,
        mesh=mesh,
        in_specs=(
            P("dp", "tensor"),
            P("dp", "tensor"),
            P("dp", "tensor"),
            P("dp", "tensor"),
            P("dp", None),
            P("dp", None),
            P("dp", None, None, "tensor"),
            P("dp", None, None, "tensor"),
            P("dp", None),
            P("tensor", None),
            P("tensor"),
        ),
        out_specs=(P("dp", "tensor"), P("dp", "tensor")),
        check_vma=False,
    )
```

```python
import functools
import math

import jax
import jax.numpy as jnp
from jax import lax
from jax.experimental import pallas as pl
from jax.experimental.pallas import tpu as pltpu
from jax.sharding import PartitionSpec as P

D = 8192
HEADS = 32
KV_HEADS = 8
HD = 128
MOST = 64
GROUP = HEADS // KV_HEADS
BLOCK = 32
FRESH = 128
PAIRS = 48
CHUNKS = 8
PIECE = 8
UNROLL = 8
LOW = -1e30
DEAD = 8192.0
SCALE = 1.0 / math.sqrt(HD)
NT = (((1,), (1,)), ((), ()))


def pair_plan(counts, packs):
    roll = counts.shape[0]
    ids = jnp.arange(roll, dtype=jnp.int32)
    before = ids[None, :] < ids[:, None]
    starts = jnp.sum(jnp.where(before, counts[None, :], 0), axis=1)
    ends = starts + counts
    first = starts // BLOCK
    spans = (ends - 1) // BLOCK - first + 1
    offsets = jnp.sum(jnp.where(before, spans[None, :], 0), axis=1)
    slot = jnp.arange(PAIRS, dtype=jnp.int32)[:, None]
    hit = (slot >= offsets[None, :]) & (slot < (offsets + spans)[None, :])

    def pick(values):
        return jnp.sum(jnp.where(hit, values, 0), axis=1)

    block = pick(first[None, :] + slot - offsets[None, :])
    ahead = jnp.sum(jnp.where((block < PIECE) & jnp.any(hit, axis=1), 1, 0))
    plan = jnp.stack(
        [
            block,
            pick(packs[None, :]),
            pick(starts[None, :]),
            pick(ends[None, :]),
            jnp.full((PAIRS,), ahead),
        ]
    ).astype(jnp.int32)
    rows = jnp.arange(512, dtype=jnp.int32)[:, None]
    row_start = jnp.max(jnp.where(starts[None, :] <= rows, starts[None, :], 0), axis=1)
    return plan, jnp.broadcast_to(row_start[:, None], (512, HD))


def stack_heads(ref, base):
    return [ref[pl.ds(base, BLOCK), h * HD : (h + 1) * HD] for h in range(GROUP)]


def payload_kernel(lengths_hbm, keys, values, out, lengths, held, sems, lengths_sem):
    packs, prefix, _ = keys.shape
    tile = packs // CHUNKS

    def copies(c):
        part = pl.ds(c * tile, tile)
        front, back = held.at[part, pl.ds(0, prefix)], held.at[part, pl.ds(prefix, prefix)]
        return (
            pltpu.make_async_copy(keys.at[part], front, sems.at[0, c]),
            pltpu.make_async_copy(values.at[part], back, sems.at[1, c]),
            pltpu.make_async_copy(held.at[part], out.at[part], sems.at[2, c]),
        )

    steps = [copies(c) for c in range(CHUNKS)]
    fetch = pltpu.make_async_copy(lengths_hbm, lengths, lengths_sem)
    fetch.start()
    for step in steps:
        step[0].start()
        step[1].start()
    fetch.wait()
    position = lax.broadcasted_iota(jnp.int32, keys.shape[1:], 0)
    for c, step in enumerate(steps):
        step[0].wait()
        for u in range(tile):
            pack = c * tile + u
            found = held[pack, :prefix].astype(jnp.float32)
            marked = jnp.where(position < lengths[0, pack], found, DEAD)
            held[pack, :prefix] = marked.astype(jnp.bfloat16)
        step[1].wait()
        step[2].start()
    for step in steps:
        step[2].wait()


def fresh_kernel(q, fresh_k, fresh_v, row_start, mean_out, level_out):
    def body(block, carry):
        base = pl.multiple_of(block * BLOCK, BLOCK)
        left = jnp.concatenate(stack_heads(q, base), axis=0)
        window = pl.ds(base, FRESH)
        found = lax.dot_general(left, fresh_k[window, :], NT, preferred_element_type=jnp.float32)
        key = base - (FRESH - BLOCK) + lax.broadcasted_iota(jnp.int32, found.shape, 1)
        sub = lax.broadcasted_iota(jnp.int32, found.shape, 0)
        row = base + jnp.bitwise_and(sub, BLOCK - 1)
        start = jnp.concatenate([row_start[pl.ds(base, BLOCK), :]] * GROUP, axis=0)
        found = jnp.where((key <= row) & (key >= start), found * SCALE, LOW)
        top = jnp.max(found, axis=1, keepdims=True)
        lifted = jnp.exp(found - top)
        total = jnp.sum(lifted, axis=1, keepdims=True)
        mean_out[block] = jnp.dot(
            (lifted / total).astype(jnp.bfloat16),
            fresh_v[window, :],
            preferred_element_type=jnp.float32,
        )
        level_out[block] = jnp.broadcast_to(top + jnp.log(total), found.shape)
        return carry

    lax.fori_loop(0, 512 // BLOCK, body, 0, unroll=2)


def main_kernel(first, plan, starts, q, cache_hbm, mean_hbm, level_hbm, *refs):
    cache, means, levels, scores, weights, mixed, sems, stage_sems = refs[-8:]
    count = (len(refs) - 9) // 2
    sources, out, staged = refs[:count], refs[count], refs[count + 1 : -8]
    stage = []
    for place_of, (source, target) in enumerate(zip(sources, staged)):
        if source.shape == target.shape:
            parts = [(source, target)]
        elif source.shape[1] == 2 * target.shape[1]:
            parts = [(source.at[:, pl.ds(1024 * (place_of % 2), 1024)], target)]
        else:
            parts = [
                (source.at[:, pl.ds(pl.multiple_of(starts[i], 512), 512)], target.at[:, pl.ds(512 * (i % 2), 512)])
                for i in range(len(stage), len(stage) + 2)
            ]
        for origin, goal in parts:
            stage.append(pltpu.make_async_copy(origin, goal, stage_sems.at[len(stage)]))
    half = cache.shape[1] // 2
    fetch = [
        pltpu.make_async_copy(
            cache_hbm.at[:, pl.ds(i * half, half)], cache.at[:, pl.ds(i * half, half)], sems.at[i]
        )
        for i in range(2)
    ]
    blocks = pl.ds(first, PIECE)
    fetch.append(pltpu.make_async_copy(level_hbm.at[blocks], levels, sems.at[2]))
    fetch.append(pltpu.make_async_copy(mean_hbm.at[blocks], means, sems.at[3]))
    for i in (0, 2, 3, 1):
        fetch[i].start()
    ones = jnp.ones((16, HD), jnp.bfloat16)
    ahead = plan[4, 0]
    if first == 0:
        lower, upper = 0, lax.div(ahead + UNROLL - 1, UNROLL)
    else:
        lower, upper = lax.div(ahead, UNROLL), PAIRS // UNROLL

    def place(i):
        block = plan[0, i] - first
        return jnp.where((block >= 0) & (block < PIECE), block, PIECE)

    def own_rows(base, i):
        row = base + lax.broadcasted_iota(jnp.int32, (BLOCK, HD), 0)
        return (row >= plan[2, i]) & (row < plan[3, i])

    def score(step, carry):
        for u in range(UNROLL):
            i = step * UNROLL + u
            block = place(i)
            base = pl.multiple_of(plan[0, i] * BLOCK, BLOCK)
            left = jnp.concatenate(stack_heads(q, base) + [ones], axis=0)
            both = lax.dot_general(
                left, cache[plan[1, i], :half], NT, preferred_element_type=jnp.float32
            )
            live = both[GROUP * BLOCK : GROUP * BLOCK + 1] < 32.0 * DEAD
            found = jnp.where(live, both[: GROUP * BLOCK] * SCALE, LOW)
            mine = own_rows(base, i)
            for h in range(GROUP):
                part = pl.ds(h * BLOCK, BLOCK)
                scores[block, part] = jnp.where(
                    mine, found[h * BLOCK : (h + 1) * BLOCK], scores[block, part]
                )
        return carry

    def soften(block, carry):
        cached = scores[block]
        level = levels[block]
        top = jnp.maximum(jnp.max(cached, axis=1, keepdims=True), level)
        lifted = jnp.exp(cached - top)
        fresh = jnp.exp(level - top)
        share = 1.0 / (jnp.sum(lifted, axis=1, keepdims=True) + fresh)
        weights[block] = (lifted * share).astype(jnp.bfloat16)
        mixed[block] = means[block] * (fresh * share)
        return carry

    def mix(step, carry):
        for u in range(UNROLL):
            i = step * UNROLL + u
            block = place(i)
            found = jnp.dot(
                weights[block], cache[plan[1, i], half:], preferred_element_type=jnp.float32
            )
            mine = own_rows(plan[0, i] * BLOCK, i)
            for h in range(GROUP):
                part = pl.ds(h * BLOCK, BLOCK)
                mixed[block, part] += jnp.where(mine, found[h * BLOCK : (h + 1) * BLOCK], 0.0)
        return carry

    fetch[0].wait()
    for copy in stage:
        copy.start()
    lax.fori_loop(lower, upper, score, 0)
    fetch[2].wait()
    fetch[3].wait()
    lax.fori_loop(0, PIECE, soften, 0, unroll=PIECE)
    fetch[1].wait()
    lax.fori_loop(lower, upper, mix, 0)
    for block in range(PIECE):
        total = mixed[block].astype(jnp.bfloat16)
        base = block * BLOCK
        for h in range(GROUP):
            out[base : base + BLOCK, h * HD : (h + 1) * HD] = total[h * BLOCK : (h + 1) * BLOCK]
    for copy in stage:
        copy.wait()


def whole(count):
    return [pl.BlockSpec(memory_space=pltpu.VMEM)] * count


def in_hbm(*values):
    return [pltpu.with_memory_space_constraint(value, pltpu.HBM) for value in values]


def far(count):
    return [pl.BlockSpec(memory_space=pltpu.HBM)] * count


def anywhere(count):
    return [pl.BlockSpec(memory_space=pl.ANY)] * count


def make_payload(lengths, keys, values):
    packs, prefix, width = keys.shape
    return pl.pallas_call(
        payload_kernel,
        out_shape=jax.ShapeDtypeStruct((packs, 2 * prefix, width), keys.dtype),
        in_specs=far(3),
        out_specs=far(1)[0],
        scratch_shapes=[
            pltpu.SMEM(lengths.shape, lengths.dtype),
            pltpu.VMEM((packs, 2 * prefix, width), keys.dtype),
            pltpu.SemaphoreType.DMA((3, CHUNKS)),
            pltpu.SemaphoreType.DMA,
        ],
        compiler_params=pltpu.CompilerParams(vmem_limit_bytes=4 << 20),
        cost_estimate=pl.CostEstimate(flops=1 << 20, bytes_accessed=4 << 20, transcendentals=0),
    )(*in_hbm(lengths, keys, values))


def cut_kernel(starts, weight, after, *refs):
    outs, sems = refs[:-1], refs[-1]
    copies = []
    for out in outs:
        for i in range(out.shape[1] // 512):
            slot = len(copies)
            source = weight.at[:, pl.ds(pl.multiple_of(starts[slot], 512), 512)]
            target = out.at[:, pl.ds(i * 512, 512)]
            copies.append(pltpu.make_async_copy(source, target, sems.at[slot]))
    for copy in copies:
        copy.start()
    for copy in copies:
        copy.wait()


def cut(starts, weight, widths, after):
    rows = weight.shape[0]
    return pl.pallas_call(
        cut_kernel,
        out_shape=tuple(pltpu.VMEM((rows, width), weight.dtype) for width in widths),
        grid_spec=pltpu.PrefetchScalarGridSpec(
            num_scalar_prefetch=1,
            grid=(),
            in_specs=far(1) + anywhere(1),
            out_specs=tuple(whole(len(widths))),
            scratch_shapes=[pltpu.SemaphoreType.DMA((sum(widths) // 512,))],
        ),
        compiler_params=pltpu.CompilerParams(vmem_limit_bytes=8 << 20),
        cost_estimate=pl.CostEstimate(flops=0, bytes_accessed=12 << 20, transcendentals=0),
    )(starts, *in_hbm(weight), after)


def attend_fresh(queries, new_keys, new_values, row_start):
    front = ((FRESH - BLOCK, 0), (0, 0))
    area = jax.ShapeDtypeStruct((512 // BLOCK, GROUP * BLOCK, HD), jnp.float32)
    return pl.pallas_call(
        fresh_kernel,
        out_shape=(area, area),
        in_specs=whole(4),
        out_specs=tuple(whole(2)),
        compiler_params=pltpu.CompilerParams(vmem_limit_bytes=5 << 20),
        cost_estimate=pl.CostEstimate(
            flops=1 << 31, bytes_accessed=4 << 20, transcendentals=1 << 18
        ),
    )(queries, jnp.pad(new_keys, front), jnp.pad(new_values, front), row_start)


def attend(first, plan, starts, queries, cache, fresh, sources=()):
    area = fresh[0].shape[1:]
    rows = jax.ShapeDtypeStruct((PIECE * BLOCK, queries.shape[1]), queries.dtype)
    staged = [pltpu.VMEM((source.shape[0], 1024), source.dtype) for source in sources]
    return pl.pallas_call(
        functools.partial(main_kernel, first),
        out_shape=(rows, *staged),
        grid_spec=pltpu.PrefetchScalarGridSpec(
            num_scalar_prefetch=2,
            grid=(),
            in_specs=whole(1) + anywhere(3 + len(sources)),
            out_specs=tuple(whole(1 + len(staged))),
            scratch_shapes=[
                pltpu.VMEM(cache.shape, cache.dtype),
                pltpu.VMEM((PIECE, *area), jnp.float32),
                pltpu.VMEM((PIECE, *area), jnp.float32),
                pltpu.VMEM((PIECE + 1, *area), jnp.float32),
                pltpu.VMEM((PIECE + 1, *area), jnp.bfloat16),
                pltpu.VMEM((PIECE + 1, *area), jnp.float32),
                pltpu.SemaphoreType.DMA((4,)),
                pltpu.SemaphoreType.DMA((len(sources) + 2,)),
            ],
        ),
        compiler_params=pltpu.CompilerParams(vmem_limit_bytes=(7 + len(sources)) << 20),
        cost_estimate=pl.CostEstimate(
            flops=1 << 31, bytes_accessed=4 << 20, transcendentals=1 << 18
        ),
    )(plan, starts, queries, cache, *in_hbm(*fresh), *in_hbm(*sources))


def attention(counts, packs, queries, marked, values, new_keys, new_values):
    plan, row_start = pair_plan(counts, packs)
    fresh = attend_fresh(queries, new_keys, new_values, row_start)
    cache = jnp.concatenate([marked, values], axis=1)
    return jnp.concatenate([attend(i, plan, plan[0], queries, cache, fresh)[0] for i in (0, PIECE)], axis=0)


def on_device(
    queries,
    new_keys,
    new_values,
    hidden,
    row_counts,
    pack_of,
    cache_keys,
    cache_values,
    prefix_lengths,
    out_weight,
    norm_gain,
):
    count = lax.axis_size("tensor")
    me = lax.axis_index("tensor")
    f32 = jnp.float32
    bf16 = jnp.bfloat16

    def swap(value, mask):
        return lax.ppermute(value, "tensor", [(t, t ^ mask) for t in range(count)])

    def shared(mask):
        to = jnp.bitwise_xor(me, mask)
        first = [to * 1024, jnp.bitwise_xor(to, 6) * 1024]
        second = [to * 1024 + 512, jnp.bitwise_xor(to, 2) * 1024 + 512]
        return first, second

    payload = make_payload(prefix_lengths, cache_keys[0], cache_values[0])
    cache = lax.all_to_all(payload, "dp", split_axis=0, concat_axis=0, tiled=True)

    starts = sum([shared(mask)[half] for mask, half in ((2, 0), (6, 1), (3, 0), (7, 1))], [])
    starts = jnp.stack(starts + sum(shared(1), []))
    pieces = cut(starts, out_weight, (1024, 1024, 1024, 1024, 2048), payload)
    *near_mats, sibling = [swap(piece, mask) for piece, mask in zip(pieces, (2, 6, 3, 7, 1))]

    plan, row_start = pair_plan(row_counts[0], pack_of[0])
    fresh = attend_fresh(queries, new_keys, new_values, row_start)
    plan, sibling, near_mats[:2] = lax.optimization_barrier((plan, sibling, near_mats[:2]))
    starts = jnp.stack(sum(shared(0), []))
    attended = attend(0, plan, starts, queries, cache, fresh)
    sources = (out_weight, out_weight, sibling, sibling, *near_mats)
    rest, *mats = attend(PIECE, plan, starts, queries, cache, fresh, sources)
    attended = [attended[0], rest]
    here, sibling, same, cross = (mats[i : i + 2] for i in (0, 2, 4, 6))

    def times(rows, mat):
        return jnp.dot(rows, mat, preferred_element_type=f32)

    others = [swap(rows, 1) for rows in attended]
    near = [[swap(rows, mask) for mask in (2, 6)] for rows in attended]
    own = []
    got = []
    sent = []
    for rows, other, close in zip(attended, others, near):
        local = [times(rows, here[half]) + times(other, sibling[half]) for half in range(2)]
        close, local, sent = lax.optimization_barrier((close, local, sent))
        totals = [
            local[half] + times(close[half], same[half]) + times(swap(close[half], 1), cross[half])
            for half in range(2)
        ]
        own.append([total[:, :512] for total in totals])
        sent = [total[:, 512:].astype(bf16) for total in totals]
        got.append([swap(part, mask) for part, mask in zip(sent, (6, 2))])

    delta = jnp.concatenate(
        [
            jnp.concatenate([a + b.astype(f32) for a, b in zip(*pair)], axis=1)
            for pair in zip(own, got)
        ],
        axis=0,
    )
    summed = hidden.astype(f32) + delta
    residual_out = summed.astype(bf16)
    squares = jnp.sum(summed * summed, axis=1)
    squares = squares + swap(squares, 1)
    squares = squares + swap(squares, 4) + swap(squares, 2) + swap(squares, 6)
    mean_square = squares / D
    normed = (summed * lax.rsqrt(mean_square + 1e-06)[:, None] * norm_gain[None, :]).astype(bf16)
    return (residual_out, normed)


def solution(mesh):
    return jax.shard_map(
        on_device,
        mesh=mesh,
        in_specs=(
            P("dp", "tensor"),
            P("dp", "tensor"),
            P("dp", "tensor"),
            P("dp", "tensor"),
            P("dp", None),
            P("dp", None),
            P("dp", None, None, "tensor"),
            P("dp", None, None, "tensor"),
            P("dp", None),
            P("tensor", None),
            P("tensor"),
        ),
        out_specs=(P("dp", "tensor"), P("dp", "tensor")),
        check_vma=False,
    )
```

```python
import functools
import math

import jax
import jax.numpy as jnp
from jax import lax
from jax.experimental import pallas as pl
from jax.experimental.pallas import tpu as pltpu
from jax.sharding import PartitionSpec as P

D = 8192
HEADS = 32
KV_HEADS = 8
HD = 128
MOST = 64
GROUP = HEADS // KV_HEADS
BLOCK = 32
FRESH = 128
PAIRS = 48
CHUNKS = 8
PIECE = 8
UNROLL = 8
LOW = -1e30
DEAD = 8192.0
SCALE = 1.0 / math.sqrt(HD)
NT = (((1,), (1,)), ((), ()))


def pair_plan(counts, packs):
    roll = counts.shape[0]
    ids = jnp.arange(roll, dtype=jnp.int32)
    before = ids[None, :] < ids[:, None]
    starts = jnp.sum(jnp.where(before, counts[None, :], 0), axis=1)
    ends = starts + counts
    first = starts // BLOCK
    spans = (ends - 1) // BLOCK - first + 1
    offsets = jnp.sum(jnp.where(before, spans[None, :], 0), axis=1)
    slot = jnp.arange(PAIRS, dtype=jnp.int32)[:, None]
    hit = (slot >= offsets[None, :]) & (slot < (offsets + spans)[None, :])

    def pick(values):
        return jnp.sum(jnp.where(hit, values, 0), axis=1)

    block = pick(first[None, :] + slot - offsets[None, :])
    ahead = jnp.sum(jnp.where((block < PIECE) & jnp.any(hit, axis=1), 1, 0))
    plan = jnp.stack(
        [
            block,
            pick(packs[None, :]),
            pick(starts[None, :]),
            pick(ends[None, :]),
            jnp.full((PAIRS,), ahead),
        ]
    ).astype(jnp.int32)
    rows = jnp.arange(512, dtype=jnp.int32)[:, None]
    row_start = jnp.max(jnp.where(starts[None, :] <= rows, starts[None, :], 0), axis=1)
    return plan, jnp.broadcast_to(row_start[:, None], (512, HD))


def stack_heads(ref, base):
    return [ref[pl.ds(base, BLOCK), h * HD : (h + 1) * HD] for h in range(GROUP)]


def payload_kernel(lengths_hbm, keys, values, out, lengths, held, sems, lengths_sem):
    packs, prefix, _ = keys.shape
    tile = packs // CHUNKS

    def copies(c):
        part = pl.ds(c * tile, tile)
        front, back = held.at[part, pl.ds(0, prefix)], held.at[part, pl.ds(prefix, prefix)]
        return (
            pltpu.make_async_copy(keys.at[part], front, sems.at[0, c]),
            pltpu.make_async_copy(values.at[part], back, sems.at[1, c]),
            pltpu.make_async_copy(held.at[part], out.at[part], sems.at[2, c]),
        )

    steps = [copies(c) for c in range(CHUNKS)]
    fetch = pltpu.make_async_copy(lengths_hbm, lengths, lengths_sem)
    fetch.start()
    for step in steps:
        step[0].start()
        step[1].start()
    fetch.wait()
    position = lax.broadcasted_iota(jnp.int32, keys.shape[1:], 0)
    for c, step in enumerate(steps):
        step[0].wait()
        for u in range(tile):
            pack = c * tile + u
            found = held[pack, :prefix].astype(jnp.float32)
            marked = jnp.where(position < lengths[0, pack], found, DEAD)
            held[pack, :prefix] = marked.astype(jnp.bfloat16)
        step[1].wait()
        step[2].start()
    for step in steps:
        step[2].wait()


def fresh_kernel(q, fresh_k, fresh_v, row_start, mean_out, level_out):
    def body(block, carry):
        base = pl.multiple_of(block * BLOCK, BLOCK)
        left = jnp.concatenate(stack_heads(q, base), axis=0)
        window = pl.ds(base, FRESH)
        found = lax.dot_general(left, fresh_k[window, :], NT, preferred_element_type=jnp.float32)
        key = base - (FRESH - BLOCK) + lax.broadcasted_iota(jnp.int32, found.shape, 1)
        sub = lax.broadcasted_iota(jnp.int32, found.shape, 0)
        row = base + jnp.bitwise_and(sub, BLOCK - 1)
        start = jnp.concatenate([row_start[pl.ds(base, BLOCK), :]] * GROUP, axis=0)
        found = jnp.where((key <= row) & (key >= start), found * SCALE, LOW)
        top = jnp.max(found, axis=1, keepdims=True)
        lifted = jnp.exp(found - top)
        total = jnp.sum(lifted, axis=1, keepdims=True)
        mean_out[block] = jnp.dot(
            (lifted / total).astype(jnp.bfloat16),
            fresh_v[window, :],
            preferred_element_type=jnp.float32,
        )
        level_out[block] = jnp.broadcast_to(top + jnp.log(total), found.shape)
        return carry

    lax.fori_loop(0, 512 // BLOCK, body, 0, unroll=2)


def main_kernel(first, plan, starts, q, cache, mean_hbm, level_hbm, *refs):
    means, levels, scores, weights, mixed, sems, stage_sems = refs[-7:]
    count = (len(refs) - 8) // 2
    sources, out, staged = refs[:count], refs[count], refs[count + 1 : -7]
    stage = []
    for place_of, (source, target) in enumerate(zip(sources, staged)):
        if source.shape == target.shape:
            parts = [(source, target)]
        elif source.shape[1] == 2 * target.shape[1]:
            parts = [(source.at[:, pl.ds(1024 * (place_of % 2), 1024)], target)]
        else:
            parts = [
                (source.at[:, pl.ds(pl.multiple_of(starts[i], 512), 512)], target.at[:, pl.ds(512 * (i % 2), 512)])
                for i in range(len(stage), len(stage) + 2)
            ]
        for origin, goal in parts:
            stage.append(pltpu.make_async_copy(origin, goal, stage_sems.at[len(stage)]))
    half = cache.shape[1] // 2
    blocks = pl.ds(first, PIECE)
    fetch = [
        pltpu.make_async_copy(level_hbm.at[blocks], levels, sems.at[0]),
        pltpu.make_async_copy(mean_hbm.at[blocks], means, sems.at[1]),
    ]
    for copy in fetch + stage:
        copy.start()
    ones = jnp.ones((16, HD), jnp.bfloat16)
    ahead = plan[4, 0]
    if first == 0:
        lower, upper = 0, lax.div(ahead + UNROLL - 1, UNROLL)
    else:
        lower, upper = lax.div(ahead, UNROLL), PAIRS // UNROLL

    def place(i):
        block = plan[0, i] - first
        return jnp.where((block >= 0) & (block < PIECE), block, PIECE)

    def own_rows(base, i):
        row = base + lax.broadcasted_iota(jnp.int32, (BLOCK, HD), 0)
        return (row >= plan[2, i]) & (row < plan[3, i])

    def score(step, carry):
        for u in range(UNROLL):
            i = step * UNROLL + u
            block = place(i)
            base = pl.multiple_of(plan[0, i] * BLOCK, BLOCK)
            left = jnp.concatenate(stack_heads(q, base) + [ones], axis=0)
            both = lax.dot_general(
                left, cache[plan[1, i], :half], NT, preferred_element_type=jnp.float32
            )
            live = both[GROUP * BLOCK : GROUP * BLOCK + 1] < 32.0 * DEAD
            found = jnp.where(live, both[: GROUP * BLOCK] * SCALE, LOW)
            mine = own_rows(base, i)
            for h in range(GROUP):
                part = pl.ds(h * BLOCK, BLOCK)
                scores[block, part] = jnp.where(
                    mine, found[h * BLOCK : (h + 1) * BLOCK], scores[block, part]
                )
        return carry

    def soften(block, carry):
        cached = scores[block]
        level = levels[block]
        top = jnp.maximum(jnp.max(cached, axis=1, keepdims=True), level)
        lifted = jnp.exp(cached - top)
        fresh = jnp.exp(level - top)
        share = 1.0 / (jnp.sum(lifted, axis=1, keepdims=True) + fresh)
        weights[block] = (lifted * share).astype(jnp.bfloat16)
        mixed[block] = means[block] * (fresh * share)
        return carry

    def mix(step, carry):
        for u in range(UNROLL):
            i = step * UNROLL + u
            block = place(i)
            found = jnp.dot(
                weights[block], cache[plan[1, i], half:], preferred_element_type=jnp.float32
            )
            mine = own_rows(plan[0, i] * BLOCK, i)
            for h in range(GROUP):
                part = pl.ds(h * BLOCK, BLOCK)
                mixed[block, part] += jnp.where(mine, found[h * BLOCK : (h + 1) * BLOCK], 0.0)
        return carry

    lax.fori_loop(lower, upper, score, 0)
    for copy in fetch:
        copy.wait()
    lax.fori_loop(0, PIECE, soften, 0, unroll=PIECE)
    lax.fori_loop(lower, upper, mix, 0)
    for block in range(PIECE):
        total = mixed[block].astype(jnp.bfloat16)
        base = block * BLOCK
        for h in range(GROUP):
            out[base : base + BLOCK, h * HD : (h + 1) * HD] = total[h * BLOCK : (h + 1) * BLOCK]
    for copy in stage:
        copy.wait()


def whole(count):
    return [pl.BlockSpec(memory_space=pltpu.VMEM)] * count


def in_hbm(*values):
    return [pltpu.with_memory_space_constraint(value, pltpu.HBM) for value in values]


def far(count):
    return [pl.BlockSpec(memory_space=pltpu.HBM)] * count


def anywhere(count):
    return [pl.BlockSpec(memory_space=pl.ANY)] * count


def make_payload(lengths, keys, values):
    packs, prefix, width = keys.shape
    return pl.pallas_call(
        payload_kernel,
        out_shape=jax.ShapeDtypeStruct((packs, 2 * prefix, width), keys.dtype),
        in_specs=far(3),
        out_specs=far(1)[0],
        scratch_shapes=[
            pltpu.SMEM(lengths.shape, lengths.dtype),
            pltpu.VMEM((packs, 2 * prefix, width), keys.dtype),
            pltpu.SemaphoreType.DMA((3, CHUNKS)),
            pltpu.SemaphoreType.DMA,
        ],
        compiler_params=pltpu.CompilerParams(vmem_limit_bytes=4 << 20),
        cost_estimate=pl.CostEstimate(flops=1 << 20, bytes_accessed=4 << 20, transcendentals=0),
    )(*in_hbm(lengths, keys, values))


def cut_kernel(starts, weight, after, *refs):
    outs, sems = refs[:-1], refs[-1]
    copies = []
    for out in outs:
        for i in range(out.shape[1] // 512):
            slot = len(copies)
            source = weight.at[:, pl.ds(pl.multiple_of(starts[slot], 512), 512)]
            target = out.at[:, pl.ds(i * 512, 512)]
            copies.append(pltpu.make_async_copy(source, target, sems.at[slot]))
    for copy in copies:
        copy.start()
    for copy in copies:
        copy.wait()


def cut(starts, weight, widths, after):
    rows = weight.shape[0]
    return pl.pallas_call(
        cut_kernel,
        out_shape=tuple(pltpu.VMEM((rows, width), weight.dtype) for width in widths),
        grid_spec=pltpu.PrefetchScalarGridSpec(
            num_scalar_prefetch=1,
            grid=(),
            in_specs=far(1) + anywhere(1),
            out_specs=tuple(whole(len(widths))),
            scratch_shapes=[pltpu.SemaphoreType.DMA((sum(widths) // 512,))],
        ),
        compiler_params=pltpu.CompilerParams(vmem_limit_bytes=8 << 20),
        cost_estimate=pl.CostEstimate(flops=0, bytes_accessed=12 << 20, transcendentals=0),
    )(starts, *in_hbm(weight), after)


def attend_fresh(queries, new_keys, new_values, row_start):
    front = ((FRESH - BLOCK, 0), (0, 0))
    area = jax.ShapeDtypeStruct((512 // BLOCK, GROUP * BLOCK, HD), jnp.float32)
    return pl.pallas_call(
        fresh_kernel,
        out_shape=(area, area),
        in_specs=whole(4),
        out_specs=tuple(whole(2)),
        compiler_params=pltpu.CompilerParams(vmem_limit_bytes=5 << 20),
        cost_estimate=pl.CostEstimate(
            flops=1 << 31, bytes_accessed=4 << 20, transcendentals=1 << 18
        ),
    )(queries, jnp.pad(new_keys, front), jnp.pad(new_values, front), row_start)


def attend(first, plan, starts, queries, cache, fresh, sources=()):
    area = fresh[0].shape[1:]
    rows = jax.ShapeDtypeStruct((PIECE * BLOCK, queries.shape[1]), queries.dtype)
    staged = [pltpu.VMEM((source.shape[0], 1024), source.dtype) for source in sources]
    return pl.pallas_call(
        functools.partial(main_kernel, first),
        out_shape=(rows, *staged),
        grid_spec=pltpu.PrefetchScalarGridSpec(
            num_scalar_prefetch=2,
            grid=(),
            in_specs=whole(2) + anywhere(2 + len(sources)),
            out_specs=tuple(whole(1 + len(staged))),
            scratch_shapes=[
                pltpu.VMEM((PIECE, *area), jnp.float32),
                pltpu.VMEM((PIECE, *area), jnp.float32),
                pltpu.VMEM((PIECE + 1, *area), jnp.float32),
                pltpu.VMEM((PIECE + 1, *area), jnp.bfloat16),
                pltpu.VMEM((PIECE + 1, *area), jnp.float32),
                pltpu.SemaphoreType.DMA((2,)),
                pltpu.SemaphoreType.DMA((len(sources) + 2,)),
            ],
        ),
        compiler_params=pltpu.CompilerParams(vmem_limit_bytes=12 << 20),
        cost_estimate=pl.CostEstimate(
            flops=1 << 31, bytes_accessed=4 << 20, transcendentals=1 << 18
        ),
    )(plan, starts, queries, cache, *in_hbm(*fresh, *sources))


def on_device(
    queries,
    new_keys,
    new_values,
    hidden,
    row_counts,
    pack_of,
    cache_keys,
    cache_values,
    prefix_lengths,
    out_weight,
    norm_gain,
):
    count = lax.axis_size("tensor")
    me = lax.axis_index("tensor")
    f32 = jnp.float32
    bf16 = jnp.bfloat16

    def swap(value, mask):
        return lax.ppermute(value, "tensor", [(t, t ^ mask) for t in range(count)])

    def shared(mask):
        to = jnp.bitwise_xor(me, mask)
        first = [to * 1024, jnp.bitwise_xor(to, 6) * 1024]
        second = [to * 1024 + 512, jnp.bitwise_xor(to, 2) * 1024 + 512]
        return first, second

    payload = make_payload(prefix_lengths, cache_keys[0], cache_values[0])
    cache = lax.all_to_all(payload, "dp", split_axis=0, concat_axis=0, tiled=True)
    cache = pltpu.with_memory_space_constraint(cache, pltpu.VMEM)

    starts = sum([shared(mask)[half] for mask, half in ((2, 0), (6, 1), (3, 0), (7, 1))], [])
    starts = jnp.stack(starts + sum(shared(1), []))
    pieces = cut(starts, out_weight, (1024, 1024, 1024, 1024, 2048), payload)
    *near_mats, sibling = [swap(piece, mask) for piece, mask in zip(pieces, (2, 6, 3, 7, 1))]

    plan, row_start = pair_plan(row_counts[0], pack_of[0])
    fresh = attend_fresh(queries, new_keys, new_values, row_start)
    plan, sibling, near_mats[:2] = lax.optimization_barrier((plan, sibling, near_mats[:2]))
    starts = jnp.stack(sum(shared(0), []))
    rows = attend(0, plan, starts, queries, cache, fresh)[0]
    sources = (out_weight, out_weight, sibling, sibling, *near_mats)
    rest, *mats = attend(PIECE, plan, starts, queries, cache, fresh, sources)
    attended = [rows, rest]
    here, sibling, same, cross = (mats[i : i + 2] for i in (0, 2, 4, 6))

    def times(rows, mat):
        return jnp.dot(rows, mat, preferred_element_type=f32)

    others = [swap(rows, 1) for rows in attended]
    near = [[swap(rows, mask) for mask in (2, 6)] for rows in attended]
    own = []
    got = []
    sent = []
    for rows, other, close in zip(attended, others, near):
        local = [times(rows, here[half]) + times(other, sibling[half]) for half in range(2)]
        close, local, sent = lax.optimization_barrier((close, local, sent))
        totals = [
            local[half] + times(close[half], same[half]) + times(swap(close[half], 1), cross[half])
            for half in range(2)
        ]
        own.append([total[:, :512] for total in totals])
        sent = [total[:, 512:].astype(bf16) for total in totals]
        got.append([swap(part, mask) for part, mask in zip(sent, (6, 2))])

    delta = jnp.concatenate(
        [
            jnp.concatenate([a + b.astype(f32) for a, b in zip(*pair)], axis=1)
            for pair in zip(own, got)
        ],
        axis=0,
    )
    summed = hidden.astype(f32) + delta
    residual_out = summed.astype(bf16)
    squares = jnp.sum(summed * summed, axis=1)
    squares = squares + swap(squares, 1)
    squares = squares + swap(squares, 4) + swap(squares, 2) + swap(squares, 6)
    mean_square = squares / D
    normed = (summed * lax.rsqrt(mean_square + 1e-06)[:, None] * norm_gain[None, :]).astype(bf16)
    return (residual_out, normed)


def solution(mesh):
    return jax.shard_map(
        on_device,
        mesh=mesh,
        in_specs=(
            P("dp", "tensor"),
            P("dp", "tensor"),
            P("dp", "tensor"),
            P("dp", "tensor"),
            P("dp", None),
            P("dp", None),
            P("dp", None, None, "tensor"),
            P("dp", None, None, "tensor"),
            P("dp", None),
            P("tensor", None),
            P("tensor"),
        ),
        out_specs=(P("dp", "tensor"), P("dp", "tensor")),
        check_vma=False,
    )
```

```python
import functools
import math

import jax
import jax.numpy as jnp
from jax import lax
from jax.experimental import pallas as pl
from jax.experimental.pallas import tpu as pltpu
from jax.sharding import PartitionSpec as P

D = 8192
HEADS = 32
KV_HEADS = 8
HD = 128
MOST = 64
GROUP = HEADS // KV_HEADS
BLOCK = 32
FRESH = 128
PAIRS = 48
CHUNKS = 8
PIECE = 8
UNROLL = 8
LOW = -1e30
DEAD = 8192.0
SCALE = 1.0 / math.sqrt(HD)
NT = (((1,), (1,)), ((), ()))


def pair_plan(counts, packs):
    roll = counts.shape[0]
    ids = jnp.arange(roll, dtype=jnp.int32)
    before = ids[None, :] < ids[:, None]
    starts = jnp.sum(jnp.where(before, counts[None, :], 0), axis=1)
    ends = starts + counts
    first = starts // BLOCK
    spans = (ends - 1) // BLOCK - first + 1
    offsets = jnp.sum(jnp.where(before, spans[None, :], 0), axis=1)
    slot = jnp.arange(PAIRS, dtype=jnp.int32)[:, None]
    hit = (slot >= offsets[None, :]) & (slot < (offsets + spans)[None, :])

    def pick(values):
        return jnp.sum(jnp.where(hit, values, 0), axis=1)

    block = pick(first[None, :] + slot - offsets[None, :])
    ahead = jnp.sum(jnp.where((block < PIECE) & jnp.any(hit, axis=1), 1, 0))
    plan = jnp.stack(
        [
            block,
            pick(packs[None, :]),
            pick(starts[None, :]),
            pick(ends[None, :]),
            jnp.full((PAIRS,), ahead),
        ]
    ).astype(jnp.int32)
    rows = jnp.arange(512, dtype=jnp.int32)[:, None]
    row_start = jnp.max(jnp.where(starts[None, :] <= rows, starts[None, :], 0), axis=1)
    return plan, jnp.broadcast_to(row_start[:, None], (512, HD))


def stack_heads(ref, base):
    return [ref[pl.ds(base, BLOCK), h * HD : (h + 1) * HD] for h in range(GROUP)]


def payload_kernel(lengths_hbm, keys, values, out, lengths, held, sems, lengths_sem):
    packs, prefix, _ = keys.shape
    tile = packs // CHUNKS

    def copies(c):
        part = pl.ds(c * tile, tile)
        front, back = held.at[part, pl.ds(0, prefix)], held.at[part, pl.ds(prefix, prefix)]
        return (
            pltpu.make_async_copy(keys.at[part], front, sems.at[0, c]),
            pltpu.make_async_copy(values.at[part], back, sems.at[1, c]),
            pltpu.make_async_copy(held.at[part], out.at[part], sems.at[2, c]),
        )

    steps = [copies(c) for c in range(CHUNKS)]
    fetch = pltpu.make_async_copy(lengths_hbm, lengths, lengths_sem)
    fetch.start()
    for step in steps:
        step[0].start()
        step[1].start()
    fetch.wait()
    position = lax.broadcasted_iota(jnp.int32, keys.shape[1:], 0)
    for c, step in enumerate(steps):
        step[0].wait()
        for u in range(tile):
            pack = c * tile + u
            found = held[pack, :prefix].astype(jnp.float32)
            marked = jnp.where(position < lengths[0, pack], found, DEAD)
            held[pack, :prefix] = marked.astype(jnp.bfloat16)
        step[1].wait()
        step[2].start()
    for step in steps:
        step[2].wait()


def fresh_kernel(q, fresh_k, fresh_v, row_start, mean_out, level_out):
    def body(block, carry):
        base = pl.multiple_of(block * BLOCK, BLOCK)
        left = jnp.concatenate(stack_heads(q, base), axis=0)
        window = pl.ds(base, FRESH)
        found = lax.dot_general(left, fresh_k[window, :], NT, preferred_element_type=jnp.float32)
        key = base - (FRESH - BLOCK) + lax.broadcasted_iota(jnp.int32, found.shape, 1)
        sub = lax.broadcasted_iota(jnp.int32, found.shape, 0)
        row = base + jnp.bitwise_and(sub, BLOCK - 1)
        start = jnp.concatenate([row_start[pl.ds(base, BLOCK), :]] * GROUP, axis=0)
        found = jnp.where((key <= row) & (key >= start), found * SCALE, LOW)
        top = jnp.max(found, axis=1, keepdims=True)
        lifted = jnp.exp(found - top)
        total = jnp.sum(lifted, axis=1, keepdims=True)
        mean_out[block] = jnp.dot(
            (lifted / total).astype(jnp.bfloat16),
            fresh_v[window, :],
            preferred_element_type=jnp.float32,
        )
        level_out[block] = jnp.broadcast_to(top + jnp.log(total), found.shape)
        return carry

    lax.fori_loop(0, 512 // BLOCK, body, 0, unroll=2)


def main_kernel(first, plan, starts, q, cache_hbm, mean_hbm, level_hbm, *refs):
    cache, means, levels, scores, weights, mixed, sems, stage_sems = refs[-8:]
    stage = []
    if len(refs) > 9:
        own = [refs[16 + i % 2].at[pl.ds(512 * (i // 2), 512)] for i in range(8)]
        stage = staging(1, starts, refs[:6], refs[8:16], stage_sems.at[0])
        stage += staging(0, starts, refs[:6], own, stage_sems.at[1])
        out = refs[7]
    else:
        out = refs[0]
    half = cache.shape[1] // 2
    fetch = [
        pltpu.make_async_copy(
            cache_hbm.at[:, pl.ds(i * half, half)], cache.at[:, pl.ds(i * half, half)], sems.at[i]
        )
        for i in range(2)
    ]
    blocks = pl.ds(first, PIECE)
    fetch.append(pltpu.make_async_copy(level_hbm.at[blocks], levels, sems.at[2]))
    fetch.append(pltpu.make_async_copy(mean_hbm.at[blocks], means, sems.at[3]))
    for i in (0, 2, 3, 1):
        fetch[i].start()
    ones = jnp.ones((16, HD), jnp.bfloat16)
    ahead = plan[4, 0]
    if first == 0:
        lower, upper = 0, lax.div(ahead + UNROLL - 1, UNROLL)
    else:
        lower, upper = lax.div(ahead, UNROLL), PAIRS // UNROLL

    def place(i):
        block = plan[0, i] - first
        return jnp.where((block >= 0) & (block < PIECE), block, PIECE)

    def own_rows(base, i):
        row = base + lax.broadcasted_iota(jnp.int32, (BLOCK, HD), 0)
        return (row >= plan[2, i]) & (row < plan[3, i])

    def score(step, carry):
        for u in range(UNROLL):
            i = step * UNROLL + u
            block = place(i)
            base = pl.multiple_of(plan[0, i] * BLOCK, BLOCK)
            left = jnp.concatenate(stack_heads(q, base) + [ones], axis=0)
            both = lax.dot_general(
                left, cache[plan[1, i], :half], NT, preferred_element_type=jnp.float32
            )
            live = both[GROUP * BLOCK : GROUP * BLOCK + 1] < 32.0 * DEAD
            found = jnp.where(live, both[: GROUP * BLOCK] * SCALE, LOW)
            mine = own_rows(base, i)
            for h in range(GROUP):
                part = pl.ds(h * BLOCK, BLOCK)
                scores[block, part] = jnp.where(
                    mine, found[h * BLOCK : (h + 1) * BLOCK], scores[block, part]
                )
        return carry

    def soften(block, carry):
        cached = scores[block]
        level = levels[block]
        top = jnp.maximum(jnp.max(cached, axis=1, keepdims=True), level)
        lifted = jnp.exp(cached - top)
        fresh = jnp.exp(level - top)
        share = 1.0 / (jnp.sum(lifted, axis=1, keepdims=True) + fresh)
        weights[block] = (lifted * share).astype(jnp.bfloat16)
        mixed[block] = means[block] * (fresh * share)
        return carry

    def mix(step, carry):
        for u in range(UNROLL):
            i = step * UNROLL + u
            block = place(i)
            found = jnp.dot(
                weights[block], cache[plan[1, i], half:], preferred_element_type=jnp.float32
            )
            mine = own_rows(plan[0, i] * BLOCK, i)
            for h in range(GROUP):
                part = pl.ds(h * BLOCK, BLOCK)
                mixed[block, part] += jnp.where(mine, found[h * BLOCK : (h + 1) * BLOCK], 0.0)
        return carry

    fetch[0].wait()
    for copy in stage:
        copy.start()
    lax.fori_loop(lower, upper, score, 0)
    fetch[2].wait()
    fetch[3].wait()
    lax.fori_loop(0, PIECE, soften, 0, unroll=PIECE)
    fetch[1].wait()
    lax.fori_loop(lower, upper, mix, 0)
    for block in range(PIECE):
        total = mixed[block].astype(jnp.bfloat16)
        base = block * BLOCK
        for h in range(GROUP):
            out[base : base + BLOCK, h * HD : (h + 1) * HD] = total[h * BLOCK : (h + 1) * BLOCK]
    for copy in stage:
        copy.wait()


def whole(count):
    return [pl.BlockSpec(memory_space=pltpu.VMEM)] * count


def in_hbm(*values):
    return [pltpu.with_memory_space_constraint(value, pltpu.HBM) for value in values]


def far(count):
    return [pl.BlockSpec(memory_space=pltpu.HBM)] * count


def anywhere(count):
    return [pl.BlockSpec(memory_space=pl.ANY)] * count


def make_payload(lengths, keys, values):
    packs, prefix, width = keys.shape
    return pl.pallas_call(
        payload_kernel,
        out_shape=jax.ShapeDtypeStruct((packs, 2 * prefix, width), keys.dtype),
        in_specs=far(3),
        out_specs=far(1)[0],
        scratch_shapes=[
            pltpu.SMEM(lengths.shape, lengths.dtype),
            pltpu.VMEM((packs, 2 * prefix, width), keys.dtype),
            pltpu.SemaphoreType.DMA((3, CHUNKS)),
            pltpu.SemaphoreType.DMA,
        ],
        compiler_params=pltpu.CompilerParams(vmem_limit_bytes=4 << 20),
        cost_estimate=pl.CostEstimate(flops=1 << 20, bytes_accessed=4 << 20, transcendentals=0),
    )(*in_hbm(lengths, keys, values))


def cut_kernel(starts, weight, after, *refs):
    outs, sems = refs[:-1], refs[-1]
    copies = []
    for out in outs:
        for i in range(out.shape[0] // 512):
            slot = len(copies)
            source = weight.at[:, pl.ds(pl.multiple_of(starts[slot], 512), 512)]
            target = out.at[pl.ds(i * 512, 512)]
            copies.append(pltpu.make_async_copy(source, target, sems.at[slot]))
    for copy in copies:
        copy.start()
    for copy in copies:
        copy.wait()


def cut(starts, weight, heights, after):
    return pl.pallas_call(
        cut_kernel,
        out_shape=tuple(pltpu.VMEM((height, 512), weight.dtype) for height in heights),
        grid_spec=pltpu.PrefetchScalarGridSpec(
            num_scalar_prefetch=1,
            grid=(),
            in_specs=far(1) + anywhere(1),
            out_specs=tuple(whole(len(heights))),
            scratch_shapes=[pltpu.SemaphoreType.DMA((sum(heights) // 512,))],
        ),
        compiler_params=pltpu.CompilerParams(vmem_limit_bytes=8 << 20),
        cost_estimate=pl.CostEstimate(flops=0, bytes_accessed=12 << 20, transcendentals=0),
    )(starts, *in_hbm(weight), after)


def staging(part, starts, sources, targets, sems):
    weight, sibling, *near = sources
    blocks = []
    for half in range(2):
        start = pl.multiple_of(starts[2 * half + part], 512)
        blocks.append(weight.at[:, pl.ds(start, 512)])
    for half in range(2):
        blocks.append(sibling.at[pl.ds(1024 * half + 512 * part, 512)])
    blocks += [block.at[pl.ds(512 * part, 512)] for block in near]
    return [
        pltpu.make_async_copy(block, target, sems.at[i])
        for i, (block, target) in enumerate(zip(blocks, targets))
    ]


def attend_fresh(queries, new_keys, new_values, row_start):
    front = ((FRESH - BLOCK, 0), (0, 0))
    area = jax.ShapeDtypeStruct((512 // BLOCK, GROUP * BLOCK, HD), jnp.float32)
    return pl.pallas_call(
        fresh_kernel,
        out_shape=(area, area),
        in_specs=whole(4),
        out_specs=tuple(whole(2)),
        compiler_params=pltpu.CompilerParams(vmem_limit_bytes=5 << 20),
        cost_estimate=pl.CostEstimate(
            flops=1 << 31, bytes_accessed=4 << 20, transcendentals=1 << 18
        ),
    )(queries, jnp.pad(new_keys, front), jnp.pad(new_values, front), row_start)


def attend(first, plan, starts, queries, cache, fresh, sources=(), after=()):
    area = fresh[0].shape[1:]
    rows = jax.ShapeDtypeStruct((PIECE * BLOCK, queries.shape[1]), queries.dtype)
    staged = []
    if sources:
        staged = [pltpu.VMEM((512, 512), queries.dtype)] * 8
        staged += [pltpu.VMEM((2048, 512), queries.dtype)] * 2
    return pl.pallas_call(
        functools.partial(main_kernel, first),
        out_shape=(rows, *staged),
        grid_spec=pltpu.PrefetchScalarGridSpec(
            num_scalar_prefetch=2,
            grid=(),
            in_specs=whole(1) + anywhere(3 + len(sources) + len(after)),
            out_specs=tuple(whole(1 + len(staged))),
            scratch_shapes=[
                pltpu.VMEM(cache.shape, cache.dtype),
                pltpu.VMEM((PIECE, *area), jnp.float32),
                pltpu.VMEM((PIECE, *area), jnp.float32),
                pltpu.VMEM((PIECE + 1, *area), jnp.float32),
                pltpu.VMEM((PIECE + 1, *area), jnp.bfloat16),
                pltpu.VMEM((PIECE + 1, *area), jnp.float32),
                pltpu.SemaphoreType.DMA((4,)),
                pltpu.SemaphoreType.DMA((2, 8)),
            ],
        ),
        compiler_params=pltpu.CompilerParams(vmem_limit_bytes=(16 if sources else 7) << 20),
        cost_estimate=pl.CostEstimate(
            flops=1 << 31, bytes_accessed=4 << 20, transcendentals=1 << 18
        ),
    )(plan, starts, queries, cache, *in_hbm(*fresh), *in_hbm(*sources), *after)


def on_device(
    queries,
    new_keys,
    new_values,
    hidden,
    row_counts,
    pack_of,
    cache_keys,
    cache_values,
    prefix_lengths,
    out_weight,
    norm_gain,
):
    count = lax.axis_size("tensor")
    me = lax.axis_index("tensor")
    f32 = jnp.float32
    bf16 = jnp.bfloat16

    def swap(value, mask):
        return lax.ppermute(value, "tensor", [(t, t ^ mask) for t in range(count)])

    def shared(mask):
        to = jnp.bitwise_xor(me, mask)
        first = [to * 1024, jnp.bitwise_xor(to, 6) * 1024]
        second = [to * 1024 + 512, jnp.bitwise_xor(to, 2) * 1024 + 512]
        return first, second

    payload = make_payload(prefix_lengths, cache_keys[0], cache_values[0])
    cache = lax.all_to_all(payload, "dp", split_axis=0, concat_axis=0, tiled=True)

    starts = sum([shared(mask)[half] for mask, half in ((2, 0), (6, 1), (3, 0), (7, 1))], [])
    starts = jnp.stack(starts + sum(shared(1), []))
    pieces = cut(starts, out_weight, (1024, 1024, 1024, 1024, 2048), payload)
    *near_mats, sibling = [swap(piece, mask) for piece, mask in zip(pieces, (2, 6, 3, 7, 1))]

    plan, row_start = pair_plan(row_counts[0], pack_of[0])
    fresh = attend_fresh(queries, new_keys, new_values, row_start)
    plan, sibling, near_mats[:2] = lax.optimization_barrier((plan, sibling, near_mats[:2]))
    starts = jnp.stack(sum(shared(0), []))
    first = attend(0, plan, starts, queries, cache, fresh)[0]
    sources = (out_weight, sibling, *near_mats)
    others_a = swap(first, 1)
    second, *mats, own_0, own_1 = attend(PIECE, plan, starts, queries, cache, fresh, sources, (others_a,))
    attended = [first, second]

    def times(rows, mat):
        return jnp.dot(rows, mat, preferred_element_type=f32)

    others = [others_a, swap(second, 1)]
    near = [[swap(rows, mask) for mask in (2, 6)] for rows in attended]
    inputs = []
    got = []
    sent = []
    for rows, other, close in zip(attended, others, near):
        local = [times(rows, mats[half]) + times(other, mats[2 + half]) for half in range(2)]
        close, local, sent = lax.optimization_barrier((close, local, sent))
        side = [swap(part, 1) for part in close]
        sent = [
            local[half] + times(close[half], mats[4 + half]) + times(side[half], mats[6 + half])
            for half in range(2)
        ]
        sent = [total.astype(bf16) for total in sent]
        sent, side = lax.optimization_barrier((sent, side))
        got.append([swap(part, mask) for part, mask in zip(sent, (6, 2))])
        inputs.append([[rows, other, close[half], side[half]] for half in range(2)])

    got[0], inputs = lax.optimization_barrier((got[0], inputs))
    own = [
        times(
            jnp.concatenate([jnp.concatenate(halves[half], axis=1) for halves in inputs], axis=0),
            mat,
        )
        for half, mat in enumerate((own_0, own_1))
    ]
    own = lax.optimization_barrier(own)
    delta = jnp.concatenate(
        [
            own[half] + jnp.concatenate([pair[half] for pair in got], axis=0).astype(f32)
            for half in range(2)
        ],
        axis=1,
    )
    summed = hidden.astype(f32) + delta
    residual_out = summed.astype(bf16)
    squares = jnp.sum(summed * summed, axis=1)
    squares = squares + swap(squares, 1)
    squares = squares + swap(squares, 4) + swap(squares, 2) + swap(squares, 6)
    mean_square = squares / D
    normed = (summed * lax.rsqrt(mean_square + 1e-06)[:, None] * norm_gain[None, :]).astype(bf16)
    return (residual_out, normed)


def solution(mesh):
    return jax.shard_map(
        on_device,
        mesh=mesh,
        in_specs=(
            P("dp", "tensor"),
            P("dp", "tensor"),
            P("dp", "tensor"),
            P("dp", "tensor"),
            P("dp", None),
            P("dp", None),
            P("dp", None, None, "tensor"),
            P("dp", None, None, "tensor"),
            P("dp", None),
            P("tensor", None),
            P("tensor"),
        ),
        out_specs=(P("dp", "tensor"), P("dp", "tensor")),
        check_vma=False,
    )
```

```python
import functools
import math

import jax
import jax.numpy as jnp
from jax import lax
from jax.experimental import pallas as pl
from jax.experimental.pallas import tpu as pltpu
from jax.sharding import PartitionSpec as P

D = 8192
HEADS = 32
KV_HEADS = 8
HD = 128
MOST = 64
GROUP = HEADS // KV_HEADS
BLOCK = 32
FRESH = 128
PAIRS = 48
CHUNKS = 8
PIECE = 8
UNROLL = 8
LOW = -1e30
DEAD = 8192.0
SCALE = 1.0 / math.sqrt(HD)
NT = (((1,), (1,)), ((), ()))


def pair_plan(counts, packs):
    roll = counts.shape[0]
    ids = jnp.arange(roll, dtype=jnp.int32)
    before = ids[None, :] < ids[:, None]
    starts = jnp.sum(jnp.where(before, counts[None, :], 0), axis=1)
    ends = starts + counts
    first = starts // BLOCK
    spans = (ends - 1) // BLOCK - first + 1
    offsets = jnp.sum(jnp.where(before, spans[None, :], 0), axis=1)
    slot = jnp.arange(PAIRS, dtype=jnp.int32)[:, None]
    hit = (slot >= offsets[None, :]) & (slot < (offsets + spans)[None, :])

    def pick(values):
        return jnp.sum(jnp.where(hit, values, 0), axis=1)

    block = pick(first[None, :] + slot - offsets[None, :])
    ahead = jnp.sum(jnp.where((block < PIECE) & jnp.any(hit, axis=1), 1, 0))
    plan = jnp.stack(
        [
            block,
            pick(packs[None, :]),
            pick(starts[None, :]),
            pick(ends[None, :]),
            jnp.full((PAIRS,), ahead),
        ]
    ).astype(jnp.int32)
    rows = jnp.arange(512, dtype=jnp.int32)[:, None]
    row_start = jnp.max(jnp.where(starts[None, :] <= rows, starts[None, :], 0), axis=1)
    return plan, jnp.broadcast_to(row_start[:, None], (512, HD))


def stack_heads(ref, base):
    return [ref[pl.ds(base, BLOCK), h * HD : (h + 1) * HD] for h in range(GROUP)]


def payload_kernel(lengths_hbm, keys, values, out, lengths, held, sems, lengths_sem):
    packs, prefix, _ = keys.shape
    tile = packs // CHUNKS

    def copies(c):
        part = pl.ds(c * tile, tile)
        front, back = held.at[part, pl.ds(0, prefix)], held.at[part, pl.ds(prefix, prefix)]
        return (
            pltpu.make_async_copy(keys.at[part], front, sems.at[0, c]),
            pltpu.make_async_copy(values.at[part], back, sems.at[1, c]),
            pltpu.make_async_copy(held.at[part], out.at[part], sems.at[2, c]),
        )

    steps = [copies(c) for c in range(CHUNKS)]
    fetch = pltpu.make_async_copy(lengths_hbm, lengths, lengths_sem)
    fetch.start()
    for step in steps:
        step[0].start()
        step[1].start()
    fetch.wait()
    position = lax.broadcasted_iota(jnp.int32, keys.shape[1:], 0)
    for c, step in enumerate(steps):
        step[0].wait()
        for u in range(tile):
            pack = c * tile + u
            found = held[pack, :prefix].astype(jnp.float32)
            marked = jnp.where(position < lengths[0, pack], found, DEAD)
            held[pack, :prefix] = marked.astype(jnp.bfloat16)
        step[1].wait()
        step[2].start()
    for step in steps:
        step[2].wait()


def fresh_kernel(q, fresh_k, fresh_v, row_start, mean_out, level_out):
    def body(block, carry):
        base = pl.multiple_of(block * BLOCK, BLOCK)
        left = jnp.concatenate(stack_heads(q, base), axis=0)
        window = pl.ds(base, FRESH)
        found = lax.dot_general(left, fresh_k[window, :], NT, preferred_element_type=jnp.float32)
        key = base - (FRESH - BLOCK) + lax.broadcasted_iota(jnp.int32, found.shape, 1)
        sub = lax.broadcasted_iota(jnp.int32, found.shape, 0)
        row = base + jnp.bitwise_and(sub, BLOCK - 1)
        start = jnp.concatenate([row_start[pl.ds(base, BLOCK), :]] * GROUP, axis=0)
        found = jnp.where((key <= row) & (key >= start), found * SCALE, LOW)
        top = jnp.max(found, axis=1, keepdims=True)
        lifted = jnp.exp(found - top)
        total = jnp.sum(lifted, axis=1, keepdims=True)
        mean_out[block] = jnp.dot(
            (lifted / total).astype(jnp.bfloat16),
            fresh_v[window, :],
            preferred_element_type=jnp.float32,
        )
        level_out[block] = jnp.broadcast_to(top + jnp.log(total), found.shape)
        return carry

    lax.fori_loop(0, 512 // BLOCK, body, 0, unroll=2)


def main_kernel(first, plan, starts, q, cache_hbm, mean_hbm, level_hbm, *refs):
    cache, means, levels, scores, weights, mixed, sems, stage_sems = refs[-8:]
    stage = []
    if len(refs) > 9:
        own = [refs[16 + i % 2].at[pl.ds(512 * (i // 2), 512)] for i in range(8)]
        stage = staging(1, starts, refs[:6], refs[8:16], stage_sems.at[0])
        stage += staging(0, starts, refs[:6], own, stage_sems.at[1])
        out = refs[7]
    else:
        out = refs[0]
    half = cache.shape[1] // 2
    fetch = [
        pltpu.make_async_copy(
            cache_hbm.at[:, pl.ds(i * half, half)], cache.at[:, pl.ds(i * half, half)], sems.at[i]
        )
        for i in range(2)
    ]
    blocks = pl.ds(first, PIECE)
    fetch.append(pltpu.make_async_copy(level_hbm.at[blocks], levels, sems.at[2]))
    fetch.append(pltpu.make_async_copy(mean_hbm.at[blocks], means, sems.at[3]))
    for i in (0, 2, 3, 1):
        fetch[i].start()
    ones = jnp.ones((16, HD), jnp.bfloat16)
    ahead = plan[4, 0]
    if first == 0:
        lower, upper = 0, lax.div(ahead + UNROLL - 1, UNROLL)
    else:
        lower, upper = lax.div(ahead, UNROLL), PAIRS // UNROLL

    def place(i):
        block = plan[0, i] - first
        return jnp.where((block >= 0) & (block < PIECE), block, PIECE)

    def own_rows(base, i):
        row = base + lax.broadcasted_iota(jnp.int32, (BLOCK, HD), 0)
        return (row >= plan[2, i]) & (row < plan[3, i])

    def score(step, carry):
        for u in range(UNROLL):
            i = step * UNROLL + u
            block = place(i)
            base = pl.multiple_of(plan[0, i] * BLOCK, BLOCK)
            left = jnp.concatenate(stack_heads(q, base) + [ones], axis=0)
            both = lax.dot_general(
                left, cache[plan[1, i], :half], NT, preferred_element_type=jnp.float32
            )
            live = both[GROUP * BLOCK : GROUP * BLOCK + 1] < 32.0 * DEAD
            found = jnp.where(live, both[: GROUP * BLOCK] * SCALE, LOW)
            mine = own_rows(base, i)
            for h in range(GROUP):
                part = pl.ds(h * BLOCK, BLOCK)
                scores[block, part] = jnp.where(
                    mine, found[h * BLOCK : (h + 1) * BLOCK], scores[block, part]
                )
        return carry

    def soften(block, carry):
        cached = scores[block]
        level = levels[block]
        top = jnp.maximum(jnp.max(cached, axis=1, keepdims=True), level)
        lifted = jnp.exp(cached - top)
        fresh = jnp.exp(level - top)
        share = 1.0 / (jnp.sum(lifted, axis=1, keepdims=True) + fresh)
        weights[block] = (lifted * share).astype(jnp.bfloat16)
        mixed[block] = means[block] * (fresh * share)
        return carry

    def mix(step, carry):
        for u in range(UNROLL):
            i = step * UNROLL + u
            block = place(i)
            found = jnp.dot(
                weights[block], cache[plan[1, i], half:], preferred_element_type=jnp.float32
            )
            mine = own_rows(plan[0, i] * BLOCK, i)
            for h in range(GROUP):
                part = pl.ds(h * BLOCK, BLOCK)
                mixed[block, part] += jnp.where(mine, found[h * BLOCK : (h + 1) * BLOCK], 0.0)
        return carry

    fetch[0].wait()
    for copy in stage:
        copy.start()
    lax.fori_loop(lower, upper, score, 0)
    fetch[2].wait()
    fetch[3].wait()
    lax.fori_loop(0, PIECE, soften, 0, unroll=PIECE)
    fetch[1].wait()
    lax.fori_loop(lower, upper, mix, 0)
    for block in range(PIECE):
        total = mixed[block].astype(jnp.bfloat16)
        base = block * BLOCK
        for h in range(GROUP):
            out[base : base + BLOCK, h * HD : (h + 1) * HD] = total[h * BLOCK : (h + 1) * BLOCK]
    for copy in stage:
        copy.wait()


def whole(count):
    return [pl.BlockSpec(memory_space=pltpu.VMEM)] * count


def in_hbm(*values):
    return [pltpu.with_memory_space_constraint(value, pltpu.HBM) for value in values]


def far(count):
    return [pl.BlockSpec(memory_space=pltpu.HBM)] * count


def anywhere(count):
    return [pl.BlockSpec(memory_space=pl.ANY)] * count


def make_payload(lengths, keys, values):
    packs, prefix, width = keys.shape
    return pl.pallas_call(
        payload_kernel,
        out_shape=jax.ShapeDtypeStruct((packs, 2 * prefix, width), keys.dtype),
        in_specs=far(3),
        out_specs=far(1)[0],
        scratch_shapes=[
            pltpu.SMEM(lengths.shape, lengths.dtype),
            pltpu.VMEM((packs, 2 * prefix, width), keys.dtype),
            pltpu.SemaphoreType.DMA((3, CHUNKS)),
            pltpu.SemaphoreType.DMA,
        ],
        compiler_params=pltpu.CompilerParams(vmem_limit_bytes=4 << 20),
        cost_estimate=pl.CostEstimate(flops=1 << 20, bytes_accessed=4 << 20, transcendentals=0),
    )(*in_hbm(lengths, keys, values))


def cut_kernel(starts, weight, after, *refs):
    outs, sems = refs[:-1], refs[-1]
    copies = []
    for out in outs:
        for i in range(out.shape[0] // 512):
            slot = len(copies)
            source = weight.at[:, pl.ds(pl.multiple_of(starts[slot], 512), 512)]
            target = out.at[pl.ds(i * 512, 512)]
            copies.append(pltpu.make_async_copy(source, target, sems.at[slot]))
    for copy in copies:
        copy.start()
    for copy in copies:
        copy.wait()


def cut(starts, weight, heights, after):
    return pl.pallas_call(
        cut_kernel,
        out_shape=tuple(pltpu.VMEM((height, 512), weight.dtype) for height in heights),
        grid_spec=pltpu.PrefetchScalarGridSpec(
            num_scalar_prefetch=1,
            grid=(),
            in_specs=far(1) + anywhere(1),
            out_specs=tuple(whole(len(heights))),
            scratch_shapes=[pltpu.SemaphoreType.DMA((sum(heights) // 512,))],
        ),
        compiler_params=pltpu.CompilerParams(vmem_limit_bytes=8 << 20),
        cost_estimate=pl.CostEstimate(flops=0, bytes_accessed=12 << 20, transcendentals=0),
    )(starts, *in_hbm(weight), after)


def staging(part, starts, sources, targets, sems):
    weight, sibling, *near = sources
    blocks = []
    for half in range(2):
        start = pl.multiple_of(starts[2 * half + part], 512)
        blocks.append(weight.at[:, pl.ds(start, 512)])
    for half in range(2):
        blocks.append(sibling.at[pl.ds(1024 * half + 512 * part, 512)])
    blocks += [block.at[pl.ds(512 * part, 512)] for block in near]
    return [
        pltpu.make_async_copy(block, target, sems.at[i])
        for i, (block, target) in enumerate(zip(blocks, targets))
    ]


def attend_fresh(queries, new_keys, new_values, row_start):
    front = ((FRESH - BLOCK, 0), (0, 0))
    area = jax.ShapeDtypeStruct((512 // BLOCK, GROUP * BLOCK, HD), jnp.float32)
    return pl.pallas_call(
        fresh_kernel,
        out_shape=(area, area),
        in_specs=whole(4),
        out_specs=tuple(whole(2)),
        compiler_params=pltpu.CompilerParams(vmem_limit_bytes=5 << 20),
        cost_estimate=pl.CostEstimate(
            flops=1 << 31, bytes_accessed=4 << 20, transcendentals=1 << 18
        ),
    )(queries, jnp.pad(new_keys, front), jnp.pad(new_values, front), row_start)


def attend(first, plan, starts, queries, cache, fresh, sources=(), after=()):
    area = fresh[0].shape[1:]
    rows = jax.ShapeDtypeStruct((PIECE * BLOCK, queries.shape[1]), queries.dtype)
    staged = []
    if sources:
        staged = [pltpu.VMEM((512, 512), queries.dtype)] * 8
        staged += [pltpu.VMEM((2048, 512), queries.dtype)] * 2
    return pl.pallas_call(
        functools.partial(main_kernel, first),
        out_shape=(rows, *staged),
        grid_spec=pltpu.PrefetchScalarGridSpec(
            num_scalar_prefetch=2,
            grid=(),
            in_specs=whole(1) + anywhere(3 + len(sources) + len(after)),
            out_specs=tuple(whole(1 + len(staged))),
            scratch_shapes=[
                pltpu.VMEM(cache.shape, cache.dtype),
                pltpu.VMEM((PIECE, *area), jnp.float32),
                pltpu.VMEM((PIECE, *area), jnp.float32),
                pltpu.VMEM((PIECE + 1, *area), jnp.float32),
                pltpu.VMEM((PIECE + 1, *area), jnp.bfloat16),
                pltpu.VMEM((PIECE + 1, *area), jnp.float32),
                pltpu.SemaphoreType.DMA((4,)),
                pltpu.SemaphoreType.DMA((2, 8)),
            ],
        ),
        compiler_params=pltpu.CompilerParams(vmem_limit_bytes=(16 if sources else 7) << 20),
        cost_estimate=pl.CostEstimate(
            flops=1 << 31, bytes_accessed=4 << 20, transcendentals=1 << 18
        ),
    )(plan, starts, queries, cache, *in_hbm(*fresh), *in_hbm(*sources), *after)


def on_device(
    queries,
    new_keys,
    new_values,
    hidden,
    row_counts,
    pack_of,
    cache_keys,
    cache_values,
    prefix_lengths,
    out_weight,
    norm_gain,
):
    count = lax.axis_size("tensor")
    me = lax.axis_index("tensor")
    f32 = jnp.float32
    bf16 = jnp.bfloat16

    def swap(value, mask):
        return lax.ppermute(value, "tensor", [(t, t ^ mask) for t in range(count)])

    def shared(mask):
        to = jnp.bitwise_xor(me, mask)
        first = [to * 1024, jnp.bitwise_xor(to, 6) * 1024]
        second = [to * 1024 + 512, jnp.bitwise_xor(to, 2) * 1024 + 512]
        return first, second

    payload = make_payload(prefix_lengths, cache_keys[0], cache_values[0])
    cache = lax.all_to_all(payload, "dp", split_axis=0, concat_axis=0, tiled=True)

    starts = sum([shared(mask)[half] for mask, half in ((2, 0), (6, 1), (3, 0), (7, 1))], [])
    starts = jnp.stack(starts + sum(shared(1), []))
    pieces = cut(starts, out_weight, (1024, 1024, 1024, 1024, 2048), payload)
    *near_mats, sibling = [swap(piece, mask) for piece, mask in zip(pieces, (2, 6, 3, 7, 1))]

    plan, row_start = pair_plan(row_counts[0], pack_of[0])
    fresh = attend_fresh(queries, new_keys, new_values, row_start)
    plan, sibling, near_mats[:2] = lax.optimization_barrier((plan, sibling, near_mats[:2]))
    starts = jnp.stack(sum(shared(0), []))
    first = attend(0, plan, starts, queries, cache, fresh)[0]
    sources = (out_weight, sibling, *near_mats)
    others_a = swap(first, 1)
    second, *mats, own_0, own_1 = attend(PIECE, plan, starts, queries, cache, fresh, sources, (others_a,))
    attended = [first, second]

    def times(rows, mat):
        return jnp.dot(rows, mat, preferred_element_type=f32)

    others = [others_a, swap(second, 1)]
    near = [[swap(rows, mask) for mask in (2, 6)] for rows in attended]
    inputs = []
    got = []
    sent = []
    for rows, other, close in zip(attended, others, near):
        if sent:
            sent, inputs[0] = lax.optimization_barrier((sent, inputs[0]))
            got.append([swap(part, mask) for part, mask in zip(sent, (6, 2))])
        local = [times(rows, mats[half]) + times(other, mats[2 + half]) for half in range(2)]
        local = lax.optimization_barrier(local)
        side = [swap(part, 1) for part in close]
        sent = [
            local[half] + times(close[half], mats[4 + half]) + times(side[half], mats[6 + half])
            for half in range(2)
        ]
        sent = [total.astype(bf16) for total in sent]
        inputs.append([[rows, other, close[half], side[half]] for half in range(2)])
    sent, inputs[1] = lax.optimization_barrier((sent, inputs[1]))
    got.append([swap(part, mask) for part, mask in zip(sent, (6, 2))])

    own = [
        [times(jnp.concatenate(parts, axis=1), mat) for parts, mat in zip(halves, (own_0, own_1))]
        for halves in inputs
    ]
    own = [[lax.optimization_barrier(part) for part in halves] for halves in own]
    delta = jnp.concatenate(
        [
            jnp.concatenate([mine + part.astype(f32) for mine, part in zip(*pair)], axis=1)
            for pair in zip(own, got)
        ],
        axis=0,
    )
    summed = hidden.astype(f32) + delta
    residual_out = summed.astype(bf16)
    squares = jnp.sum(summed * summed, axis=1)
    squares = squares + swap(squares, 1)
    squares = squares + swap(squares, 4) + swap(squares, 2) + swap(squares, 6)
    mean_square = squares / D
    normed = (summed * lax.rsqrt(mean_square + 1e-06)[:, None] * norm_gain[None, :]).astype(bf16)
    return (residual_out, normed)


def solution(mesh):
    return jax.shard_map(
        on_device,
        mesh=mesh,
        in_specs=(
            P("dp", "tensor"),
            P("dp", "tensor"),
            P("dp", "tensor"),
            P("dp", "tensor"),
            P("dp", None),
            P("dp", None),
            P("dp", None, None, "tensor"),
            P("dp", None, None, "tensor"),
            P("dp", None),
            P("tensor", None),
            P("tensor"),
        ),
        out_specs=(P("dp", "tensor"), P("dp", "tensor")),
        check_vma=False,
    )
```

```python
import functools
import math

import jax
import jax.numpy as jnp
from jax import lax
from jax.experimental import pallas as pl
from jax.experimental.pallas import tpu as pltpu
from jax.sharding import PartitionSpec as P

D = 8192
HEADS = 32
KV_HEADS = 8
HD = 128
MOST = 64
GROUP = HEADS // KV_HEADS
BLOCK = 32
FRESH = 128
PAIRS = 48
CHUNKS = 8
PIECE = 8
UNROLL = 8
LOW = -1e30
DEAD = 8192.0
SCALE = 1.0 / math.sqrt(HD)
NT = (((1,), (1,)), ((), ()))


def pair_plan(counts, packs):
    roll = counts.shape[0]
    ids = jnp.arange(roll, dtype=jnp.int32)
    before = ids[None, :] < ids[:, None]
    starts = jnp.sum(jnp.where(before, counts[None, :], 0), axis=1)
    ends = starts + counts
    first = starts // BLOCK
    spans = (ends - 1) // BLOCK - first + 1
    offsets = jnp.sum(jnp.where(before, spans[None, :], 0), axis=1)
    slot = jnp.arange(PAIRS, dtype=jnp.int32)[:, None]
    hit = (slot >= offsets[None, :]) & (slot < (offsets + spans)[None, :])

    def pick(values):
        return jnp.sum(jnp.where(hit, values, 0), axis=1)

    block = pick(first[None, :] + slot - offsets[None, :])
    ahead = jnp.sum(jnp.where((block < PIECE) & jnp.any(hit, axis=1), 1, 0))
    plan = jnp.stack(
        [
            block,
            pick(packs[None, :]),
            pick(starts[None, :]),
            pick(ends[None, :]),
            jnp.full((PAIRS,), ahead),
        ]
    ).astype(jnp.int32)
    rows = jnp.arange(512, dtype=jnp.int32)[:, None]
    row_start = jnp.max(jnp.where(starts[None, :] <= rows, starts[None, :], 0), axis=1)
    return plan, jnp.broadcast_to(row_start[:, None], (512, HD))


def stack_heads(ref, base):
    return [ref[pl.ds(base, BLOCK), h * HD : (h + 1) * HD] for h in range(GROUP)]


def payload_kernel(lengths_hbm, keys, values, out, lengths, held, sems, lengths_sem):
    packs, prefix, _ = keys.shape
    tile = packs // CHUNKS

    def copies(c):
        part = pl.ds(c * tile, tile)
        front, back = held.at[part, pl.ds(0, prefix)], held.at[part, pl.ds(prefix, prefix)]
        return (
            pltpu.make_async_copy(keys.at[part], front, sems.at[0, c]),
            pltpu.make_async_copy(values.at[part], back, sems.at[1, c]),
            pltpu.make_async_copy(held.at[part], out.at[part], sems.at[2, c]),
        )

    steps = [copies(c) for c in range(CHUNKS)]
    fetch = pltpu.make_async_copy(lengths_hbm, lengths, lengths_sem)
    fetch.start()
    for step in steps:
        step[0].start()
        step[1].start()
    fetch.wait()
    position = lax.broadcasted_iota(jnp.int32, keys.shape[1:], 0)
    for c, step in enumerate(steps):
        step[0].wait()
        for u in range(tile):
            pack = c * tile + u
            found = held[pack, :prefix].astype(jnp.float32)
            marked = jnp.where(position < lengths[0, pack], found, DEAD)
            held[pack, :prefix] = marked.astype(jnp.bfloat16)
        step[1].wait()
        step[2].start()
    for step in steps:
        step[2].wait()


def fresh_kernel(q, fresh_k, fresh_v, row_start, mean_out, level_out):
    def body(block, carry):
        base = pl.multiple_of(block * BLOCK, BLOCK)
        left = jnp.concatenate(stack_heads(q, base), axis=0)
        window = pl.ds(base, FRESH)
        found = lax.dot_general(left, fresh_k[window, :], NT, preferred_element_type=jnp.float32)
        key = base - (FRESH - BLOCK) + lax.broadcasted_iota(jnp.int32, found.shape, 1)
        sub = lax.broadcasted_iota(jnp.int32, found.shape, 0)
        row = base + jnp.bitwise_and(sub, BLOCK - 1)
        start = jnp.concatenate([row_start[pl.ds(base, BLOCK), :]] * GROUP, axis=0)
        found = jnp.where((key <= row) & (key >= start), found * SCALE, LOW)
        top = jnp.max(found, axis=1, keepdims=True)
        lifted = jnp.exp(found - top)
        total = jnp.sum(lifted, axis=1, keepdims=True)
        mean_out[block] = jnp.dot(
            (lifted / total).astype(jnp.bfloat16),
            fresh_v[window, :],
            preferred_element_type=jnp.float32,
        )
        level_out[block] = jnp.broadcast_to(top + jnp.log(total), found.shape)
        return carry

    lax.fori_loop(0, 512 // BLOCK, body, 0, unroll=2)


def main_kernel(first, plan, starts, q, cache_hbm, mean_hbm, level_hbm, *refs):
    cache, means, levels, scores, weights, mixed, sems, stage_sems = refs[-8:]
    count, waits = (2, 0) if first == 0 else (4, 1)
    out, *targets = refs[count + waits : -8]
    own = [targets[4 + i % 2].at[pl.ds(512 * (i // 2), 512)] for i in range(4)]
    stage = staging(1, starts, refs[:count], targets[:4], stage_sems.at[0])
    stage += staging(0, starts, refs[:count], own, stage_sems.at[1])
    half = cache.shape[1] // 2
    fetch = [
        pltpu.make_async_copy(
            cache_hbm.at[:, pl.ds(i * half, half)], cache.at[:, pl.ds(i * half, half)], sems.at[i]
        )
        for i in range(2)
    ]
    blocks = pl.ds(first, PIECE)
    fetch.append(pltpu.make_async_copy(level_hbm.at[blocks], levels, sems.at[2]))
    fetch.append(pltpu.make_async_copy(mean_hbm.at[blocks], means, sems.at[3]))
    for i in (0, 2, 3, 1):
        fetch[i].start()
    ones = jnp.ones((16, HD), jnp.bfloat16)
    ahead = plan[4, 0]
    if first == 0:
        lower, upper = 0, lax.div(ahead + UNROLL - 1, UNROLL)
    else:
        lower, upper = lax.div(ahead, UNROLL), PAIRS // UNROLL

    def place(i):
        block = plan[0, i] - first
        return jnp.where((block >= 0) & (block < PIECE), block, PIECE)

    def own_rows(base, i):
        row = base + lax.broadcasted_iota(jnp.int32, (BLOCK, HD), 0)
        return (row >= plan[2, i]) & (row < plan[3, i])

    def score(step, carry):
        for u in range(UNROLL):
            i = step * UNROLL + u
            block = place(i)
            base = pl.multiple_of(plan[0, i] * BLOCK, BLOCK)
            left = jnp.concatenate(stack_heads(q, base) + [ones], axis=0)
            both = lax.dot_general(
                left, cache[plan[1, i], :half], NT, preferred_element_type=jnp.float32
            )
            live = both[GROUP * BLOCK : GROUP * BLOCK + 1] < 32.0 * DEAD
            found = jnp.where(live, both[: GROUP * BLOCK] * SCALE, LOW)
            mine = own_rows(base, i)
            for h in range(GROUP):
                part = pl.ds(h * BLOCK, BLOCK)
                scores[block, part] = jnp.where(
                    mine, found[h * BLOCK : (h + 1) * BLOCK], scores[block, part]
                )
        return carry

    def soften(block, carry):
        cached = scores[block]
        level = levels[block]
        top = jnp.maximum(jnp.max(cached, axis=1, keepdims=True), level)
        lifted = jnp.exp(cached - top)
        fresh = jnp.exp(level - top)
        share = 1.0 / (jnp.sum(lifted, axis=1, keepdims=True) + fresh)
        weights[block] = (lifted * share).astype(jnp.bfloat16)
        mixed[block] = means[block] * (fresh * share)
        return carry

    def mix(step, carry):
        for u in range(UNROLL):
            i = step * UNROLL + u
            block = place(i)
            found = jnp.dot(
                weights[block], cache[plan[1, i], half:], preferred_element_type=jnp.float32
            )
            mine = own_rows(plan[0, i] * BLOCK, i)
            for h in range(GROUP):
                part = pl.ds(h * BLOCK, BLOCK)
                mixed[block, part] += jnp.where(mine, found[h * BLOCK : (h + 1) * BLOCK], 0.0)
        return carry

    fetch[0].wait()
    for copy in stage:
        copy.start()
    lax.fori_loop(lower, upper, score, 0)
    fetch[2].wait()
    fetch[3].wait()
    lax.fori_loop(0, PIECE, soften, 0, unroll=PIECE)
    fetch[1].wait()
    lax.fori_loop(lower, upper, mix, 0)
    for block in range(PIECE):
        total = mixed[block].astype(jnp.bfloat16)
        base = block * BLOCK
        for h in range(GROUP):
            out[base : base + BLOCK, h * HD : (h + 1) * HD] = total[h * BLOCK : (h + 1) * BLOCK]
    for copy in stage:
        copy.wait()


def whole(count):
    return [pl.BlockSpec(memory_space=pltpu.VMEM)] * count


def in_hbm(*values):
    return [pltpu.with_memory_space_constraint(value, pltpu.HBM) for value in values]


def far(count):
    return [pl.BlockSpec(memory_space=pltpu.HBM)] * count


def anywhere(count):
    return [pl.BlockSpec(memory_space=pl.ANY)] * count


def make_payload(lengths, keys, values):
    packs, prefix, width = keys.shape
    return pl.pallas_call(
        payload_kernel,
        out_shape=jax.ShapeDtypeStruct((packs, 2 * prefix, width), keys.dtype),
        in_specs=far(3),
        out_specs=far(1)[0],
        scratch_shapes=[
            pltpu.SMEM(lengths.shape, lengths.dtype),
            pltpu.VMEM((packs, 2 * prefix, width), keys.dtype),
            pltpu.SemaphoreType.DMA((3, CHUNKS)),
            pltpu.SemaphoreType.DMA,
        ],
        compiler_params=pltpu.CompilerParams(vmem_limit_bytes=4 << 20),
        cost_estimate=pl.CostEstimate(flops=1 << 20, bytes_accessed=4 << 20, transcendentals=0),
    )(*in_hbm(lengths, keys, values))


def cut_kernel(starts, weight, after, *refs):
    outs, sems = refs[:-1], refs[-1]
    copies = []
    for out in outs:
        for i in range(out.shape[0] // 512):
            slot = len(copies)
            source = weight.at[:, pl.ds(pl.multiple_of(starts[slot], 512), 512)]
            target = out.at[pl.ds(i * 512, 512)]
            copies.append(pltpu.make_async_copy(source, target, sems.at[slot]))
    for copy in copies:
        copy.start()
    for copy in copies:
        copy.wait()


def cut(starts, weight, heights, after):
    return pl.pallas_call(
        cut_kernel,
        out_shape=tuple(pltpu.VMEM((height, 512), weight.dtype) for height in heights),
        grid_spec=pltpu.PrefetchScalarGridSpec(
            num_scalar_prefetch=1,
            grid=(),
            in_specs=far(1) + anywhere(1),
            out_specs=tuple(whole(len(heights))),
            scratch_shapes=[pltpu.SemaphoreType.DMA((sum(heights) // 512,))],
        ),
        compiler_params=pltpu.CompilerParams(vmem_limit_bytes=8 << 20),
        cost_estimate=pl.CostEstimate(flops=0, bytes_accessed=12 << 20, transcendentals=0),
    )(starts, *in_hbm(weight), after)


def staging(part, starts, sources, targets, sems):
    if len(sources) == 2:
        weight, sibling = sources
        blocks = []
        for half in range(2):
            start = pl.multiple_of(starts[2 * half + part], 512)
            blocks.append(weight.at[:, pl.ds(start, 512)])
        for half in range(2):
            blocks.append(sibling.at[pl.ds(1024 * half + 512 * part, 512)])
    else:
        blocks = [block.at[pl.ds(512 * part, 512)] for block in sources]
    return [
        pltpu.make_async_copy(block, target, sems.at[i])
        for i, (block, target) in enumerate(zip(blocks, targets))
    ]


def attend_fresh(queries, new_keys, new_values, row_start):
    front = ((FRESH - BLOCK, 0), (0, 0))
    area = jax.ShapeDtypeStruct((512 // BLOCK, GROUP * BLOCK, HD), jnp.float32)
    return pl.pallas_call(
        fresh_kernel,
        out_shape=(area, area),
        in_specs=whole(4),
        out_specs=tuple(whole(2)),
        compiler_params=pltpu.CompilerParams(vmem_limit_bytes=5 << 20),
        cost_estimate=pl.CostEstimate(
            flops=1 << 31, bytes_accessed=4 << 20, transcendentals=1 << 18
        ),
    )(queries, jnp.pad(new_keys, front), jnp.pad(new_values, front), row_start)


def attend(first, plan, starts, queries, cache, fresh, sources, after=()):
    area = fresh[0].shape[1:]
    rows = jax.ShapeDtypeStruct((PIECE * BLOCK, queries.shape[1]), queries.dtype)
    staged = [pltpu.VMEM((512, 512), queries.dtype)] * 4
    staged += [pltpu.VMEM((1024, 512), queries.dtype)] * 2
    return pl.pallas_call(
        functools.partial(main_kernel, first),
        out_shape=(rows, *staged),
        grid_spec=pltpu.PrefetchScalarGridSpec(
            num_scalar_prefetch=2,
            grid=(),
            in_specs=whole(1) + anywhere(3 + len(sources) + len(after)),
            out_specs=tuple(whole(1 + len(staged))),
            scratch_shapes=[
                pltpu.VMEM(cache.shape, cache.dtype),
                pltpu.VMEM((PIECE, *area), jnp.float32),
                pltpu.VMEM((PIECE, *area), jnp.float32),
                pltpu.VMEM((PIECE + 1, *area), jnp.float32),
                pltpu.VMEM((PIECE + 1, *area), jnp.bfloat16),
                pltpu.VMEM((PIECE + 1, *area), jnp.float32),
                pltpu.SemaphoreType.DMA((4,)),
                pltpu.SemaphoreType.DMA((2, 4)),
            ],
        ),
        compiler_params=pltpu.CompilerParams(vmem_limit_bytes=12 << 20),
        cost_estimate=pl.CostEstimate(
            flops=1 << 31, bytes_accessed=4 << 20, transcendentals=1 << 18
        ),
    )(plan, starts, queries, cache, *in_hbm(*fresh), *in_hbm(*sources), *after)


def on_device(
    queries,
    new_keys,
    new_values,
    hidden,
    row_counts,
    pack_of,
    cache_keys,
    cache_values,
    prefix_lengths,
    out_weight,
    norm_gain,
):
    count = lax.axis_size("tensor")
    me = lax.axis_index("tensor")
    f32 = jnp.float32
    bf16 = jnp.bfloat16

    def swap(value, mask):
        return lax.ppermute(value, "tensor", [(t, t ^ mask) for t in range(count)])

    def shared(mask):
        to = jnp.bitwise_xor(me, mask)
        first = [to * 1024, jnp.bitwise_xor(to, 6) * 1024]
        second = [to * 1024 + 512, jnp.bitwise_xor(to, 2) * 1024 + 512]
        return first, second

    payload = make_payload(prefix_lengths, cache_keys[0], cache_values[0])
    cache = lax.all_to_all(payload, "dp", split_axis=0, concat_axis=0, tiled=True)

    starts = sum([shared(mask)[half] for mask, half in ((2, 0), (6, 1), (3, 0), (7, 1))], [])
    starts = jnp.stack(starts + sum(shared(1), []))
    pieces = cut(starts, out_weight, (1024, 1024, 1024, 1024, 2048), payload)
    *near_mats, sibling = [swap(piece, mask) for piece, mask in zip(pieces, (2, 6, 3, 7, 1))]

    plan, row_start = pair_plan(row_counts[0], pack_of[0])
    fresh = attend_fresh(queries, new_keys, new_values, row_start)
    plan, sibling, near_mats[:2] = lax.optimization_barrier((plan, sibling, near_mats[:2]))
    starts = jnp.stack(sum(shared(0), []))
    first, *mats, own_0, own_1 = attend(
        0, plan, starts, queries, cache, fresh, (out_weight, sibling)
    )
    others_a = swap(first, 1)
    second, *rest = attend(PIECE, plan, starts, queries, cache, fresh, near_mats, (others_a,))
    mats += rest[:4]
    own_mats = ((own_0, rest[4]), (own_1, rest[5]))
    attended = [first, second]

    def times(rows, mat):
        return jnp.dot(rows, mat, preferred_element_type=f32)

    others = [others_a, swap(second, 1)]
    near = [[swap(rows, mask) for mask in (2, 6)] for rows in attended]
    inputs = []
    got = []
    sent = []
    for rows, other, close in zip(attended, others, near):
        if sent:
            sent, inputs[0] = lax.optimization_barrier((sent, inputs[0]))
            got.append([swap(part, mask) for part, mask in zip(sent, (6, 2))])
        local = [times(rows, mats[half]) + times(other, mats[2 + half]) for half in range(2)]
        local = lax.optimization_barrier(local)
        side = [swap(part, 1) for part in close]
        sent = [
            local[half] + times(close[half], mats[4 + half]) + times(side[half], mats[6 + half])
            for half in range(2)
        ]
        sent = [total.astype(bf16) for total in sent]
        inputs.append([[rows, other, close[half], side[half]] for half in range(2)])
    sent, inputs[1] = lax.optimization_barrier((sent, inputs[1]))
    got.append([swap(part, mask) for part, mask in zip(sent, (6, 2))])

    own = [
        [
            times(jnp.concatenate(parts[:2], axis=1), mat[0])
            + times(jnp.concatenate(parts[2:], axis=1), mat[1])
            for parts, mat in zip(halves, own_mats)
        ]
        for halves in inputs
    ]
    own = [[lax.optimization_barrier(part) for part in halves] for halves in own]
    delta = jnp.concatenate(
        [
            jnp.concatenate([mine + part.astype(f32) for mine, part in zip(*pair)], axis=1)
            for pair in zip(own, got)
        ],
        axis=0,
    )
    summed = hidden.astype(f32) + delta
    residual_out = summed.astype(bf16)
    squares = jnp.sum(summed * summed, axis=1)
    squares = squares + swap(squares, 1)
    squares = squares + swap(squares, 4) + swap(squares, 2) + swap(squares, 6)
    mean_square = squares / D
    normed = (summed * lax.rsqrt(mean_square + 1e-06)[:, None] * norm_gain[None, :]).astype(bf16)
    return (residual_out, normed)


def solution(mesh):
    return jax.shard_map(
        on_device,
        mesh=mesh,
        in_specs=(
            P("dp", "tensor"),
            P("dp", "tensor"),
            P("dp", "tensor"),
            P("dp", "tensor"),
            P("dp", None),
            P("dp", None),
            P("dp", None, None, "tensor"),
            P("dp", None, None, "tensor"),
            P("dp", None),
            P("tensor", None),
            P("tensor"),
        ),
        out_specs=(P("dp", "tensor"), P("dp", "tensor")),
        check_vma=False,
    )
```

```python
import functools
import math

import jax
import jax.numpy as jnp
from jax import lax
from jax.experimental import pallas as pl
from jax.experimental.pallas import tpu as pltpu
from jax.sharding import PartitionSpec as P

D = 8192
HEADS = 32
KV_HEADS = 8
HD = 128
MOST = 64
GROUP = HEADS // KV_HEADS
BLOCK = 32
FRESH = 128
PAIRS = 48
CHUNKS = 8
PIECE = 8
UNROLL = 8
LOW = -1e30
DEAD = 8192.0
SCALE = 1.0 / math.sqrt(HD)
NT = (((1,), (1,)), ((), ()))


def pair_plan(counts, packs):
    roll = counts.shape[0]
    ids = jnp.arange(roll, dtype=jnp.int32)
    before = ids[None, :] < ids[:, None]
    starts = jnp.sum(jnp.where(before, counts[None, :], 0), axis=1)
    ends = starts + counts
    first = starts // BLOCK
    spans = (ends - 1) // BLOCK - first + 1
    offsets = jnp.sum(jnp.where(before, spans[None, :], 0), axis=1)
    slot = jnp.arange(PAIRS, dtype=jnp.int32)[:, None]
    hit = (slot >= offsets[None, :]) & (slot < (offsets + spans)[None, :])

    def pick(values):
        return jnp.sum(jnp.where(hit, values, 0), axis=1)

    block = pick(first[None, :] + slot - offsets[None, :])
    ahead = jnp.sum(jnp.where((block < PIECE) & jnp.any(hit, axis=1), 1, 0))
    plan = jnp.stack(
        [
            block,
            pick(packs[None, :]),
            pick(starts[None, :]),
            pick(ends[None, :]),
            jnp.full((PAIRS,), ahead),
        ]
    ).astype(jnp.int32)
    rows = jnp.arange(512, dtype=jnp.int32)[:, None]
    row_start = jnp.max(jnp.where(starts[None, :] <= rows, starts[None, :], 0), axis=1)
    return plan, jnp.broadcast_to(row_start[:, None], (512, HD))


def stack_heads(ref, base):
    return [ref[pl.ds(base, BLOCK), h * HD : (h + 1) * HD] for h in range(GROUP)]


def payload_kernel(lengths_hbm, keys, values, out, lengths, held, sems, lengths_sem):
    packs, prefix, _ = keys.shape
    tile = packs // CHUNKS

    def copies(c):
        part = pl.ds(c * tile, tile)
        front, back = held.at[part, pl.ds(0, prefix)], held.at[part, pl.ds(prefix, prefix)]
        return (
            pltpu.make_async_copy(keys.at[part], front, sems.at[0, c]),
            pltpu.make_async_copy(values.at[part], back, sems.at[1, c]),
            pltpu.make_async_copy(held.at[part], out.at[part], sems.at[2, c]),
        )

    steps = [copies(c) for c in range(CHUNKS)]
    fetch = pltpu.make_async_copy(lengths_hbm, lengths, lengths_sem)
    fetch.start()
    for step in steps:
        step[0].start()
        step[1].start()
    fetch.wait()
    position = lax.broadcasted_iota(jnp.int32, keys.shape[1:], 0)
    for c, step in enumerate(steps):
        step[0].wait()
        for u in range(tile):
            pack = c * tile + u
            found = held[pack, :prefix].astype(jnp.float32)
            marked = jnp.where(position < lengths[0, pack], found, DEAD)
            held[pack, :prefix] = marked.astype(jnp.bfloat16)
        step[1].wait()
        step[2].start()
    for step in steps:
        step[2].wait()


def fresh_kernel(q, fresh_k, fresh_v, row_start, mean_out, level_out):
    def body(block, carry):
        base = pl.multiple_of(block * BLOCK, BLOCK)
        left = jnp.concatenate(stack_heads(q, base), axis=0)
        window = pl.ds(base, FRESH)
        found = lax.dot_general(left, fresh_k[window, :], NT, preferred_element_type=jnp.float32)
        key = base - (FRESH - BLOCK) + lax.broadcasted_iota(jnp.int32, found.shape, 1)
        sub = lax.broadcasted_iota(jnp.int32, found.shape, 0)
        row = base + jnp.bitwise_and(sub, BLOCK - 1)
        start = jnp.concatenate([row_start[pl.ds(base, BLOCK), :]] * GROUP, axis=0)
        found = jnp.where((key <= row) & (key >= start), found * SCALE, LOW)
        top = jnp.max(found, axis=1, keepdims=True)
        lifted = jnp.exp(found - top)
        total = jnp.sum(lifted, axis=1, keepdims=True)
        mean_out[block] = jnp.dot(
            (lifted / total).astype(jnp.bfloat16),
            fresh_v[window, :],
            preferred_element_type=jnp.float32,
        )
        level_out[block] = jnp.broadcast_to(top + jnp.log(total), found.shape)
        return carry

    lax.fori_loop(0, 512 // BLOCK, body, 0, unroll=2)


def main_kernel(first, plan, starts, q, cache_hbm, mean_hbm, level_hbm, *refs):
    cache, means, levels, scores, weights, mixed, sems, stage_sems = refs[-8:]
    count = (len(refs) - 9) // 2
    sources, out, staged = refs[:count], refs[count], refs[count + 1 : -8]
    stage = []
    for place_of, (source, target) in enumerate(zip(sources, staged)):
        if source.shape == target.shape:
            parts = [(source, target)]
        elif source.shape[1] == 2 * target.shape[1]:
            parts = [(source.at[:, pl.ds(1024 * (place_of % 2), 1024)], target)]
        else:
            parts = [
                (source.at[:, pl.ds(pl.multiple_of(starts[i], 512), 512)], target.at[:, pl.ds(512 * (i % 2), 512)])
                for i in range(len(stage), len(stage) + 2)
            ]
        for origin, goal in parts:
            stage.append(pltpu.make_async_copy(origin, goal, stage_sems.at[len(stage)]))
    half = cache.shape[1] // 2
    fetch = [
        pltpu.make_async_copy(
            cache_hbm.at[:, pl.ds(i * half, half)], cache.at[:, pl.ds(i * half, half)], sems.at[i]
        )
        for i in range(2)
    ]
    blocks = pl.ds(first, PIECE)
    fetch.append(pltpu.make_async_copy(level_hbm.at[blocks], levels, sems.at[2]))
    fetch.append(pltpu.make_async_copy(mean_hbm.at[blocks], means, sems.at[3]))
    for i in (0, 2, 3, 1):
        fetch[i].start()
    ones = jnp.ones((16, HD), jnp.bfloat16)
    ahead = plan[4, 0]
    if first == 0:
        lower, upper = 0, lax.div(ahead + UNROLL - 1, UNROLL)
    else:
        lower, upper = lax.div(ahead, UNROLL), PAIRS // UNROLL

    def place(i):
        block = plan[0, i] - first
        return jnp.where((block >= 0) & (block < PIECE), block, PIECE)

    def own_rows(base, i):
        row = base + lax.broadcasted_iota(jnp.int32, (BLOCK, HD), 0)
        return (row >= plan[2, i]) & (row < plan[3, i])

    def score(step, carry):
        for u in range(UNROLL):
            i = step * UNROLL + u
            block = place(i)
            base = pl.multiple_of(plan[0, i] * BLOCK, BLOCK)
            left = jnp.concatenate(stack_heads(q, base) + [ones], axis=0)
            both = lax.dot_general(
                left, cache[plan[1, i], :half], NT, preferred_element_type=jnp.float32
            )
            live = both[GROUP * BLOCK : GROUP * BLOCK + 1] < 32.0 * DEAD
            found = jnp.where(live, both[: GROUP * BLOCK] * SCALE, LOW)
            mine = own_rows(base, i)
            for h in range(GROUP):
                part = pl.ds(h * BLOCK, BLOCK)
                scores[block, part] = jnp.where(
                    mine, found[h * BLOCK : (h + 1) * BLOCK], scores[block, part]
                )
        return carry

    def soften(block, carry):
        cached = scores[block]
        level = levels[block]
        top = jnp.maximum(jnp.max(cached, axis=1, keepdims=True), level)
        lifted = jnp.exp(cached - top)
        fresh = jnp.exp(level - top)
        share = 1.0 / (jnp.sum(lifted, axis=1, keepdims=True) + fresh)
        weights[block] = (lifted * share).astype(jnp.bfloat16)
        mixed[block] = means[block] * (fresh * share)
        return carry

    def mix(step, carry):
        for u in range(UNROLL):
            i = step * UNROLL + u
            block = place(i)
            found = jnp.dot(
                weights[block], cache[plan[1, i], half:], preferred_element_type=jnp.float32
            )
            mine = own_rows(plan[0, i] * BLOCK, i)
            for h in range(GROUP):
                part = pl.ds(h * BLOCK, BLOCK)
                mixed[block, part] += jnp.where(mine, found[h * BLOCK : (h + 1) * BLOCK], 0.0)
        return carry

    fetch[0].wait()
    for copy in stage:
        copy.start()
    lax.fori_loop(lower, upper, score, 0)
    fetch[2].wait()
    fetch[3].wait()
    lax.fori_loop(0, PIECE, soften, 0, unroll=PIECE)
    fetch[1].wait()
    lax.fori_loop(lower, upper, mix, 0)
    for block in range(PIECE):
        total = mixed[block].astype(jnp.bfloat16)
        base = block * BLOCK
        for h in range(GROUP):
            out[base : base + BLOCK, h * HD : (h + 1) * HD] = total[h * BLOCK : (h + 1) * BLOCK]
    for copy in stage:
        copy.wait()


def whole(count):
    return [pl.BlockSpec(memory_space=pltpu.VMEM)] * count


def in_hbm(*values):
    return [pltpu.with_memory_space_constraint(value, pltpu.HBM) for value in values]


def far(count):
    return [pl.BlockSpec(memory_space=pltpu.HBM)] * count


def anywhere(count):
    return [pl.BlockSpec(memory_space=pl.ANY)] * count


def make_payload(lengths, keys, values):
    packs, prefix, width = keys.shape
    return pl.pallas_call(
        payload_kernel,
        out_shape=jax.ShapeDtypeStruct((packs, 2 * prefix, width), keys.dtype),
        in_specs=far(3),
        out_specs=far(1)[0],
        scratch_shapes=[
            pltpu.SMEM(lengths.shape, lengths.dtype),
            pltpu.VMEM((packs, 2 * prefix, width), keys.dtype),
            pltpu.SemaphoreType.DMA((3, CHUNKS)),
            pltpu.SemaphoreType.DMA,
        ],
        compiler_params=pltpu.CompilerParams(vmem_limit_bytes=4 << 20),
        cost_estimate=pl.CostEstimate(flops=1 << 20, bytes_accessed=4 << 20, transcendentals=0),
    )(*in_hbm(lengths, keys, values))


def cut_kernel(starts, weight, after, *refs):
    outs, sems = refs[:-1], refs[-1]
    copies = []
    for out in outs:
        for i in range(out.shape[1] // 512):
            slot = len(copies)
            source = weight.at[:, pl.ds(pl.multiple_of(starts[slot], 512), 512)]
            target = out.at[:, pl.ds(i * 512, 512)]
            copies.append(pltpu.make_async_copy(source, target, sems.at[slot]))
    for copy in copies:
        copy.start()
    for copy in copies:
        copy.wait()


def cut(starts, weight, widths, after):
    rows = weight.shape[0]
    return pl.pallas_call(
        cut_kernel,
        out_shape=tuple(pltpu.VMEM((rows, width), weight.dtype) for width in widths),
        grid_spec=pltpu.PrefetchScalarGridSpec(
            num_scalar_prefetch=1,
            grid=(),
            in_specs=far(1) + anywhere(1),
            out_specs=tuple(whole(len(widths))),
            scratch_shapes=[pltpu.SemaphoreType.DMA((sum(widths) // 512,))],
        ),
        compiler_params=pltpu.CompilerParams(vmem_limit_bytes=8 << 20),
        cost_estimate=pl.CostEstimate(flops=0, bytes_accessed=12 << 20, transcendentals=0),
    )(starts, *in_hbm(weight), after)


def attend_fresh(queries, new_keys, new_values, row_start):
    front = ((FRESH - BLOCK, 0), (0, 0))
    area = jax.ShapeDtypeStruct((512 // BLOCK, GROUP * BLOCK, HD), jnp.float32)
    return pl.pallas_call(
        fresh_kernel,
        out_shape=(area, area),
        in_specs=whole(4),
        out_specs=tuple(whole(2)),
        compiler_params=pltpu.CompilerParams(vmem_limit_bytes=5 << 20),
        cost_estimate=pl.CostEstimate(
            flops=1 << 31, bytes_accessed=4 << 20, transcendentals=1 << 18
        ),
    )(queries, jnp.pad(new_keys, front), jnp.pad(new_values, front), row_start)


def attend(first, plan, starts, queries, cache, fresh, sources=()):
    area = fresh[0].shape[1:]
    rows = jax.ShapeDtypeStruct((PIECE * BLOCK, queries.shape[1]), queries.dtype)
    staged = [pltpu.VMEM((source.shape[0], 1024), source.dtype) for source in sources]
    return pl.pallas_call(
        functools.partial(main_kernel, first),
        out_shape=(rows, *staged),
        grid_spec=pltpu.PrefetchScalarGridSpec(
            num_scalar_prefetch=2,
            grid=(),
            in_specs=whole(1) + anywhere(3 + len(sources)),
            out_specs=tuple(whole(1 + len(staged))),
            scratch_shapes=[
                pltpu.VMEM(cache.shape, cache.dtype),
                pltpu.VMEM((PIECE, *area), jnp.float32),
                pltpu.VMEM((PIECE, *area), jnp.float32),
                pltpu.VMEM((PIECE + 1, *area), jnp.float32),
                pltpu.VMEM((PIECE + 1, *area), jnp.bfloat16),
                pltpu.VMEM((PIECE + 1, *area), jnp.float32),
                pltpu.SemaphoreType.DMA((4,)),
                pltpu.SemaphoreType.DMA((len(sources) + 2,)),
            ],
        ),
        compiler_params=pltpu.CompilerParams(vmem_limit_bytes=(7 + len(sources)) << 20),
        cost_estimate=pl.CostEstimate(
            flops=1 << 31, bytes_accessed=4 << 20, transcendentals=1 << 18
        ),
    )(plan, starts, queries, cache, *in_hbm(*fresh), *in_hbm(*sources))


def attention(counts, packs, queries, marked, values, new_keys, new_values):
    plan, row_start = pair_plan(counts, packs)
    fresh = attend_fresh(queries, new_keys, new_values, row_start)
    cache = jnp.concatenate([marked, values], axis=1)
    return jnp.concatenate([attend(i, plan, plan[0], queries, cache, fresh)[0] for i in (0, PIECE)], axis=0)


def on_device(
    queries,
    new_keys,
    new_values,
    hidden,
    row_counts,
    pack_of,
    cache_keys,
    cache_values,
    prefix_lengths,
    out_weight,
    norm_gain,
):
    count = lax.axis_size("tensor")
    me = lax.axis_index("tensor")
    f32 = jnp.float32
    bf16 = jnp.bfloat16

    def swap(value, mask):
        return lax.ppermute(value, "tensor", [(t, t ^ mask) for t in range(count)])

    def shared(mask):
        to = jnp.bitwise_xor(me, mask)
        first = [to * 1024, jnp.bitwise_xor(to, 6) * 1024]
        second = [to * 1024 + 512, jnp.bitwise_xor(to, 2) * 1024 + 512]
        return first, second

    payload = make_payload(prefix_lengths, cache_keys[0], cache_values[0])
    cache = lax.all_to_all(payload, "dp", split_axis=0, concat_axis=0, tiled=True)

    starts = sum([shared(mask)[half] for mask, half in ((2, 0), (6, 1), (3, 0), (7, 1))], [])
    starts = jnp.stack(starts + sum(shared(1), []))
    pieces = cut(starts, out_weight, (1024, 1024, 1024, 1024, 2048), payload)
    *near_mats, sibling = [swap(piece, mask) for piece, mask in zip(pieces, (2, 6, 3, 7, 1))]

    plan, row_start = pair_plan(row_counts[0], pack_of[0])
    fresh = attend_fresh(queries, new_keys, new_values, row_start)
    plan, sibling, near_mats[:2] = lax.optimization_barrier((plan, sibling, near_mats[:2]))
    starts = jnp.stack(sum(shared(0), []))
    attended = attend(0, plan, starts, queries, cache, fresh)
    sources = (out_weight, out_weight, sibling, sibling, *near_mats)
    rest, *mats = attend(PIECE, plan, starts, queries, cache, fresh, sources)
    attended = [attended[0], rest]
    here, sibling, same, cross = (mats[i : i + 2] for i in (0, 2, 4, 6))

    def times(rows, mat):
        return jnp.dot(rows, mat, preferred_element_type=f32)

    others = [swap(rows, 1) for rows in attended]
    near = [[swap(rows, mask) for mask in (2, 6)] for rows in attended]
    own = []
    got = []
    sent = []
    for rows, other, close in zip(attended, others, near):
        local = [times(rows, here[half]) + times(other, sibling[half]) for half in range(2)]
        close, local, sent = lax.optimization_barrier((close, local, sent))
        totals = [
            local[half] + times(close[half], same[half]) + times(swap(close[half], 1), cross[half])
            for half in range(2)
        ]
        own.append([total[:, :512] for total in totals])
        sent = [total[:, 512:].astype(bf16) for total in totals]
        got.append([swap(part, mask) for part, mask in zip(sent, (6, 2))])

    delta = jnp.concatenate(
        [
            jnp.concatenate([a + b.astype(f32) for a, b in zip(*pair)], axis=1)
            for pair in zip(own, got)
        ],
        axis=0,
    )
    summed = hidden.astype(f32) + delta
    residual_out = summed.astype(bf16)
    squares = jnp.sum(summed * summed, axis=1)
    squares = squares + sum(swap(squares, mask) for mask in (4, 5, 2, 3, 6, 7, 1))
    mean_square = squares / D
    normed = (summed * lax.rsqrt(mean_square + 1e-06)[:, None] * norm_gain[None, :]).astype(bf16)
    return (residual_out, normed)


def solution(mesh):
    return jax.shard_map(
        on_device,
        mesh=mesh,
        in_specs=(
            P("dp", "tensor"),
            P("dp", "tensor"),
            P("dp", "tensor"),
            P("dp", "tensor"),
            P("dp", None),
            P("dp", None),
            P("dp", None, None, "tensor"),
            P("dp", None, None, "tensor"),
            P("dp", None),
            P("tensor", None),
            P("tensor"),
        ),
        out_specs=(P("dp", "tensor"), P("dp", "tensor")),
        check_vma=False,
    )
```
